128 devices in a mesh: group: 8 (over y_hi, z), dp: 16 (over x, y_lo, core).
Axes of the slice: x: 4, y: 4 (y_hi: 2, y_lo: 2; y = y_hi * 2 + y_lo), z: 4, core: 2. Of those that a mesh axis runs over, the one named last changes fastest.
Arguments:
- tokens: float32 [128, 577, 384], P(('group', 'dp')), may hold values from -6 to 6
- cotangent: float32 [128, 577, 384], P(('group', 'dp')), may hold values from -6 to 6
- live: int32 [128], P(('group', 'dp')), may hold values from 0 to 1, as said below
- slot_of: int32 [8], replicated, may hold values from 0 to 7, as said below
- weights: float32 [8, 384, 1536], P('group', None, 'dp'), as said below
- momentum: float32 [8, 384, 1536], P('group', None, 'dp'), as said below
- vec: float32 [24, 384], P('group', 'dp')
- vec_first: float32 [24, 384], P('group', 'dp')
- vec_second: float32 [24, 384], P('group', 'dp'), as said below
Outputs:
- block_out: float32 [128, 577, 384], P(('group', 'dp'))
- token_grad: float32 [128, 577, 384], P(('group', 'dp'))
- weight_grad: float32 [8, 384, 1536], P('group', None, 'dp')
- new_momentum: float32 [8, 384, 1536], P('group', None, 'dp')
- new_weights: float32 [8, 384, 1536], P('group', None, 'dp')
- first_new: float32 [24, 384], P('group', 'dp')
- second_new: float32 [24, 384], P('group', 'dp')
- vec_new: float32 [24, 384], P('group', 'dp')
The draws below stay inside these ranges and needn't reach their ends.
Inputs may be any that keep to these rules, and one draw needn't show every extreme that they name: `live`: 1 where the device's slot holds an image, 0 where it is empty; every draw has full and empty slots. A permutation: matrix m lies in slot slot_of[m]; slot q lies on group index q. `weights`: slot q holds the matrix m with slot_of[m] = q in its first n(m) columns and zeros beyond. `momentum`: laid out like weights, zeros beyond n(m) columns. `vec_second`: positive.
All inputs are finite; a program needn't handle non-finite values.
Results may differ from the reference program's by a relative error of at most 0.02.
The reference program's roundings to bfloat16 on the way count: a program that leaves them out, or rounds other values in their place, can miss the bound.
Values may be sent and summed in bfloat16 or wider, within the bound.
No kernel may reach another device: no remote copies, remote signals or barrier semaphores. Data moves between devices by JAX's collectives and lax.ppermute only.
A program may use at most 192 MiB of HBM per device.

```python
import math
import jax
import jax.numpy as jnp
from jax import lax

D = 384
HEADS = 6
FF = 1536
P_SIZE = 577
LAYERS = 2
NEWTON_STEPS = 5
STEP = 10
IMAGES = 128
MATS = 8
VROWS = 24


def slot_order(key):
    return jax.random.permutation(jax.random.fold_in(key, 101), MATS).astype(jnp.int32)


def slot_kinds(key):
    order = slot_order(key)
    slot_ids = lax.iota(jnp.int32, MATS)
    slot_match = order[None, :] == slot_ids[:, None]
    return jnp.sum(jnp.where(slot_match, slot_ids[None, :] % 4, 0), 1)


def gradient_scale():
    return 0.5 * math.sqrt(0.75 * P_SIZE * IMAGES)


def packed_matrices(key, kinds, scales):
    widths = jnp.array([3 * D, D, FF, FF], jnp.int32)
    table = jnp.array(scales, jnp.float32)
    kind_match = kinds[:, None] == lax.iota(jnp.int32, 4)[None, :]
    slot_width = jnp.sum(jnp.where(kind_match, widths[None, :], 0), 1)
    slot_scale = jnp.sum(jnp.where(kind_match, table[None, :], 0.0), 1)
    noise = jax.random.normal(key, (MATS, D, FF), jnp.float32)
    live_cols = lax.iota(jnp.int32, FF)[None, None, :] < slot_width[:, None, None]
    return jnp.where(live_cols, noise * slot_scale[:, None, None], 0.0)


def draw_slot_of(key, part):
    return slot_order(key)


def draw_weights(key, part):
    kinds = slot_kinds(key)
    key = jax.random.fold_in(key, 2)
    return packed_matrices(key, kinds, [1.4 * D ** (-0.5), 2.0 * D ** (-0.5), D ** (-0.5), 1.5 * FF ** (-0.5)])


def draw_momentum(key, part):
    kinds = slot_kinds(key)
    key = jax.random.fold_in(key, 3)
    spread = gradient_scale()
    return packed_matrices(key, kinds, [spread, spread, spread, spread])


def draw_vec(key, part):
    key = jax.random.fold_in(key, 4)
    per_layer = VROWS // LAYERS
    row_kind = lax.iota(jnp.int32, VROWS) % per_layer
    gain_rows = (row_kind == 0) | (row_kind == 5)
    noise = jax.random.normal(key, (VROWS, D), jnp.float32)
    return jnp.where(gain_rows[:, None], 1.0 + 0.1 * noise, 0.2 * noise)


def draw_vec_first(key, part):
    key = jax.random.fold_in(key, 5)
    return jax.random.normal(key, (VROWS, D), jnp.float32) * (0.1 / 0.9 * gradient_scale())


def draw_vec_second(key, part):
    key = jax.random.fold_in(key, 6)
    factor = jnp.exp(jax.random.uniform(key, (VROWS, D), jnp.float32, 0.0, math.log(4.0)))
    spread = gradient_scale()
    return factor * (0.001 / 0.999 * spread * spread)


def draw_live(key, part):
    key = jax.random.fold_in(key, 7)
    subkeys = jax.random.split(key, 3)
    occupied = (jax.random.randint(subkeys[0], (IMAGES,), 0, 4) < 3).astype(jnp.int32)
    full_at = jax.random.randint(subkeys[1], (), 0, IMAGES)
    empty_at = (full_at + 1 + jax.random.randint(subkeys[2], (), 0, IMAGES - 1)) % IMAGES
    return occupied.at[full_at].set(1).at[empty_at].set(0)


def shard_levels(own_key, dims, shards, least, largest):
    loudness, own = 1.0, jax.random.fold_in(own_key, 6)
    for axis_at, shards_of in shards:
        draws = jnp.exp(jax.random.uniform(jax.random.fold_in(own, axis_at), (shards_of,), jnp.float32, least / len(shards), largest / len(shards)))
        loudness = loudness * jnp.repeat(draws, dims[axis_at] // shards_of).reshape([-1 if axis == axis_at else 1 for axis in range(len(dims))])
    return loudness


def normal_values(rng, extent, deviation, bound, pieces=(), kind=jnp.bfloat16):
    values = deviation * jax.random.normal(rng, extent, jnp.float32)
    if pieces:
        values = values * shard_levels(rng, extent, pieces, -0.22, 0.18)
    return jnp.clip(values, -bound, bound).astype(kind)


def setup_inputs(seed: int = 0) -> dict:
    key_list = jax.random.split(jax.random.key(seed), 10)
    return {
        "tokens": normal_values(key_list[0], (IMAGES, P_SIZE, D), 1.0, 6.0, ((0, 128),), jnp.float32),
        "cotangent": normal_values(key_list[1], (IMAGES, P_SIZE, D), 1.0, 6.0, ((0, 128),), jnp.float32),
        "live": draw_live(jax.random.fold_in(key_list[9], 71), 0),
        "slot_of": draw_slot_of(jax.random.fold_in(key_list[9], 71), 0),
        "weights": draw_weights(jax.random.fold_in(key_list[9], 71), 0),
        "momentum": draw_momentum(jax.random.fold_in(key_list[9], 71), 0),
        "vec": draw_vec(jax.random.fold_in(key_list[9], 71), 0),
        "vec_first": draw_vec_first(jax.random.fold_in(key_list[9], 71), 0),
        "vec_second": draw_vec_second(jax.random.fold_in(key_list[9], 71), 0),
    }


@jax.custom_vjp
def low(v):
    return lax.optimization_barrier(v.astype(jnp.bfloat16)).astype(jnp.float32)

@jax.custom_vjp
def low_back(v):
    return v

def low_keep(v):
    return (low(v), None)

def low_pass(kept, grad):
    return (grad,)

def back_keep(v):
    return (v, None)

def back_low(kept, grad):
    return (low(grad),)
low.defvjp(low_keep, low_pass)
low_back.defvjp(back_keep, back_low)
norm_eps = 1e-06
ortho_eps = 1e-07
coef_a = 3.4445
coef_b = -4.775
coef_c = 2.0315
momentum_keep = 0.95
muon_rate = 0.25
muon_decay = 0.01
muon_shape = 0.5
adam_rate = 0.4
first_keep = 0.9
second_keep = 0.999
adam_eps = 1e-08
highest = lax.Precision.HIGHEST

def layer_norm(values, gain, shift):
    center = values - lax.optimization_barrier(jnp.mean(values, -1, keepdims=True))
    return center * lax.rsqrt(lax.optimization_barrier(jnp.mean(center * center, -1, keepdims=True)) + norm_eps) * gain + shift

def encoder_layer(inputs, w_qkv, w_out, w_up, w_down, vec_rows):
    length, features = inputs.shape
    head_size = features // HEADS
    normed = low(layer_norm(inputs, vec_rows[0], vec_rows[1]))
    qkv_bias = jnp.concatenate([vec_rows[2], jnp.zeros_like(vec_rows[2]), vec_rows[3]])
    qkv = low(low_back(jnp.dot(normed, w_qkv, precision=highest) + qkv_bias))
    queries = qkv[:, :features].reshape(length, HEADS, head_size)
    key_heads = qkv[:, features:2 * features].reshape(length, HEADS, head_size)
    value_heads = qkv[:, 2 * features:].reshape(length, HEADS, head_size)
    scores = low_back(jnp.einsum('qhd,khd->hqk', queries, key_heads, precision=highest) * head_size ** (-0.5))
    prob_rows = jax.nn.softmax(scores, axis=-1)
    attended = jnp.einsum('hqk,khd->qhd', low(prob_rows), value_heads, precision=highest).reshape(length, features)
    attended = low(low_back(attended))
    middle = inputs + low_back(jnp.dot(attended, w_out, precision=highest) + vec_rows[4])
    normed_two = low(layer_norm(middle, vec_rows[5], vec_rows[6]))
    hidden = low_back(jnp.dot(normed_two, w_up, precision=highest) + vec_rows[8:].reshape(-1))
    active = low(jax.nn.gelu(hidden, approximate=False))
    return middle + low_back(jnp.dot(active, w_down.T, precision=highest) + vec_rows[7])

def network(image_rows, mats_in, vec_in):
    mats_low = [low(member) for member in mats_in]
    vec_low = low(vec_in)
    per_layer = VROWS // LAYERS
    for layer_at in range(LAYERS):
        base = 4 * layer_at
        image_rows = encoder_layer(image_rows, mats_low[base], mats_low[base + 1], mats_low[base + 2], mats_low[base + 3], vec_low[layer_at * per_layer:(layer_at + 1) * per_layer])
    return image_rows

def orthogonalize(moment):
    norm_value = jnp.sqrt(lax.optimization_barrier(jnp.sum(moment * moment, axis=(1, 2), keepdims=True)))
    current = moment / (norm_value + ortho_eps)
    for iteration in range(NEWTON_STEPS):
        gram_sum = jnp.einsum('sdc,sec->sde', current, current, precision=highest)
        polynomial = coef_b * gram_sum + coef_c * jnp.einsum('sde,sef->sdf', gram_sum, gram_sum, precision=highest)
        current = coef_a * current + jnp.einsum('sde,sec->sdc', polynomial, current, precision=highest)
    return current

def reference(tokens, cotangent, live, slot_of, weights, momentum, vec, vec_first, vec_second):
    widths = [3 * D, D, FF, FF]
    mats = tuple((weights[slot_of[mat_index]][:, :widths[mat_index % 4]] for mat_index in range(MATS)))
    block_size = 4
    blocks = IMAGES // block_size
    image_blocks = tokens.reshape(blocks, block_size, P_SIZE, D)
    alive = live.astype(tokens.dtype)
    cot_blocks = (cotangent * alive[:, None, None]).reshape(blocks, block_size, P_SIZE, D)

    def batched(images, mats_in, vec_in):
        return jax.vmap(network, in_axes=(0, None, None))(images, mats_in, vec_in)

    def one_block(totals, block_item):
        images, cots = block_item
        block_outs, pullback = jax.vjp(batched, images, mats, vec)
        image_grads, mat_grads, vec_grad = pullback(cots)
        totals = (tuple((total + extra for total, extra in zip(totals[0], mat_grads))), totals[1] + vec_grad)
        return (totals, (block_outs, image_grads))
    start = (tuple((jnp.zeros_like(member) for member in mats)), jnp.zeros_like(vec))
    (mat_totals, vec_grad), (outs_all, grads_all) = lax.scan(one_block, start, (image_blocks, cot_blocks))
    slot_ids = lax.iota(jnp.int32, MATS)
    slot_match = slot_of[None, :] == slot_ids[:, None]
    stacked = jnp.stack([jnp.pad(member, ((0, 0), (0, FF - member.shape[1]))) for member in mat_totals])
    weight_grad = jnp.einsum('qm,mdc->qdc', slot_match.astype(stacked.dtype), stacked, precision=highest)
    width_row = jnp.array(widths * LAYERS, stacked.dtype)
    slot_width = lax.optimization_barrier(jnp.sum(jnp.where(slot_match, width_row[None, :], 0.0), 1))
    new_moment = momentum_keep * momentum + weight_grad
    ortho = orthogonalize(new_moment)
    step_scale = (muon_rate * muon_shape * jnp.sqrt(slot_width))[:, None, None]
    new_weights = weights * (1.0 - muon_rate * muon_decay) - step_scale * ortho
    first_new = first_keep * vec_first + (1.0 - first_keep) * vec_grad
    second_new = second_keep * vec_second + (1.0 - second_keep) * vec_grad * vec_grad
    vec_new = vec - adam_rate * (first_new / (1.0 - first_keep ** STEP) / (jnp.sqrt(second_new / (1.0 - second_keep ** STEP)) + adam_eps))
    return (outs_all.reshape(IMAGES, P_SIZE, D), grads_all.reshape(IMAGES, P_SIZE, D), weight_grad, new_moment, new_weights, first_new, second_new, vec_new)
```

```python
import jax
import jax.numpy as jnp
from jax import lax
from jax.experimental import pallas as pl
from jax.experimental.pallas import tpu as pltpu
from jax.sharding import PartitionSpec as P

HEADS = 6
FF = 1536
LAYERS = 2
NEWTON_STEPS = 5
STEP = 10
MATS = 8
VROWS = 24


norm_eps = 1e-06
ortho_eps = 1e-07
coef_a = 3.4445
coef_b = -4.775
coef_c = 2.0315
momentum_keep = 0.95
muon_rate = 0.25
muon_decay = 0.01
muon_shape = 0.5
adam_rate = 0.4
first_keep = 0.9
second_keep = 0.999
adam_eps = 1e-08
highest = lax.Precision.HIGHEST
half_root = 0.7071067811865476
density = 0.3989422804014327


def normalize(values):
    center = values - jnp.mean(values, -1, keepdims=True)
    inv_std = lax.rsqrt(jnp.mean(center * center, -1, keepdims=True) + norm_eps)
    return (center * inv_std, inv_std)


def norm_back(upstream, normed, inv_std, gain):
    scaled = upstream * gain
    return inv_std * (
        scaled
        - jnp.mean(scaled, -1, keepdims=True)
        - normed * jnp.mean(scaled * normed, -1, keepdims=True)
    )


def gelu_slope(values):
    return (
        0.5 * (1.0 + lax.erf(values * half_root))
        + values * jnp.exp(-0.5 * values * values) * density
    )


def row_contract(left_op, right_op):
    return lax.dot_general(
        left_op, right_op, (((0,), (0,)), ((), ())), preferred_element_type=jnp.float32
    )


def col_contract(left_op, right_op):
    return lax.dot_general(
        left_op, right_op, (((1,), (1,)), ((), ())), preferred_element_type=jnp.float32
    )


def split_heads(packed, head_count):
    length, triple = packed.shape
    features = triple // 3
    head_size = features // head_count
    pieces = [
        packed[:, slot_at * features : (slot_at + 1) * features].reshape(
            length, head_count, head_size
        )
        for slot_at in range(3)
    ]
    return (pieces[0], pieces[1], pieces[2])


def layer_forward(inputs, w_qkv, w_out, w_up, w_down, vec_rows, bias_up, head_count):
    length, features = inputs.shape
    head_size = features // head_count
    normed_one, inv_one = normalize(inputs)
    normed_low = (normed_one * vec_rows[0] + vec_rows[1]).astype(jnp.bfloat16)
    qkv_bias = jnp.concatenate([vec_rows[2], jnp.zeros_like(vec_rows[2]), vec_rows[3]])
    qkv_low = (col_contract(normed_low, w_qkv) + qkv_bias).astype(
        jnp.bfloat16
    )
    queries, key_heads, value_heads = split_heads(qkv_low, head_count)
    scores = jnp.einsum(
        "qhd,khd->hqk", queries, key_heads, preferred_element_type=jnp.float32
    ) * head_size ** (-0.5)
    row_max = jnp.max(scores, -1, keepdims=True)
    exponent = jnp.exp(scores - row_max)
    row_sum = jnp.sum(exponent, -1, keepdims=True)
    log_total = row_max + jnp.log(row_sum)
    prob_low = (exponent / row_sum).astype(jnp.bfloat16)
    attended = jnp.einsum("hqk,khd->qhd", prob_low, value_heads, preferred_element_type=jnp.float32)
    attn_low = attended.reshape(length, features).astype(jnp.bfloat16)
    middle = inputs + (col_contract(attn_low, w_out) + vec_rows[4])
    normed_two, inv_two = normalize(middle)
    hidden_low = (normed_two * vec_rows[5] + vec_rows[6]).astype(jnp.bfloat16)
    hidden = col_contract(hidden_low, w_up) + bias_up
    active_low = jax.nn.gelu(hidden, approximate=False).astype(jnp.bfloat16)
    result = middle + (jnp.dot(active_low, w_down, preferred_element_type=jnp.float32) + vec_rows[7])
    stored = (
        normed_one,
        inv_one,
        normed_low,
        qkv_low,
        log_total,
        attn_low,
        normed_two,
        inv_two,
        hidden_low,
        hidden,
        active_low,
    )
    return (result, stored)


def layer_backward(upstream, w_qkv, w_out, w_up, w_down, vec_rows, stored, head_count):
    (
        normed_one,
        inv_one,
        normed_low,
        qkv_low,
        log_total,
        attn_low,
        normed_two,
        inv_two,
        hidden_low,
        hidden,
        active_low,
    ) = stored
    length, features = upstream.shape
    head_size = features // head_count
    down_low = upstream.astype(jnp.bfloat16)
    grad_down = row_contract(active_low, down_low)
    up_low = (
        col_contract(down_low, w_down) * gelu_slope(hidden)
    ).astype(jnp.bfloat16)
    grad_up = row_contract(up_low, hidden_low)
    back_hidden = jnp.dot(up_low, w_up, preferred_element_type=jnp.float32)
    middle_grad = upstream + norm_back(back_hidden, normed_two, inv_two, vec_rows[5])
    out_low = middle_grad.astype(jnp.bfloat16)
    grad_out = row_contract(out_low, attn_low)
    attn_grad = (
        jnp.dot(out_low, w_out, preferred_element_type=jnp.float32).astype(jnp.bfloat16).reshape(length, head_count, head_size)
    )
    queries, key_heads, value_heads = split_heads(qkv_low, head_count)
    scores = jnp.einsum(
        "qhd,khd->hqk", queries, key_heads, preferred_element_type=jnp.float32
    ) * head_size ** (-0.5)
    prob_rows = jnp.exp(scores - log_total)
    value_grad = jnp.einsum(
        "hqk,qhd->khd",
        prob_rows.astype(jnp.bfloat16),
        attn_grad,
        preferred_element_type=jnp.float32,
    )
    prob_grad = jnp.einsum(
        "qhd,khd->hqk", attn_grad, value_heads, preferred_element_type=jnp.float32
    )
    score_low = (
        prob_rows * (prob_grad - jnp.sum(prob_grad * prob_rows, -1, keepdims=True))
    ).astype(jnp.bfloat16)
    query_grad = jnp.einsum(
        "hqk,khd->qhd", score_low, key_heads, preferred_element_type=jnp.float32
    ) * head_size ** (-0.5)
    key_grad = jnp.einsum(
        "hqk,qhd->khd", score_low, queries, preferred_element_type=jnp.float32
    ) * head_size ** (-0.5)
    qkv_grad = jnp.concatenate(
        [
            query_grad.reshape(length, features),
            key_grad.reshape(length, features),
            value_grad.reshape(length, features),
        ],
        1,
    ).astype(jnp.bfloat16)
    grad_qkv = row_contract(qkv_grad, normed_low)
    back_normed = jnp.dot(qkv_grad, w_qkv, preferred_element_type=jnp.float32)
    input_grad = middle_grad + norm_back(back_normed, normed_one, inv_one, vec_rows[0])
    qkv_sum = jnp.sum(qkv_grad.astype(jnp.float32), 0)
    vec_grad = (
            jnp.stack(
                [
                    jnp.sum(back_normed * normed_one, 0),
                    jnp.sum(back_normed, 0),
                    qkv_sum[:features],
                    qkv_sum[2 * features :],
                    jnp.sum(out_low.astype(jnp.float32), 0),
                    jnp.sum(back_hidden * normed_two, 0),
                    jnp.sum(back_hidden, 0),
                    jnp.sum(down_low.astype(jnp.float32), 0),
                ]
            ),
            jnp.sum(up_low.astype(jnp.float32), 0),
    )
    return (input_grad, (grad_qkv, grad_out, grad_up, grad_down), vec_grad)


BLK = 96
RINGX = 4
RINGZ = 4


def near(part, change, only=None):
    pairs = [(at, change(at)) for at in range(16)]
    if only is not None:
        pairs = [pair for pair in pairs if only(pair[1])]
    return lax.ppermute(part, "dp", pairs)


def other_core(part):
    return near(part, lambda at: at ^ 1)


def other_row(part):
    return near(part, lambda at: at ^ 2)


def along_x(part, hops, only=None):
    return near(part, lambda at: (at + 4 * hops) % 16, only)


def along_group(part, flip, hops):
    pairs = [(at, (at ^ (4 * flip)) // 4 * 4 + (at + hops) % RINGZ) for at in range(8)]
    return lax.ppermute(part, "group", pairs)


STEPS = [(flip, hops) for flip in range(2) for hops in range(RINGZ)]


def sum_everywhere(part):
    part = part + other_core(part)
    part = part + other_row(part)
    part = part + along_x(part, 1) + along_x(part, 2) + along_x(part, 3)
    part = part + along_group(part, 0, 1) + along_group(part, 0, 2) + along_group(part, 0, 3)
    return part + along_group(part, 1, 0)


class Place:
    def __init__(self):
        spot = lax.axis_index("dp")
        self.x = spot // 4
        self.row = (spot // 2) % 2
        self.core = spot % 2
        group = lax.axis_index("group")
        self.flip = group // RINGZ
        self.z = group % RINGZ


def rotate(parts, start):
    return lax.dynamic_slice_in_dim(jnp.concatenate([parts, parts], 0), start, RINGX, 0)


def pick(flag, parts, axis):
    first, second = jnp.split(parts, 2, axis)
    first, second = first.squeeze(axis), second.squeeze(axis)
    return jnp.where(flag == 0, first, second), jnp.where(flag == 0, second, first)


def ordered(flag, own, other, axis):
    return jnp.where(flag == 0, jnp.stack([own, other], axis), jnp.stack([other, own], axis))


def to_own_order(row, place):
    cube = row.reshape(RINGX, 2, 2, BLK)
    cube = jnp.stack(pick(place.core, cube, 2))
    cube = jnp.stack(pick(place.row, cube, 2), 1)
    cube = rotate(cube.transpose(2, 0, 1, 3), place.x).transpose(1, 2, 0, 3)
    return cube.reshape(-1)


def from_own_order(row, place):
    cube = row.reshape(2, 2, RINGX, BLK)
    cube = rotate(cube.transpose(2, 0, 1, 3), (RINGX - place.x) % RINGX)
    cube = ordered(place.row, cube[:, :, 0], cube[:, :, 1], 1)
    cube = ordered(place.core, cube[:, :, 0], cube[:, :, 1], 2)
    return cube.reshape(-1)


def gather_hidden(block, x_first):
    if x_first:
        wide = jnp.stack([block] + [along_x(block, -hops) for hops in (1, 2, 3)])
        wide = jnp.stack([wide, other_row(wide)])
    else:
        pair = jnp.stack([block, other_row(block)])
        wide = jnp.stack([pair] + [along_x(pair, -hops) for hops in (1, 2, 3)], 1)
    return jnp.stack([wide, other_core(wide)]).reshape(-1, block.shape[-1])


def gather_heads(block_qkv, block_out, place):
    own = jnp.stack([block_qkv] + [along_x(block_qkv, -hops) for hops in (1, 2, 3)])
    from_first = [along_x(block_out, hops, lambda at, hops=hops: at // 4 == hops) for hops in (1, 2, 3)]
    whole_out = jnp.where(place.x == 0, block_out, from_first[0] + from_first[1] + from_first[2])
    wide = rotate(own, (RINGX - place.x) % RINGX)
    wide = jnp.concatenate([wide[:3], whole_out[None]], 0)
    wide = ordered(place.row, wide, other_row(wide), 1)
    wide = ordered(place.core, wide, other_core(wide), 2)
    wide = wide.reshape(-1, block_qkv.shape[-1])
    return wide[: 12 * BLK], wide[12 * BLK :]


def half(part):
    return part.astype(jnp.bfloat16)


def full(part):
    return part.astype(jnp.float32)


def scatter_hidden(grad, row_first):
    cube = grad.reshape(2, 2, RINGX, BLK, -1)
    kept = cube[0] + full(other_core(half(cube[1])))
    if row_first:
        kept = kept[0] + full(other_row(half(kept[1])))
        sent = half(kept[1:])
        return kept[0] + sum(full(along_x(sent[hops - 1], hops)) for hops in (1, 2, 3))
    sent = half(kept[:, 1:])
    kept = kept[:, 0] + sum(full(along_x(sent[:, hops - 1], hops)) for hops in (1, 2, 3))
    return kept[0] + full(other_row(half(kept[1])))


def scatter_heads(grad_qkv, grad_out, place):
    cube = jnp.concatenate([grad_qkv, grad_out], 0).reshape(RINGX, 2, 2, BLK, -1)
    mine, theirs = pick(place.core, cube, 2)
    mine = mine + full(other_core(half(theirs)))
    mine, theirs = pick(place.row, mine, 1)
    mine = mine + full(other_row(half(theirs)))
    block_out = half(mine[3])
    turned = rotate(jnp.concatenate([mine[:3], jnp.zeros_like(mine[:1])], 0), place.x)
    sent = half(turned[1:])
    sum_qkv = turned[0] + sum(full(along_x(sent[hops - 1], hops)) for hops in (1, 2, 3))
    arrived = sum(
        full(along_x(block_out, hops, lambda at: at // 4 == 0)) for hops in (1, 2, 3)
    )
    sum_out = jnp.where(place.x == 0, mine[3] + arrived, 0.0)
    return sum_qkv, sum_out


def split_dot(left, right):
    left_high, right_high = half(left), half(right)
    left_low, right_low = half(left - full(left_high)), half(right - full(right_high))

    def product(one, two):
        return jnp.dot(one, two, preferred_element_type=jnp.float32)

    return product(left_high, right_high) + (
        product(left_high, right_low) + product(left_low, right_high)
    )


def newton_kernel(all_ref, own_ref, out_ref):
    size = all_ref.shape[1]
    gram = row_contract(all_ref[...], all_ref[...])
    diagonal = lax.broadcasted_iota(jnp.int32, (size, size), 0) == lax.broadcasted_iota(
        jnp.int32, (size, size), 1
    )
    trace = jnp.sum(jnp.where(diagonal, gram, 0.0), keepdims=True)
    inverse = 1.0 / (jnp.sqrt(trace) + ortho_eps)
    gram = gram * inverse * inverse
    total = None
    for iteration in range(NEWTON_STEPS):
        squared = split_dot(gram, gram)
        step = jnp.where(diagonal, coef_a, 0.0) + coef_b * gram + coef_c * squared
        total = step if total is None else split_dot(step, total)
        if iteration < NEWTON_STEPS - 1:
            gram = split_dot(step, split_dot(step, gram))
    total = total * inverse
    high = half(total)
    low = half(total - full(high))
    own = own_ref[...]
    out_ref[...] = jnp.dot(own, high, preferred_element_type=jnp.float32) + jnp.dot(
        own, low, preferred_element_type=jnp.float32
    )


def on_device(tokens, cotangent, live, slot_of, weights, momentum, vec, vec_first, vec_second):
    place = Place()
    group_at = lax.axis_index("group")
    data_at = lax.axis_index("dp")
    features = weights.shape[1]
    vec_here, vec_cols = vec.shape
    widths = [3 * features, features, FF, FF]
    per_layer = VROWS // LAYERS
    vec_low = full(half(vec))
    spread = lax.dynamic_update_slice(
        jnp.zeros((VROWS, features), jnp.float32),
        vec_low,
        (group_at * vec_here, data_at * vec_cols),
    )
    vec_full = sum_everywhere(spread)
    own_block = half(weights[0].T)
    slots = jnp.stack(
        [
            own_block if (flip, hops) == (0, 0) else along_group(own_block, flip, -hops)
            for flip, hops in STEPS
        ]
    )
    blocks = []
    for mat_index in range(MATS):
        slot = slot_of[mat_index]
        at = ((slot // RINGZ) ^ place.flip) * RINGZ + (slot % RINGZ - place.z + RINGZ) % RINGZ
        blocks.append(lax.dynamic_index_in_dim(slots, at, 0, keepdims=False))
    matrices = []
    for layer_at in range(LAYERS):
        four = blocks[4 * layer_at : 4 * layer_at + 4]
        matrices.append(
            gather_heads(four[0], four[1], place)
            + (gather_hidden(four[2], True), gather_hidden(four[3], False))
        )
    stream = tokens[0]
    memory = []
    for layer_at in range(LAYERS):
        vec_rows = vec_full[layer_at * per_layer : (layer_at + 1) * per_layer]
        bias_up = to_own_order(vec_rows[8:].reshape(-1), place)
        stream, stored = layer_forward(stream, *matrices[layer_at], vec_rows, bias_up, HEADS)
        memory.append(stored)
    upstream = cotangent[0] * full(live)[0]
    mat_sums = [None] * MATS
    vec_grads = [None] * LAYERS
    for layer_at in range(LAYERS - 1, -1, -1):
        vec_rows = vec_full[layer_at * per_layer : (layer_at + 1) * per_layer]
        upstream, four_grads, (vec_top, bias_grad) = layer_backward(
            upstream, *matrices[layer_at], vec_rows, memory[layer_at], HEADS
        )
        vec_grads[layer_at] = jnp.concatenate(
            [vec_top, from_own_order(bias_grad, place).reshape(-1, features)], 0
        )
        mat_sums[4 * layer_at + 2] = scatter_hidden(four_grads[2], True)
        mat_sums[4 * layer_at + 3] = scatter_hidden(four_grads[3], False)
        mat_sums[4 * layer_at], mat_sums[4 * layer_at + 1] = scatter_heads(
            four_grads[0], four_grads[1], place
        )
    stacked = jnp.stack(mat_sums)
    slot_ids = lax.iota(jnp.int32, MATS)
    slot_match = slot_of[None, :] == slot_ids[:, None]
    mat_of = jnp.sum(jnp.where(slot_match, slot_ids[None, :], 0), 1)

    def for_slot(flip, hops):
        slot = (place.flip ^ flip) * RINGZ + (place.z + hops) % RINGZ
        return lax.dynamic_index_in_dim(stacked, mat_of[slot], 0, keepdims=False)

    grad_rows = for_slot(0, 0) + sum(
        full(along_group(half(for_slot(flip, hops)), flip, hops)) for flip, hops in STEPS[1:]
    )
    vec_sum = sum_everywhere(jnp.concatenate(vec_grads, 0))
    shard_vec = lax.dynamic_slice(
        vec_sum, (group_at * vec_here, data_at * vec_cols), (vec_here, vec_cols)
    )
    moment_rows = momentum_keep * momentum[0].T + grad_rows
    moment_low = half(moment_rows)
    moment_all = gather_hidden(moment_low, True)
    ortho_rows = pl.pallas_call(
        newton_kernel,
        out_shape=jax.ShapeDtypeStruct((BLK, features), jnp.float32),
        in_specs=[pl.BlockSpec(memory_space=pltpu.VMEM)] * 2,
        out_specs=pl.BlockSpec(memory_space=pltpu.VMEM),
        compiler_params=pltpu.CompilerParams(vmem_limit_bytes=48 << 20),
        name="newton",
    )(moment_all, moment_low)
    width_row = jnp.array(widths * LAYERS, jnp.float32)
    slot_width = jnp.sum(jnp.where(slot_of == group_at, width_row, 0.0))
    step_scale = muon_rate * muon_shape * jnp.sqrt(slot_width)
    new_weights = weights * (1.0 - muon_rate * muon_decay) - step_scale * ortho_rows.T[None]
    first_new = first_keep * vec_first + (1.0 - first_keep) * shard_vec
    second_new = second_keep * vec_second + (1.0 - second_keep) * shard_vec * shard_vec
    vec_new = vec - adam_rate * (
        first_new
        / (1.0 - first_keep**STEP)
        / (jnp.sqrt(second_new / (1.0 - second_keep**STEP)) + adam_eps)
    )
    return (
        stream[None],
        upstream[None],
        grad_rows.T[None],
        moment_rows.T[None],
        new_weights,
        first_new,
        second_new,
        vec_new,
    )


def solution(mesh):
    placed = (
        P(("group", "dp"), None, None),
        P(("group", "dp"), None, None),
        P(("group", "dp")),
        P(),
        P("group", None, "dp"),
        P("group", None, "dp"),
        P("group", "dp"),
        P("group", "dp"),
        P("group", "dp"),
    )
    return jax.shard_map(
        on_device,
        mesh=mesh,
        in_specs=placed,
        out_specs=(
            P(("group", "dp"), None, None),
            P(("group", "dp"), None, None),
            P("group", None, "dp"),
            P("group", None, "dp"),
            P("group", None, "dp"),
            P("group", "dp"),
            P("group", "dp"),
            P("group", "dp"),
        ),
        check_vma=False,
    )
```

```python
import jax
import jax.numpy as jnp
from jax import lax
from jax.experimental import pallas as pl
from jax.experimental.pallas import tpu as pltpu
from jax.sharding import PartitionSpec as P

HEADS = 6
FF = 1536
LAYERS = 2
NEWTON_STEPS = 5
STEP = 10
MATS = 8
VROWS = 24


norm_eps = 1e-06
ortho_eps = 1e-07
coef_a = 3.4445
coef_b = -4.775
coef_c = 2.0315
momentum_keep = 0.95
muon_rate = 0.25
muon_decay = 0.01
muon_shape = 0.5
adam_rate = 0.4
first_keep = 0.9
second_keep = 0.999
adam_eps = 1e-08
half_root = 0.7071067811865476
density = 0.3989422804014327


def normalize(values):
    center = values - jnp.mean(values, -1, keepdims=True)
    inv_std = lax.rsqrt(jnp.mean(center * center, -1, keepdims=True) + norm_eps)
    return (center * inv_std, inv_std)


def norm_back(upstream, normed, inv_std, gain):
    scaled = upstream * gain
    return inv_std * (
        scaled
        - jnp.mean(scaled, -1, keepdims=True)
        - normed * jnp.mean(scaled * normed, -1, keepdims=True)
    )


def gelu_slope(values):
    return (
        0.5 * (1.0 + lax.erf(values * half_root))
        + values * jnp.exp(-0.5 * values * values) * density
    )


def row_contract(left_op, right_op):
    return lax.dot_general(
        left_op, right_op, (((0,), (0,)), ((), ())), preferred_element_type=jnp.float32
    )


def col_contract(left_op, right_op):
    return lax.dot_general(
        left_op, right_op, (((1,), (1,)), ((), ())), preferred_element_type=jnp.float32
    )


BLK = 96
WIDE = 384
VPAD = 32
RINGX = 4
RINGZ = 4
STEPS = [(flip, hops) for flip in range(2) for hops in range(RINGZ)]


def half(part):
    return part.astype(jnp.bfloat16)


def full(part):
    return part.astype(jnp.float32)


def near(part, change):
    return lax.ppermute(part, "dp", [(at, change(at)) for at in range(16)])


def other_core(part):
    return near(part, lambda at: at ^ 1)


def other_row(part):
    return near(part, lambda at: at ^ 2)


def along_x(part, hops):
    return near(part, lambda at: (at + 4 * hops) % 16)


def along_group(part, flip, hops):
    pairs = [(at, (at ^ (4 * flip)) // 4 * 4 + (at + hops) % RINGZ) for at in range(8)]
    return lax.ppermute(part, "group", pairs)


def my_place():
    spot = lax.axis_index("dp")
    return spot >> 2, (spot >> 1) & 1, spot & 1


def my_group():
    group = lax.axis_index("group")
    return group >> 2, group & 3


def rows_at(start, count=BLK):
    return pl.ds(pl.multiple_of(start, 32), count)


def small_call(kernel, outs, ins, slot_first=False, scratch=(), name=None, vmem=32):
    specs = [pl.BlockSpec(memory_space=pltpu.VMEM)] * len(ins)
    if slot_first:
        specs[0] = pl.BlockSpec(memory_space=pltpu.SMEM)
    return pl.pallas_call(
        kernel,
        out_shape=[jax.ShapeDtypeStruct((rows, WIDE), kind) for rows, kind in outs],
        in_specs=specs,
        out_specs=[pl.BlockSpec(memory_space=pltpu.VMEM)] * len(outs),
        scratch_shapes=list(scratch),
        compiler_params=pltpu.CompilerParams(vmem_limit_bytes=vmem << 20),
        name=name,
    )(*ins)


def choose_kernel(slot_ref, *refs):
    blocks, (first_ref, second_ref, third_ref), hold = refs[:8], refs[8:11], refs[11]
    flip, z = my_group()
    spread = None
    for at, block in enumerate(blocks):
        hold[at] = block[:BLK]
        piece = full(block[BLK:])
        spread = piece if spread is None else spread + piece

    def matrix(mat_index):
        slot = slot_ref[mat_index]
        return hold[((slot >> 2) ^ flip) * RINGZ + ((slot - z) & 3)]

    first_ref[:BLK] = matrix(0)
    first_ref[BLK : 2 * BLK] = matrix(1)
    first_ref[2 * BLK :] = half(spread)
    second_ref[:BLK] = matrix(2)
    second_ref[BLK:] = matrix(3)
    for member in range(4):
        third_ref[member * BLK : (member + 1) * BLK] = matrix(4 + member)


def merge_x_kernel(heads, hidden, spread, *refs):
    parts, out_ref, hold = refs[:4], refs[4], refs[5]
    x, _, _ = my_place()
    for at in range(4):
        hold[at] = parts[at][...]
    put = 0
    if heads:
        for at in range(3):
            out_ref[at * BLK : (at + 1) * BLK] = hold[(at - x) & 3, :BLK]
        out_ref[3 * BLK : 4 * BLK] = hold[(0 - x) & 3, BLK : 2 * BLK]
        put = 4 * BLK
    if hidden:
        base = 2 * BLK if heads else 0
        for member in range(2):
            for at in range(4):
                start = base + member * BLK
                out_ref[put : put + BLK] = parts[at][start : start + BLK]
                put += BLK
    if spread:
        base = parts[0].shape[0] - VPAD
        total = full(parts[0][base:])
        for at in range(1, 4):
            total = total + full(parts[at][base:])
        out_ref[put : put + VPAD] = half(total)


def final_kernel(heads, hidden, spread, *refs):
    parts, outs = refs[:4], list(refs[4:])
    _, row, core = my_place()
    base = 0
    if heads:
        qkv_ref, out_ref = outs[:2]
        outs = outs[2:]
        for at_part, part in enumerate(parts):
            piece = (row ^ (at_part & 1)) * 2 * BLK + (core ^ (at_part >> 1)) * BLK
            for at in range(3):
                qkv_ref[rows_at(at * WIDE + piece)] = part[at * BLK : (at + 1) * BLK]
            out_ref[rows_at(piece)] = part[3 * BLK : 4 * BLK]
        base = 4 * BLK
    if hidden:
        for member in range(2):
            for at_part, part in enumerate(parts):
                start = base + member * WIDE
                outs[member][at_part * WIDE : (at_part + 1) * WIDE] = part[start : start + WIDE]
        base += 2 * WIDE
        outs = outs[2:]
    if spread:
        total = full(parts[0][base:])
        for part in parts[1:]:
            total = total + full(part[base:])
        outs[0][...] = total


def gather_steps(part, heads, hidden, spread, name):
    rows = 4 * BLK * heads + 8 * BLK * hidden + VPAD * spread
    parts = [part] + [along_x(part, -hops) for hops in (1, 2, 3)]
    (own,) = small_call(
        lambda *refs: merge_x_kernel(heads, hidden, spread, *refs),
        [(rows, jnp.bfloat16)],
        parts,
        scratch=[pltpu.VMEM((4, *part.shape), jnp.bfloat16)],
        name=name + "_merge_x",
    )
    return own, rows


def gather_last(own, heads, hidden, spread, name):
    beside = other_row(own)
    parts = [own, beside, other_core(own), other_core(beside)]
    outs = []
    if heads:
        outs += [(3 * WIDE, jnp.bfloat16), (WIDE, jnp.bfloat16)]
    if hidden:
        outs += [(FF, jnp.bfloat16)] * 2
    if spread:
        outs += [(VPAD, jnp.float32)]
    return small_call(
        lambda *refs: final_kernel(heads, hidden, spread, *refs), outs, parts, name=name + "_whole"
    )


def put_vec(ref, start, value):
    high = half(value)
    ref[start : start + VPAD] = high
    ref[start + VPAD : start + 2 * VPAD] = half(value - full(high))


def get_vec(ref, start):
    return full(ref[start : start + VPAD]) + full(ref[start + VPAD : start + 2 * VPAD])


def split_core_kernel(heads, hidden, spread, *refs):
    refs = list(refs)
    keep_ref, sent_ref = refs[-2:]
    _, _, core = my_place()
    put = 0
    if heads:
        qkv_ref, out_ref = refs[:2]
        refs = refs[2:]
        for row in range(2):
            for at in range(4):
                source = out_ref if at == 3 else qkv_ref
                start = (0 if at == 3 else at * WIDE) + row * 2 * BLK
                keep_ref[put : put + BLK] = source[rows_at(start + core * BLK)]
                sent_ref[put : put + BLK] = source[rows_at(start + (1 - core) * BLK)]
                put += BLK
    if hidden:
        for source in refs[:2]:
            keep_ref[put : put + 2 * WIDE] = source[: 2 * WIDE]
            sent_ref[put : put + 2 * WIDE] = source[2 * WIDE :]
            put += 2 * WIDE
        refs = refs[2:]
    if spread:
        put_vec(sent_ref, put, refs[0][...])


def split_row_kernel(heads, hidden, spread, *refs):
    had_ref, came_ref = refs[:2]
    keep_ref, sent_ref = refs[2 + spread : 4 + spread]
    _, row, _ = my_place()

    def total(start):
        at = rows_at(start, WIDE)
        return full(had_ref[at]) + full(came_ref[at])

    put, base = 0, 0
    if heads:
        keep_ref[:WIDE] = total(row * WIDE)
        sent_ref[:WIDE] = half(total((1 - row) * WIDE))
        put, base = WIDE, 2 * WIDE
    if hidden:
        for _ in range(2):
            keep_ref[put : put + WIDE] = total(base)
            sent_ref[put : put + WIDE] = half(total(base + WIDE))
            put, base = put + WIDE, base + 2 * WIDE
    if spread:
        value = refs[2][...] + get_vec(came_ref, base)
        refs[-1][...] = value
        put_vec(sent_ref, put, value)


def split_x_kernel(heads, hidden, spread, *refs):
    had_ref, came_ref = refs[:2]
    keep_ref, *sent_refs = refs[2 + spread : 6 + spread]
    hold = refs[-1]
    x, _, _ = my_place()
    count = had_ref.shape[0]
    hold[...] = had_ref[...] + full(came_ref[:count])
    for hops, target in enumerate([keep_ref] + sent_refs):
        kind = target.dtype
        put, base = 0, 0
        if heads:
            at = (x + hops) & 3
            piece = hold[rows_at(at * BLK)]
            target[:BLK] = jnp.where(at == 3, 0.0, piece).astype(kind)
            target[BLK : 2 * BLK] = hold[3 * BLK : 4 * BLK].astype(kind)
            put, base = 2 * BLK, WIDE
        if hidden:
            for _ in range(2):
                start = base + hops * BLK
                target[put : put + BLK] = hold[start : start + BLK].astype(kind)
                put, base = put + BLK, base + WIDE
        if spread and hops:
            value = refs[2][...] + get_vec(came_ref, base)
            refs[-2][...] = value
            put_vec(target, put, value)


def sum_x_kernel(heads, keep_ref, *refs):
    parts, out_ref = refs[:3], refs[3]
    x, _, _ = my_place()
    total = keep_ref[...]
    for part in parts:
        total = total + full(part[...])
    out_ref[...] = total
    if heads:
        out_ref[BLK : 2 * BLK] = jnp.where(x == 0, total[BLK : 2 * BLK], 0.0)


def scatter_core(grads, heads, hidden, spread, name):
    rows = 8 * BLK * heads + 16 * BLK * hidden
    keep, sent = small_call(
        lambda *refs: split_core_kernel(heads, hidden, spread, *refs),
        [(rows, jnp.bfloat16), (rows + 2 * VPAD * spread, jnp.bfloat16)],
        grads,
        name=name + "_split_core",
    )
    return keep, sent


def scatter_row(keep, came, heads, hidden, spread, name, vec_sum=None):
    rows = 4 * BLK * heads + 8 * BLK * hidden
    return small_call(
        lambda *refs: split_row_kernel(heads, hidden, spread, *refs),
        [(rows, jnp.float32), (rows + 2 * VPAD * spread, jnp.bfloat16)]
        + [(VPAD, jnp.float32)] * spread,
        [keep, came] + [vec_sum] * spread,
        name=name + "_split_row",
    )


def scatter_x(keep, came, heads, hidden, spread, name, vec_sum=None):
    rows = 2 * BLK * heads + 2 * BLK * hidden
    return small_call(
        lambda *refs: split_x_kernel(heads, hidden, spread, *refs),
        [(rows, jnp.float32)]
        + [(rows + 2 * VPAD * spread, jnp.bfloat16)] * 3
        + [(VPAD, jnp.float32)] * spread,
        [keep, came] + [vec_sum] * spread,
        scratch=[pltpu.VMEM(keep.shape, jnp.float32)],
        name=name + "_split_x",
    )


def spread_x(sent):
    return [along_x(part, hops + 1) for hops, part in enumerate(sent)]


def split_group_kernel(slot_ref, *refs):
    second_ref, third_ref, keep_ref, *parts = refs[:6]
    vec_ref, own_ref = refs[6], refs[7]
    sent_refs, vec_out, hold = refs[8:15], refs[15], refs[16]
    flip, z = my_group()
    x, _, _ = my_place()
    total = keep_ref[...]
    value = vec_ref[...]
    for part in parts:
        total = total + full(part[: 2 * BLK])
        value = value + get_vec(part, 2 * BLK)
    vec_out[...] = value
    hold[0] = total[:BLK]
    hold[1] = jnp.where(x == 0, total[BLK:], 0.0)
    for member in range(2):
        hold[2 + member] = second_ref[member * BLK : (member + 1) * BLK]
    for member in range(4):
        hold[4 + member] = third_ref[member * BLK : (member + 1) * BLK]
    for at, (turn, hops) in enumerate(STEPS):
        slot = (flip ^ turn) * RINGZ + ((z + hops) & 3)
        mat_index = jnp.int32(0)
        for member in range(1, MATS):
            mat_index = jnp.where(slot_ref[member] == slot, member, mat_index)
        if at == 0:
            own_ref[...] = hold[mat_index]
        else:
            sent_refs[at - 1][:BLK] = half(hold[mat_index])
            put_vec(sent_refs[at - 1], BLK, value)


def renew_kernel(own_ref, *refs):
    parts, (vec_ref, moment_ref) = refs[:7], refs[7:9]
    grad_ref, new_ref, low_ref, vec_out = refs[9:]
    total, value = own_ref[...], vec_ref[...]
    for part in parts:
        total = total + full(part[:BLK])
        value = value + get_vec(part, BLK)
    grad_ref[...] = total
    vec_out[...] = value
    renewed = momentum_keep * moment_ref[...] + total
    new_ref[...] = renewed
    low_ref[...] = half(renewed)


def split_dot(left, right):
    left_high, right_high = half(left), half(right)
    left_low, right_low = half(left - full(left_high)), half(right - full(right_high))

    def product(one, two):
        return jnp.dot(one, two, preferred_element_type=jnp.float32)

    return product(left_high, right_high) + (
        product(left_high, right_low) + product(left_low, right_high)
    )


def newton_kernel(slot_ref, *refs):
    parts, own_ref, weight_ref, out_ref = refs[:4], refs[4], refs[5], refs[6]
    size = WIDE
    gram = None
    for part in parts:
        piece = row_contract(part[...], part[...])
        gram = piece if gram is None else gram + piece
    diagonal = lax.broadcasted_iota(jnp.int32, (size, size), 0) == lax.broadcasted_iota(
        jnp.int32, (size, size), 1
    )
    trace = jnp.sum(jnp.where(diagonal, gram, 0.0), keepdims=True)
    inverse = 1.0 / (jnp.sqrt(trace) + ortho_eps)
    gram = gram * inverse * inverse
    total = None
    for iteration in range(NEWTON_STEPS):
        squared = split_dot(gram, gram)
        step = jnp.where(diagonal, coef_a, 0.0) + coef_b * gram + coef_c * squared
        total = step if total is None else split_dot(step, total)
        if iteration < NEWTON_STEPS - 1:
            gram = split_dot(step, split_dot(step, gram))
    total = total * inverse
    high = half(total)
    low = half(total - full(high))
    own = own_ref[...]
    ortho = jnp.dot(own, high, preferred_element_type=jnp.float32) + jnp.dot(
        own, low, preferred_element_type=jnp.float32
    )
    group = lax.axis_index("group")
    widths = [3 * WIDE, WIDE, FF, FF] * LAYERS
    scale = jnp.float32(0.0)
    for member in range(MATS):
        rate = muon_rate * muon_shape * widths[member] ** 0.5
        scale = jnp.where(slot_ref[member] == group, jnp.float32(rate), scale)
    out_ref[...] = weight_ref[...] * (1.0 - muon_rate * muon_decay) - scale * ortho


def turned(part):
    return half(full(part).T)


def attend_kernel(q_ref, k_ref, v_ref, out_ref, prob_ref):
    queries, keys, values = q_ref[...], k_ref[...], v_ref[...]
    queries = queries * jnp.bfloat16(0.125)
    lane = lax.broadcasted_iota(jnp.int32, keys.shape, 1)
    values_t = turned(values)
    sums = []
    for head in range(2):
        mine = half(jnp.where((lane >> 6) == head, 1.0, 0.0))
        scores = col_contract(keys * mine, queries)
        exponent = jnp.exp(scores - jnp.max(scores, 0, keepdims=True))
        probs = half(exponent * (1.0 / jnp.sum(exponent, 0, keepdims=True)))
        prob_ref[head] = probs
        sums.append(jnp.dot(values_t, probs, preferred_element_type=jnp.float32))
    row = lax.broadcasted_iota(jnp.int32, sums[0].shape, 0)
    out_ref[...] = half(jnp.where(row < 64, sums[0], sums[1]).T)


def attend(qkv_low):
    length = qkv_low.shape[0]

    def part(offset):
        return pl.BlockSpec((length, 128), lambda at: (0, offset + at))

    return pl.pallas_call(
        attend_kernel,
        grid=(HEADS // 2,),
        out_shape=[
            jax.ShapeDtypeStruct((length, WIDE), jnp.bfloat16),
            jax.ShapeDtypeStruct((HEADS, length, length), jnp.bfloat16),
        ],
        in_specs=[part(0), part(3), part(6)],
        out_specs=[part(0), pl.BlockSpec((2, length, length), lambda at: (at, 0, 0))],
        compiler_params=pltpu.CompilerParams(vmem_limit_bytes=32 << 20),
        cost_estimate=pl.CostEstimate(
            flops=4 * HEADS * length * length * 64 * 4,
            bytes_accessed=HEADS * length * length * 2 + 4 * length * WIDE * 2,
            transcendentals=HEADS * length * length,
        ),
        name="attend",
    )(qkv_low, qkv_low, qkv_low)


def attend_back_kernel(q_ref, k_ref, v_ref, up_ref, prob_ref, out_ref):
    queries, keys, values, upstream = q_ref[...], k_ref[...], v_ref[...], up_ref[...]
    lane = lax.broadcasted_iota(jnp.int32, keys.shape, 1)
    keys_t = turned(keys)
    got = []
    for head in range(2):
        mine = half(jnp.where((lane >> 6) == head, 1.0, 0.0))
        probs_low = prob_ref[head]
        probs = full(probs_low)
        prob_grad = col_contract(values * mine, upstream)
        inner = jnp.sum(prob_grad * probs, 0, keepdims=True)
        score_low = half(probs * (prob_grad - inner))
        got.append(
            (
                jnp.dot(keys_t, score_low, preferred_element_type=jnp.float32),
                jnp.dot(score_low, queries, preferred_element_type=jnp.float32),
                jnp.dot(probs_low, upstream, preferred_element_type=jnp.float32),
            )
        )
    row = lax.broadcasted_iota(jnp.int32, got[0][0].shape, 0)
    at = pl.program_id(0)
    query_grad = jnp.where(row < 64, got[0][0], got[1][0]).T * 0.125
    key_grad = jnp.where(lane < 64, got[0][1], got[1][1]) * 0.125
    value_grad = jnp.where(lane < 64, got[0][2], got[1][2])
    for third, value in enumerate((query_grad, key_grad, value_grad)):
        out_ref[:, pl.ds(pl.multiple_of(third * WIDE + at * 128, 128), 128)] = half(value)


def attend_back(qkv_low, attn_grad, probs):
    length = qkv_low.shape[0]

    def part(offset):
        return pl.BlockSpec((length, 128), lambda at: (0, offset + at))

    return pl.pallas_call(
        attend_back_kernel,
        grid=(HEADS // 2,),
        out_shape=jax.ShapeDtypeStruct(qkv_low.shape, jnp.bfloat16),
        in_specs=[
            part(0),
            part(3),
            part(6),
            part(0),
            pl.BlockSpec((2, length, length), lambda at: (at, 0, 0)),
        ],
        out_specs=pl.BlockSpec(qkv_low.shape, lambda at: (0, 0)),
        compiler_params=pltpu.CompilerParams(vmem_limit_bytes=32 << 20),
        cost_estimate=pl.CostEstimate(
            flops=8 * HEADS * length * length * 64 * 4,
            bytes_accessed=HEADS * length * length * 2 + 8 * length * WIDE * 2,
            transcendentals=0,
        ),
        name="attend_back",
    )(qkv_low, qkv_low, qkv_low, attn_grad, probs)


def attention_forward(inputs, w_qkv, w_out, vec_rows):
    normed_one, inv_one = normalize(inputs)
    normed_low = half(normed_one * vec_rows[0] + vec_rows[1])
    qkv_bias = jnp.concatenate([vec_rows[2], jnp.zeros_like(vec_rows[2]), vec_rows[3]])
    qkv_low = half(col_contract(normed_low, w_qkv) + qkv_bias)
    attn_low, probs = attend(qkv_low)
    middle = inputs + (col_contract(attn_low, w_out) + vec_rows[4])
    return middle, (normed_one, inv_one, normed_low, qkv_low, probs, attn_low)


def hidden_forward(middle, w_up, w_down, vec_rows, bias_up):
    normed_two, inv_two = normalize(middle)
    hidden_low = half(normed_two * vec_rows[5] + vec_rows[6])
    hidden = col_contract(hidden_low, w_up) + bias_up
    active_low = half(jax.nn.gelu(hidden, approximate=False))
    result = middle + (jnp.dot(active_low, w_down, preferred_element_type=jnp.float32) + vec_rows[7])
    return result, (normed_two, inv_two, hidden_low, hidden, active_low)


def hidden_backward(upstream, w_up, w_down, vec_rows, stored):
    normed_two, inv_two, hidden_low, hidden, active_low = stored
    down_low = half(upstream)
    grad_down = half(row_contract(active_low, down_low))
    up_low = half(col_contract(down_low, w_down) * gelu_slope(hidden))
    grad_up = half(row_contract(up_low, hidden_low))
    back_hidden = jnp.dot(up_low, w_up, preferred_element_type=jnp.float32)
    middle_grad = upstream + norm_back(back_hidden, normed_two, inv_two, vec_rows[5])
    sums = [
        jnp.sum(back_hidden * normed_two, 0),
        jnp.sum(back_hidden, 0),
        jnp.sum(full(down_low), 0),
    ]
    return middle_grad, grad_up, grad_down, sums, jnp.sum(full(up_low), 0)


def attention_backward(middle_grad, w_qkv, w_out, vec_rows, stored):
    normed_one, inv_one, normed_low, qkv_low, probs, attn_low = stored
    out_low = half(middle_grad)
    grad_out = half(row_contract(out_low, attn_low))
    attn_grad = half(jnp.dot(out_low, w_out, preferred_element_type=jnp.float32))
    qkv_grad = attend_back(qkv_low, attn_grad, probs)
    grad_qkv = half(row_contract(qkv_grad, normed_low))
    back_normed = jnp.dot(qkv_grad, w_qkv, preferred_element_type=jnp.float32)
    input_grad = middle_grad + norm_back(back_normed, normed_one, inv_one, vec_rows[0])
    qkv_sum = jnp.sum(full(qkv_grad), 0)
    sums = [
        jnp.sum(back_normed * normed_one, 0),
        jnp.sum(back_normed, 0),
        qkv_sum[:WIDE],
        qkv_sum[2 * WIDE :],
        jnp.sum(full(out_low), 0),
    ]
    return input_grad, grad_qkv, grad_out, sums


def turn(parts, count):
    turned_parts = [jnp.roll(parts, -by, 0) for by in range(RINGX)]
    low = jnp.where((count & 1) == 0, turned_parts[0], turned_parts[1])
    high = jnp.where((count & 1) == 0, turned_parts[2], turned_parts[3])
    return jnp.where((count & 2) == 0, low, high)


def swap(parts, flag, axis):
    return jnp.where(flag == 0, parts, jnp.flip(parts, axis))


def to_own_order(row, place):
    cube = row.reshape(RINGX, 2, 2, BLK)
    cube = turn(swap(swap(cube, place[2], 2), place[1], 1), place[0])
    return cube.transpose(2, 1, 0, 3).reshape(-1)


def from_own_order(row, place):
    cube = row.reshape(2, 2, RINGX, BLK).transpose(2, 1, 0, 3)
    cube = swap(swap(turn(cube, (4 - place[0]) & 3), place[2], 2), place[1], 1)
    return cube.reshape(-1)


def on_device(tokens, cotangent, live, slot_of, weights, momentum, vec, vec_first, vec_second):
    place = my_place()
    group_at = lax.axis_index("group")
    data_at = lax.axis_index("dp")
    vec_here, vec_cols = vec.shape
    per_layer = VROWS // LAYERS
    tie = lax.optimization_barrier
    spread = lax.dynamic_update_slice(
        jnp.zeros((VPAD, WIDE), jnp.bfloat16),
        half(vec),
        (group_at * vec_here, data_at * vec_cols),
    )
    own_block = jnp.concatenate([half(weights[0].T), spread], 0)
    slots = [own_block] + [along_group(own_block, flip, -hops) for flip, hops in STEPS[1:]]
    first, second, third = small_call(
        choose_kernel,
        [(2 * BLK + VPAD, jnp.bfloat16), (2 * BLK, jnp.bfloat16), (4 * BLK, jnp.bfloat16)],
        [slot_of] + slots,
        slot_first=True,
        scratch=[pltpu.VMEM((MATS, BLK, WIDE), jnp.bfloat16)],
        name="choose",
    )
    first_x, _ = gather_steps(first, True, False, True, "first")
    second, first_x = tie((second, first_x))
    second_x, _ = gather_steps(second, False, True, False, "second")
    w_qkv0, w_out0, vec_full = gather_last(first_x, True, False, True, "first")
    third, second_x = tie((third, second_x))
    third_x, _ = gather_steps(third, True, True, False, "third")
    w_up0, w_down0 = gather_last(second_x, False, True, False, "second")
    w_qkv1, w_out1, w_up1, w_down1 = gather_last(third_x, True, True, False, "third")
    rows0, rows1 = vec_full[:per_layer], vec_full[per_layer:VROWS]
    bias0 = to_own_order(rows0[8:].reshape(-1), place)
    bias1 = to_own_order(rows1[8:].reshape(-1), place)

    middle, attn0 = attention_forward(tokens[0], w_qkv0, w_out0, rows0)
    stream, mlp0 = hidden_forward(middle, w_up0, w_down0, rows0, bias0)
    middle, attn1 = attention_forward(stream, w_qkv1, w_out1, rows1)
    stream, mlp1 = hidden_forward(middle, w_up1, w_down1, rows1, bias1)

    upstream = cotangent[0] * full(live)[0]
    mid_grad, grad_up, grad_down, sums_two1, sums_up1 = hidden_backward(
        upstream, w_up1, w_down1, rows1, mlp1
    )
    upstream, grad_qkv, grad_out, sums_one1 = attention_backward(
        mid_grad, w_qkv1, w_out1, rows1, attn1
    )
    keep, sent = scatter_core([grad_qkv, grad_out, grad_up, grad_down], True, True, False, "third")
    upstream, sent = tie((upstream, sent))
    came = other_core(sent)
    mid_grad, grad_up, grad_down, sums_two0, sums_up0 = hidden_backward(
        upstream, w_up0, w_down0, rows0, mlp0
    )
    keep, sent = scatter_row(keep, came, True, True, False, "third")
    keep_f, sent_f = scatter_core([grad_up, grad_down], False, True, False, "second")
    mid_grad, sent, sent_f = tie((mid_grad, sent, sent_f))
    came = other_row(sent)
    came_f = other_core(sent_f)
    token_grad, grad_qkv, grad_out, sums_one0 = attention_backward(
        mid_grad, w_qkv0, w_out0, rows0, attn0
    )
    keep_f, sent_f = scatter_row(keep_f, came_f, False, True, False, "second")
    keep, *sent_x = scatter_x(keep, came, True, True, False, "third")

    def by_layer(one, two, sums_up):
        return one[:4] + [one[4]] + two + [
            from_own_order(sums_up, place).reshape(-1, WIDE)
        ]

    def vec_rows_of(parts):
        return jnp.concatenate([part.reshape(-1, WIDE) for part in parts], 0)

    vec_sum = jnp.concatenate(
        [
            vec_rows_of(by_layer(sums_one0, sums_two0, sums_up0)),
            vec_rows_of(by_layer(sums_one1, sums_two1, sums_up1)),
            jnp.zeros((VPAD - VROWS, WIDE), jnp.float32),
        ],
        0,
    )
    keep_h, sent_h = scatter_core([grad_qkv, grad_out, vec_sum], True, False, True, "first")
    sent_h, sent_f = tie((sent_h, sent_f))
    came_h = other_core(sent_h)
    came_f = other_row(sent_f)
    came_x = spread_x(sent_x)
    keep_h, sent_h, vec_sum = scatter_row(keep_h, came_h, True, False, True, "first", vec_sum)
    came_h = other_row(sent_h)
    keep_f, *sent_f = scatter_x(keep_f, came_f, False, True, False, "second")
    (third_sum,) = small_call(
        lambda *refs: sum_x_kernel(True, *refs),
        [(4 * BLK, jnp.float32)],
        [keep] + came_x,
        name="third_sum_x",
    )
    came_f = spread_x(sent_f)
    (second_sum,) = small_call(
        lambda *refs: sum_x_kernel(False, *refs),
        [(2 * BLK, jnp.float32)],
        [keep_f] + came_f,
        name="second_sum_x",
    )
    keep_h, *sent_h, vec_sum = scatter_x(keep_h, came_h, True, False, True, "first", vec_sum)
    came_h = spread_x(sent_h)
    own, *sent_g, vec_sum = small_call(
        split_group_kernel,
        [(BLK, jnp.float32)]
        + [(BLK + 2 * VPAD, jnp.bfloat16)] * 7
        + [(VPAD, jnp.float32)],
        [slot_of, second_sum, third_sum, keep_h] + came_h + [vec_sum],
        slot_first=True,
        scratch=[pltpu.VMEM((MATS, BLK, WIDE), jnp.float32)],
        name="split_group",
    )
    came_g = [along_group(part, flip, hops) for part, (flip, hops) in zip(sent_g, STEPS[1:])]
    grad_rows, moment_rows, moment_low, vec_sum = small_call(
        renew_kernel,
        [(BLK, jnp.float32), (BLK, jnp.float32), (BLK, jnp.bfloat16), (VPAD, jnp.float32)],
        [own] + came_g + [vec_sum, momentum[0].T],
        name="renew",
    )
    ring = jnp.concatenate([moment_low] + [along_x(moment_low, -hops) for hops in (1, 2, 3)], 0)
    beside = other_row(ring)
    (weight_rows,) = small_call(
        newton_kernel,
        [(BLK, jnp.float32)],
        [slot_of, ring, beside, other_core(ring), other_core(beside), moment_low, weights[0].T],
        slot_first=True,
        name="newton",
    )
    shard_vec = lax.dynamic_slice(
        vec_sum, (group_at * vec_here, data_at * vec_cols), (vec_here, vec_cols)
    )
    first_new = first_keep * vec_first + (1.0 - first_keep) * shard_vec
    second_new = second_keep * vec_second + (1.0 - second_keep) * shard_vec * shard_vec
    vec_new = vec - adam_rate * (
        first_new
        / (1.0 - first_keep**STEP)
        / (jnp.sqrt(second_new / (1.0 - second_keep**STEP)) + adam_eps)
    )
    return (
        stream[None],
        token_grad[None],
        grad_rows.T[None],
        moment_rows.T[None],
        weight_rows.T[None],
        first_new,
        second_new,
        vec_new,
    )


def solution(mesh):
    placed = (
        P(("group", "dp"), None, None),
        P(("group", "dp"), None, None),
        P(("group", "dp")),
        P(),
        P("group", None, "dp"),
        P("group", None, "dp"),
        P("group", "dp"),
        P("group", "dp"),
        P("group", "dp"),
    )
    return jax.shard_map(
        on_device,
        mesh=mesh,
        in_specs=placed,
        out_specs=(
            P(("group", "dp"), None, None),
            P(("group", "dp"), None, None),
            P("group", None, "dp"),
            P("group", None, "dp"),
            P("group", None, "dp"),
            P("group", "dp"),
            P("group", "dp"),
            P("group", "dp"),
        ),
        check_vma=False,
    )
```

```python
import jax
import jax.numpy as jnp
from jax import lax
from jax.experimental import pallas as pl
from jax.experimental.pallas import tpu as pltpu
from jax.sharding import PartitionSpec as P

HEADS = 6
FF = 1536
LAYERS = 2
NEWTON_STEPS = 5
STEP = 10
MATS = 8
VROWS = 24


norm_eps = 1e-06
ortho_eps = 1e-07
coef_a = 3.4445
coef_b = -4.775
coef_c = 2.0315
momentum_keep = 0.95
muon_rate = 0.25
muon_decay = 0.01
muon_shape = 0.5
adam_rate = 0.4
first_keep = 0.9
second_keep = 0.999
adam_eps = 1e-08
half_root = 0.7071067811865476
density = 0.3989422804014327


def normalize(values):
    center = values - jnp.mean(values, -1, keepdims=True)
    inv_std = lax.rsqrt(jnp.mean(center * center, -1, keepdims=True) + norm_eps)
    return (center * inv_std, inv_std)


def norm_back(upstream, normed, inv_std, gain):
    scaled = upstream * gain
    return inv_std * (
        scaled
        - jnp.mean(scaled, -1, keepdims=True)
        - normed * jnp.mean(scaled * normed, -1, keepdims=True)
    )


def gelu_slope(values):
    return (
        0.5 * (1.0 + lax.erf(values * half_root))
        + values * jnp.exp(-0.5 * values * values) * density
    )


def row_contract(left_op, right_op):
    return lax.dot_general(
        left_op, right_op, (((0,), (0,)), ((), ())), preferred_element_type=jnp.float32
    )


def col_contract(left_op, right_op):
    return lax.dot_general(
        left_op, right_op, (((1,), (1,)), ((), ())), preferred_element_type=jnp.float32
    )


BLK = 96
WIDE = 384
VPAD = 32
RINGX = 4
RINGZ = 4
STEPS = [(flip, hops) for flip in range(2) for hops in range(RINGZ)]


def half(part):
    return part.astype(jnp.bfloat16)


def full(part):
    return part.astype(jnp.float32)


def near(part, change):
    return lax.ppermute(part, "dp", [(at, change(at)) for at in range(16)])


def other_core(part):
    return near(part, lambda at: at ^ 1)


def other_row(part):
    return near(part, lambda at: at ^ 2)


def along_x(part, hops):
    return near(part, lambda at: (at + 4 * hops) % 16)


def along_group(part, flip, hops):
    pairs = [(at, (at ^ (4 * flip)) // 4 * 4 + (at + hops) % RINGZ) for at in range(8)]
    return lax.ppermute(part, "group", pairs)


def my_place():
    spot = lax.axis_index("dp")
    return spot >> 2, (spot >> 1) & 1, spot & 1


def my_group():
    group = lax.axis_index("group")
    return group >> 2, group & 3


def rows_at(start, count=BLK):
    return pl.ds(pl.multiple_of(start, 32), count)


def small_call(kernel, outs, ins, slot_first=False, scratch=(), name=None, vmem=32):
    specs = [pl.BlockSpec(memory_space=pltpu.VMEM)] * len(ins)
    if slot_first:
        specs[0] = pl.BlockSpec(memory_space=pltpu.SMEM)
    return pl.pallas_call(
        kernel,
        out_shape=[jax.ShapeDtypeStruct((rows, WIDE), kind) for rows, kind in outs],
        in_specs=specs,
        out_specs=[pl.BlockSpec(memory_space=pltpu.VMEM)] * len(outs),
        scratch_shapes=list(scratch),
        compiler_params=pltpu.CompilerParams(vmem_limit_bytes=vmem << 20),
        name=name,
    )(*ins)


def choose_kernel(slot_ref, *refs):
    pairs, (first_ref, second_ref, third_ref), hold = refs[:4], refs[4:7], refs[7]
    flip, z = my_group()
    spread = None
    for turn, hops in STEPS:
        base = turn * (BLK + VPAD)
        hold[turn * RINGZ + hops] = pairs[hops][base : base + BLK]
        piece = full(pairs[hops][base + BLK : base + BLK + VPAD])
        spread = piece if spread is None else spread + piece

    def matrix(mat_index):
        slot = slot_ref[mat_index]
        return hold[((slot >> 2) ^ flip) * RINGZ + ((slot - z) & 3)]

    first_ref[:BLK] = matrix(0)
    first_ref[BLK : 2 * BLK] = matrix(1)
    first_ref[2 * BLK :] = half(spread)
    second_ref[:BLK] = matrix(2)
    second_ref[BLK:] = matrix(3)
    for member in range(4):
        third_ref[member * BLK : (member + 1) * BLK] = matrix(4 + member)


def merge_x_kernel(heads, hidden, spread, *refs):
    parts, out_ref, hold = refs[:4], refs[4], refs[5]
    x, _, _ = my_place()
    for at in range(4):
        hold[at] = parts[at][...]
    put = 0
    if heads:
        for at in range(3):
            out_ref[at * BLK : (at + 1) * BLK] = hold[(at - x) & 3, :BLK]
        out_ref[3 * BLK : 4 * BLK] = hold[(0 - x) & 3, BLK : 2 * BLK]
        put = 4 * BLK
    if hidden:
        base = 2 * BLK if heads else 0
        for member in range(2):
            for at in range(4):
                start = base + member * BLK
                out_ref[put : put + BLK] = parts[at][start : start + BLK]
                put += BLK
    if spread:
        base = parts[0].shape[0] - VPAD
        total = full(parts[0][base:])
        for at in range(1, 4):
            total = total + full(parts[at][base:])
        out_ref[put : put + VPAD] = half(total)


def final_kernel(heads, hidden, spread, *refs):
    parts, outs = refs[:4], list(refs[4:])
    _, row, core = my_place()
    base = 0
    if heads:
        qkv_ref, out_ref = outs[:2]
        outs = outs[2:]
        for at_part, part in enumerate(parts):
            piece = (row ^ (at_part & 1)) * 2 * BLK + (core ^ (at_part >> 1)) * BLK
            for at in range(3):
                qkv_ref[rows_at(at * WIDE + piece)] = part[at * BLK : (at + 1) * BLK]
            out_ref[rows_at(piece)] = part[3 * BLK : 4 * BLK]
        base = 4 * BLK
    if hidden:
        for member in range(2):
            for at_part, part in enumerate(parts):
                start = base + member * WIDE
                outs[member][at_part * WIDE : (at_part + 1) * WIDE] = part[start : start + WIDE]
        base += 2 * WIDE
        outs = outs[2:]
    if spread:
        total = full(parts[0][base:])
        for part in parts[1:]:
            total = total + full(part[base:])
        outs[0][...] = total


def from_x(part):
    return [part] + [along_x(part, -hops) for hops in (1, 2, 3)]


def merge_x(parts, heads, hidden, spread, name):
    rows = 4 * BLK * heads + 8 * BLK * hidden + VPAD * spread
    (own,) = small_call(
        lambda *refs: merge_x_kernel(heads, hidden, spread, *refs),
        [(rows, jnp.bfloat16)],
        parts,
        scratch=[pltpu.VMEM((4, *parts[0].shape), jnp.bfloat16)],
        name=name + "_merge_x",
    )
    return own


def all_four(own):
    beside = other_row(own)
    return [own, beside, other_core(own), other_core(beside)]


def whole(parts, heads, hidden, spread, name):
    outs = []
    if heads:
        outs += [(3 * WIDE, jnp.bfloat16), (WIDE, jnp.bfloat16)]
    if hidden:
        outs += [(FF, jnp.bfloat16)] * 2
    if spread:
        outs += [(VPAD, jnp.float32)]
    return small_call(
        lambda *refs: final_kernel(heads, hidden, spread, *refs), outs, parts, name=name + "_whole"
    )


def put_vec(ref, start, value):
    high = half(value)
    ref[start : start + VPAD] = high
    ref[start + VPAD : start + 2 * VPAD] = half(value - full(high))


def get_vec(ref, start):
    return full(ref[start : start + VPAD]) + full(ref[start + VPAD : start + 2 * VPAD])


def split_core_kernel(heads, hidden, spread, *refs):
    refs = list(refs)
    keep_ref, sent_ref = refs[-2:]
    _, _, core = my_place()
    put = 0
    if heads:
        qkv_ref, out_ref = refs[:2]
        refs = refs[2:]
        for row in range(2):
            for at in range(4):
                source = out_ref if at == 3 else qkv_ref
                start = (0 if at == 3 else at * WIDE) + row * 2 * BLK
                keep_ref[put : put + BLK] = source[rows_at(start + core * BLK)]
                sent_ref[put : put + BLK] = source[rows_at(start + (1 - core) * BLK)]
                put += BLK
    if hidden:
        for source in refs[:2]:
            keep_ref[put : put + 2 * WIDE] = source[: 2 * WIDE]
            sent_ref[put : put + 2 * WIDE] = source[2 * WIDE :]
            put += 2 * WIDE
        refs = refs[2:]
    if spread:
        put_vec(sent_ref, put, refs[0][...])


def split_row_kernel(heads, hidden, spread, *refs):
    had_ref, came_ref = refs[:2]
    keep_ref, sent_ref = refs[2 + spread : 4 + spread]
    _, row, _ = my_place()

    def total(start):
        at = rows_at(start, WIDE)
        return full(had_ref[at]) + full(came_ref[at])

    put, base = 0, 0
    if heads:
        keep_ref[:WIDE] = total(row * WIDE)
        sent_ref[:WIDE] = half(total((1 - row) * WIDE))
        put, base = WIDE, 2 * WIDE
    if hidden:
        for _ in range(2):
            keep_ref[put : put + WIDE] = total(base)
            sent_ref[put : put + WIDE] = half(total(base + WIDE))
            put, base = put + WIDE, base + 2 * WIDE
    if spread:
        value = refs[2][...] + get_vec(came_ref, base)
        refs[-1][...] = value
        put_vec(sent_ref, put, value)


def split_x_kernel(heads, hidden, spread, *refs):
    had_ref, came_ref = refs[:2]
    keep_ref, *sent_refs = refs[2 + spread : 6 + spread]
    hold = refs[-1]
    x, _, _ = my_place()
    count = had_ref.shape[0]
    hold[...] = had_ref[...] + full(came_ref[:count])
    for hops, target in enumerate([keep_ref] + sent_refs):
        kind = target.dtype
        put, base = 0, 0
        if heads:
            at = (x + hops) & 3
            piece = hold[rows_at(at * BLK)]
            target[:BLK] = jnp.where(at == 3, 0.0, piece).astype(kind)
            target[BLK : 2 * BLK] = hold[3 * BLK : 4 * BLK].astype(kind)
            put, base = 2 * BLK, WIDE
        if hidden:
            for _ in range(2):
                start = base + hops * BLK
                target[put : put + BLK] = hold[start : start + BLK].astype(kind)
                put, base = put + BLK, base + WIDE
        if spread and hops:
            value = refs[2][...] + get_vec(came_ref, base)
            refs[-2][...] = value
            put_vec(target, put, value)


def sum_x_kernel(heads, keep_ref, *refs):
    parts, out_ref = refs[:3], refs[3]
    x, _, _ = my_place()
    total = keep_ref[...]
    for part in parts:
        total = total + full(part[...])
    out_ref[...] = total
    if heads:
        out_ref[BLK : 2 * BLK] = jnp.where(x == 0, total[BLK : 2 * BLK], 0.0)


def scatter_core(grads, heads, hidden, spread, name):
    rows = 8 * BLK * heads + 16 * BLK * hidden
    keep, sent = small_call(
        lambda *refs: split_core_kernel(heads, hidden, spread, *refs),
        [(rows, jnp.bfloat16), (rows + 2 * VPAD * spread, jnp.bfloat16)],
        grads,
        name=name + "_split_core",
    )
    return keep, sent


def scatter_row(keep, came, heads, hidden, spread, name, vec_sum=None):
    rows = 4 * BLK * heads + 8 * BLK * hidden
    return small_call(
        lambda *refs: split_row_kernel(heads, hidden, spread, *refs),
        [(rows, jnp.float32), (rows + 2 * VPAD * spread, jnp.bfloat16)]
        + [(VPAD, jnp.float32)] * spread,
        [keep, came] + [vec_sum] * spread,
        name=name + "_split_row",
    )


def scatter_x(keep, came, heads, hidden, spread, name, vec_sum=None):
    rows = 2 * BLK * heads + 2 * BLK * hidden
    return small_call(
        lambda *refs: split_x_kernel(heads, hidden, spread, *refs),
        [(rows, jnp.float32)]
        + [(rows + 2 * VPAD * spread, jnp.bfloat16)] * 3
        + [(VPAD, jnp.float32)] * spread,
        [keep, came] + [vec_sum] * spread,
        scratch=[pltpu.VMEM(keep.shape, jnp.float32)],
        name=name + "_split_x",
    )


def spread_x(sent):
    return [along_x(part, hops + 1) for hops, part in enumerate(sent)]


def split_group_kernel(slot_ref, *refs):
    second_ref, third_ref, keep_ref, *parts = refs[:6]
    vec_ref, own_ref = refs[6], refs[7]
    sent_refs, vec_out, hold = refs[8:15], refs[15], refs[16]
    flip, z = my_group()
    x, _, _ = my_place()
    total = keep_ref[...]
    value = vec_ref[...]
    for part in parts:
        total = total + full(part[: 2 * BLK])
        value = value + get_vec(part, 2 * BLK)
    vec_out[...] = value
    hold[0] = total[:BLK]
    hold[1] = jnp.where(x == 0, total[BLK:], 0.0)
    for member in range(2):
        hold[2 + member] = second_ref[member * BLK : (member + 1) * BLK]
    for member in range(4):
        hold[4 + member] = third_ref[member * BLK : (member + 1) * BLK]
    for at, (turn, hops) in enumerate(STEPS):
        slot = (flip ^ turn) * RINGZ + ((z + hops) & 3)
        mat_index = jnp.int32(0)
        for member in range(1, MATS):
            mat_index = jnp.where(slot_ref[member] == slot, member, mat_index)
        if at == 0:
            own_ref[...] = hold[mat_index]
        else:
            sent_refs[at - 1][:BLK] = half(hold[mat_index])
            put_vec(sent_refs[at - 1], BLK, value)


def renew_kernel(own_ref, *refs):
    parts, (vec_ref, moment_ref) = refs[:7], refs[7:9]
    grad_ref, new_ref, low_ref, vec_out = refs[9:]
    total, value = own_ref[...], vec_ref[...]
    for part in parts:
        total = total + full(part[:BLK])
        value = value + get_vec(part, BLK)
    grad_ref[...] = total
    vec_out[...] = value
    renewed = momentum_keep * moment_ref[...] + total
    new_ref[...] = renewed
    low_ref[...] = half(renewed)


def parts_of(value):
    high = half(value)
    return high, half(value - full(high))


def as_left(value):
    high, low = parts_of(value)
    return jnp.concatenate([high, high, low], 1)


def as_right(value):
    high, low = parts_of(value)
    return jnp.concatenate([high, low, high], 0)


def product(left, right):
    return jnp.dot(left, right, preferred_element_type=jnp.float32)


def newton_kernel(slot_ref, *refs):
    parts, own_ref, weight_ref, out_ref = refs[:4], refs[4], refs[5], refs[6]
    size = WIDE
    gram = None
    for part in parts:
        piece = row_contract(part[...], part[...])
        gram = piece if gram is None else gram + piece
    diagonal = lax.broadcasted_iota(jnp.int32, (size, size), 0) == lax.broadcasted_iota(
        jnp.int32, (size, size), 1
    )
    trace = jnp.sum(jnp.where(diagonal, gram, 0.0), keepdims=True)
    inverse = 1.0 / (jnp.sqrt(trace) + ortho_eps)
    gram = gram * inverse * inverse
    total = None
    for iteration in range(NEWTON_STEPS):
        squared = product(as_left(gram), as_right(gram))
        step = jnp.where(diagonal, coef_a, 0.0) + coef_b * gram + coef_c * squared
        left = as_left(step)
        if iteration == 0:
            total = step
            gram = product(left, as_right(product(left, as_right(gram))))
        elif iteration < NEWTON_STEPS - 1:
            both = product(left, as_right(jnp.concatenate([gram, total], 1)))
            total = both[:, size:]
            gram = product(left, as_right(both[:, :size]))
        else:
            total = product(left, as_right(total))
    high, low = parts_of(total * inverse)
    own = own_ref[...]
    ortho = product(own, high) + product(own, low)
    group = lax.axis_index("group")
    widths = [3 * WIDE, WIDE, FF, FF] * LAYERS
    scale = jnp.float32(0.0)
    for member in range(MATS):
        rate = muon_rate * muon_shape * widths[member] ** 0.5
        scale = jnp.where(slot_ref[member] == group, jnp.float32(rate), scale)
    out_ref[...] = weight_ref[...] * (1.0 - muon_rate * muon_decay) - scale * ortho


def turned(part):
    return half(full(part).T)


def attend_kernel(q_ref, k_ref, v_ref, out_ref, prob_ref):
    queries, keys, values = q_ref[...], k_ref[...], v_ref[...]
    queries = queries * jnp.bfloat16(0.125)
    lane = lax.broadcasted_iota(jnp.int32, keys.shape, 1)
    values_t = turned(values)
    sums = []
    for head in range(2):
        mine = half(jnp.where((lane >> 6) == head, 1.0, 0.0))
        scores = col_contract(keys * mine, queries)
        exponent = jnp.exp(scores - jnp.max(scores, 0, keepdims=True))
        probs = half(exponent * (1.0 / jnp.sum(exponent, 0, keepdims=True)))
        prob_ref[head] = probs
        sums.append(jnp.dot(values_t, probs, preferred_element_type=jnp.float32))
    row = lax.broadcasted_iota(jnp.int32, sums[0].shape, 0)
    out_ref[...] = half(jnp.where(row < 64, sums[0], sums[1]).T)


def attend(qkv_low):
    length = qkv_low.shape[0]

    def part(offset):
        return pl.BlockSpec((length, 128), lambda at: (0, offset + at))

    return pl.pallas_call(
        attend_kernel,
        grid=(HEADS // 2,),
        out_shape=[
            jax.ShapeDtypeStruct((length, WIDE), jnp.bfloat16),
            jax.ShapeDtypeStruct((HEADS, length, length), jnp.bfloat16),
        ],
        in_specs=[part(0), part(3), part(6)],
        out_specs=[part(0), pl.BlockSpec((2, length, length), lambda at: (at, 0, 0))],
        compiler_params=pltpu.CompilerParams(vmem_limit_bytes=32 << 20),
        cost_estimate=pl.CostEstimate(flops=1 << 20, bytes_accessed=1 << 16, transcendentals=0),
        name="attend",
    )(qkv_low, qkv_low, qkv_low)


def attend_back_kernel(q_ref, k_ref, v_ref, up_ref, prob_ref, out_ref):
    queries, keys, values, upstream = q_ref[...], k_ref[...], v_ref[...], up_ref[...]
    lane = lax.broadcasted_iota(jnp.int32, keys.shape, 1)
    keys_t = turned(keys)
    got = []
    for head in range(2):
        mine = half(jnp.where((lane >> 6) == head, 1.0, 0.0))
        probs_low = prob_ref[head]
        probs = full(probs_low)
        prob_grad = col_contract(values * mine, upstream)
        inner = jnp.sum(prob_grad * probs, 0, keepdims=True)
        score_low = half(probs * (prob_grad - inner))
        got.append(
            (
                jnp.dot(keys_t, score_low, preferred_element_type=jnp.float32),
                jnp.dot(score_low, queries, preferred_element_type=jnp.float32),
                jnp.dot(probs_low, upstream, preferred_element_type=jnp.float32),
            )
        )
    row = lax.broadcasted_iota(jnp.int32, got[0][0].shape, 0)
    at = pl.program_id(0)
    query_grad = jnp.where(row < 64, got[0][0], got[1][0]).T * 0.125
    key_grad = jnp.where(lane < 64, got[0][1], got[1][1]) * 0.125
    value_grad = jnp.where(lane < 64, got[0][2], got[1][2])
    for third, value in enumerate((query_grad, key_grad, value_grad)):
        out_ref[:, pl.ds(pl.multiple_of(third * WIDE + at * 128, 128), 128)] = half(value)


def attend_back(qkv_low, attn_grad, probs):
    length = qkv_low.shape[0]

    def part(offset):
        return pl.BlockSpec((length, 128), lambda at: (0, offset + at))

    return pl.pallas_call(
        attend_back_kernel,
        grid=(HEADS // 2,),
        out_shape=jax.ShapeDtypeStruct(qkv_low.shape, jnp.bfloat16),
        in_specs=[
            part(0),
            part(3),
            part(6),
            part(0),
            pl.BlockSpec((2, length, length), lambda at: (at, 0, 0)),
        ],
        out_specs=pl.BlockSpec(qkv_low.shape, lambda at: (0, 0)),
        compiler_params=pltpu.CompilerParams(vmem_limit_bytes=32 << 20),
        cost_estimate=pl.CostEstimate(flops=1 << 20, bytes_accessed=1 << 16, transcendentals=0),
        name="attend_back",
    )(qkv_low, qkv_low, qkv_low, attn_grad, probs)


def attention_forward(inputs, w_qkv, w_out, vec_rows, later):
    normed_one, inv_one = normalize(inputs)
    normed_low = half(normed_one * vec_rows[0] + vec_rows[1])
    qkv_bias = jnp.concatenate([vec_rows[2], jnp.zeros_like(vec_rows[2]), vec_rows[3]])
    qkv_low = half(col_contract(normed_low, w_qkv) + qkv_bias)
    attn_low, probs = attend(qkv_low)
    attn_low, later = lax.optimization_barrier((attn_low, later))
    middle = inputs + (col_contract(attn_low, w_out) + vec_rows[4])
    return middle, later, (normed_one, inv_one, normed_low, qkv_low, probs, attn_low)


def hidden_forward(middle, w_up, w_down, vec_rows, bias_up):
    normed_two, inv_two = normalize(middle)
    hidden_low = half(normed_two * vec_rows[5] + vec_rows[6])
    hidden = col_contract(hidden_low, w_up) + bias_up
    active_low = half(jax.nn.gelu(hidden, approximate=False))
    result = middle + (jnp.dot(active_low, w_down, preferred_element_type=jnp.float32) + vec_rows[7])
    return result, (normed_two, inv_two, hidden_low, hidden, active_low)


def hidden_backward_first(upstream, w_down, stored):
    normed_two, inv_two, hidden_low, hidden, active_low = stored
    down_low = half(upstream)
    grad_down = half(row_contract(active_low, down_low))
    up_low = half(col_contract(down_low, w_down) * gelu_slope(hidden))
    return up_low, grad_down, jnp.sum(full(down_low), 0), jnp.sum(full(up_low), 0)


def hidden_backward_second(upstream, up_low, w_up, vec_rows, stored):
    normed_two, inv_two, hidden_low, hidden, active_low = stored
    grad_up = half(row_contract(up_low, hidden_low))
    back_hidden = jnp.dot(up_low, w_up, preferred_element_type=jnp.float32)
    middle_grad = upstream + norm_back(back_hidden, normed_two, inv_two, vec_rows[5])
    return middle_grad, grad_up, [jnp.sum(back_hidden * normed_two, 0), jnp.sum(back_hidden, 0)]


def attention_backward_first(middle_grad, w_out, stored):
    normed_one, inv_one, normed_low, qkv_low, probs, attn_low = stored
    out_low = half(middle_grad)
    grad_out = half(row_contract(out_low, attn_low))
    attn_grad = half(jnp.dot(out_low, w_out, preferred_element_type=jnp.float32))
    return attend_back(qkv_low, attn_grad, probs), grad_out, jnp.sum(full(out_low), 0)


def attention_backward_second(middle_grad, qkv_grad, w_qkv, vec_rows, stored):
    normed_one, inv_one, normed_low, qkv_low, probs, attn_low = stored
    grad_qkv = half(row_contract(qkv_grad, normed_low))
    back_normed = jnp.dot(qkv_grad, w_qkv, preferred_element_type=jnp.float32)
    input_grad = middle_grad + norm_back(back_normed, normed_one, inv_one, vec_rows[0])
    qkv_sum = jnp.sum(full(qkv_grad), 0)
    sums = [
        jnp.sum(back_normed * normed_one, 0),
        jnp.sum(back_normed, 0),
        qkv_sum[:WIDE],
        qkv_sum[2 * WIDE :],
    ]
    return input_grad, grad_qkv, sums


def turn(parts, count):
    turned_parts = [jnp.roll(parts, -by, 0) for by in range(RINGX)]
    low = jnp.where((count & 1) == 0, turned_parts[0], turned_parts[1])
    high = jnp.where((count & 1) == 0, turned_parts[2], turned_parts[3])
    return jnp.where((count & 2) == 0, low, high)


def swap(parts, flag, axis):
    return jnp.where(flag == 0, parts, jnp.flip(parts, axis))


def to_own_order(row, place):
    cube = row.reshape(RINGX, 2, 2, BLK)
    cube = turn(swap(swap(cube, place[2], 2), place[1], 1), place[0])
    return cube.transpose(2, 1, 0, 3).reshape(-1)


def from_own_order(row, place):
    cube = row.reshape(2, 2, RINGX, BLK).transpose(2, 1, 0, 3)
    cube = swap(swap(turn(cube, (4 - place[0]) & 3), place[2], 2), place[1], 1)
    return cube.reshape(-1)


def on_device(tokens, cotangent, live, slot_of, weights, momentum, vec, vec_first, vec_second):
    place = my_place()
    group_at = lax.axis_index("group")
    data_at = lax.axis_index("dp")
    vec_here, vec_cols = vec.shape
    per_layer = VROWS // LAYERS
    tie = lax.optimization_barrier
    spread = lax.dynamic_update_slice(
        jnp.zeros((VPAD, WIDE), jnp.bfloat16),
        half(vec),
        (group_at * vec_here, data_at * vec_cols),
    )
    own_block = jnp.concatenate([half(weights[0].T), spread], 0)
    pair = jnp.concatenate([own_block, along_group(own_block, 1, 0)], 0)
    slots = [pair] + [along_group(pair, 0, -hops) for hops in (1, 2, 3)]
    first, second, third = small_call(
        choose_kernel,
        [(2 * BLK + VPAD, jnp.bfloat16), (2 * BLK, jnp.bfloat16), (4 * BLK, jnp.bfloat16)],
        [slot_of] + slots,
        slot_first=True,
        scratch=[pltpu.VMEM((MATS, BLK, WIDE), jnp.bfloat16)],
        name="choose",
    )
    first_x = merge_x(from_x(first), True, False, True, "first")
    second, third, first_x = tie((second, third, first_x))
    first_parts = all_four(first_x)
    second_parts = from_x(second)
    w_qkv0, w_out0, vec_full = whole(first_parts, True, False, True, "first")
    second_parts, third, w_qkv0 = tie((second_parts, third, w_qkv0))
    second_x = merge_x(second_parts, False, True, False, "second")
    second_x, w_qkv0, third = tie((second_x, w_qkv0, third))
    second_parts = all_four(second_x)
    third_parts = from_x(third)
    rows0, rows1 = vec_full[:per_layer], vec_full[per_layer:VROWS]
    bias0 = to_own_order(rows0[8:].reshape(-1), place)
    bias1 = to_own_order(rows1[8:].reshape(-1), place)

    middle, third_parts, attn0 = attention_forward(tokens[0], w_qkv0, w_out0, rows0, third_parts)
    third_x = merge_x(third_parts, True, True, False, "third")
    third_x, middle = tie((third_x, middle))
    third_parts = all_four(third_x)
    w_up0, w_down0 = whole(second_parts, False, True, False, "second")
    stream, mlp0 = hidden_forward(middle, w_up0, w_down0, rows0, bias0)
    w_qkv1, w_out1, w_up1, w_down1 = whole(third_parts, True, True, False, "third")
    middle, _, attn1 = attention_forward(stream, w_qkv1, w_out1, rows1, ())
    stream, mlp1 = hidden_forward(middle, w_up1, w_down1, rows1, bias1)

    upstream = cotangent[0] * full(live)[0]
    up_low, grad_down, sum_down1, sums_up1 = hidden_backward_first(upstream, w_down1, mlp1)
    mid_grad, grad_up, sums_two1 = hidden_backward_second(upstream, up_low, w_up1, rows1, mlp1)
    qkv_grad, grad_out, sum_out1 = attention_backward_first(mid_grad, w_out1, attn1)
    upstream, grad_qkv, sums_one1 = attention_backward_second(
        mid_grad, qkv_grad, w_qkv1, rows1, attn1
    )
    sums_one1, sums_two1 = sums_one1 + [sum_out1], sums_two1 + [sum_down1]

    keep, sent = scatter_core([grad_qkv, grad_out, grad_up, grad_down], True, True, False, "third")
    upstream, sent = tie((upstream, sent))
    came = other_core(sent)
    up_low, grad_down, sum_down0, sums_up0 = hidden_backward_first(upstream, w_down0, mlp0)
    up_low, came = tie((up_low, came))
    keep, sent = scatter_row(keep, came, True, True, False, "third")
    up_low, sent = tie((up_low, sent))
    came = other_row(sent)
    mid_grad, grad_up, sums_two0 = hidden_backward_second(upstream, up_low, w_up0, rows0, mlp0)
    keep_f, sent_f = scatter_core([grad_up, grad_down], False, True, False, "second")
    mid_grad, sent_f = tie((mid_grad, sent_f))
    came_f = other_core(sent_f)
    qkv_grad, grad_out, sum_out0 = attention_backward_first(mid_grad, w_out0, attn0)
    qkv_grad, came, came_f = tie((qkv_grad, came, came_f))
    keep_f, sent_f = scatter_row(keep_f, came_f, False, True, False, "second")
    keep, *sent_x = scatter_x(keep, came, True, True, False, "third")
    qkv_grad, sent_f, sent_x = tie((qkv_grad, sent_f, sent_x))
    came_f = other_row(sent_f)
    came_x = spread_x(sent_x)
    token_grad, grad_qkv, sums_one0 = attention_backward_second(
        mid_grad, qkv_grad, w_qkv0, rows0, attn0
    )
    sums_one0, sums_two0 = sums_one0 + [sum_out0], sums_two0 + [sum_down0]

    def by_layer(one, two, sums_up):
        return one[:4] + [one[4]] + two + [
            from_own_order(sums_up, place).reshape(-1, WIDE)
        ]

    def vec_rows_of(parts):
        return jnp.concatenate([part.reshape(-1, WIDE) for part in parts], 0)

    vec_sum = jnp.concatenate(
        [
            vec_rows_of(by_layer(sums_one0, sums_two0, sums_up0)),
            vec_rows_of(by_layer(sums_one1, sums_two1, sums_up1)),
            jnp.zeros((VPAD - VROWS, WIDE), jnp.float32),
        ],
        0,
    )
    keep_h, sent_h = scatter_core([grad_qkv, grad_out, vec_sum], True, False, True, "first")
    came_h = other_core(sent_h)
    keep_h, sent_h, vec_sum = scatter_row(keep_h, came_h, True, False, True, "first", vec_sum)
    came_h = other_row(sent_h)
    keep_f, *sent_f = scatter_x(keep_f, came_f, False, True, False, "second")
    (third_sum,) = small_call(
        lambda *refs: sum_x_kernel(True, *refs),
        [(4 * BLK, jnp.float32)],
        [keep] + came_x,
        name="third_sum_x",
    )
    came_f = spread_x(sent_f)
    (second_sum,) = small_call(
        lambda *refs: sum_x_kernel(False, *refs),
        [(2 * BLK, jnp.float32)],
        [keep_f] + came_f,
        name="second_sum_x",
    )
    keep_h, *sent_h, vec_sum = scatter_x(keep_h, came_h, True, False, True, "first", vec_sum)
    came_h = spread_x(sent_h)
    own, *sent_g, vec_sum = small_call(
        split_group_kernel,
        [(BLK, jnp.float32)]
        + [(BLK + 2 * VPAD, jnp.bfloat16)] * 7
        + [(VPAD, jnp.float32)],
        [slot_of, second_sum, third_sum, keep_h] + came_h + [vec_sum],
        slot_first=True,
        scratch=[pltpu.VMEM((MATS, BLK, WIDE), jnp.float32)],
        name="split_group",
    )
    came_g = [along_group(part, flip, hops) for part, (flip, hops) in zip(sent_g, STEPS[1:])]
    grad_rows, moment_rows, moment_low, vec_sum = small_call(
        renew_kernel,
        [(BLK, jnp.float32), (BLK, jnp.float32), (BLK, jnp.bfloat16), (VPAD, jnp.float32)],
        [own] + came_g + [vec_sum, momentum[0].T],
        name="renew",
    )
    ring = jnp.concatenate([moment_low] + [along_x(moment_low, -hops) for hops in (1, 2, 3)], 0)
    beside = other_row(ring)
    (weight_rows,) = small_call(
        newton_kernel,
        [(BLK, jnp.float32)],
        [slot_of, ring, beside, other_core(ring), other_core(beside), moment_low, weights[0].T],
        slot_first=True,
        name="newton",
    )
    shard_vec = lax.dynamic_slice(
        vec_sum, (group_at * vec_here, data_at * vec_cols), (vec_here, vec_cols)
    )
    first_new = first_keep * vec_first + (1.0 - first_keep) * shard_vec
    second_new = second_keep * vec_second + (1.0 - second_keep) * shard_vec * shard_vec
    vec_new = vec - adam_rate * (
        first_new
        / (1.0 - first_keep**STEP)
        / (jnp.sqrt(second_new / (1.0 - second_keep**STEP)) + adam_eps)
    )
    return (
        stream[None],
        token_grad[None],
        grad_rows.T[None],
        moment_rows.T[None],
        weight_rows.T[None],
        first_new,
        second_new,
        vec_new,
    )


def solution(mesh):
    placed = (
        P(("group", "dp"), None, None),
        P(("group", "dp"), None, None),
        P(("group", "dp")),
        P(),
        P("group", None, "dp"),
        P("group", None, "dp"),
        P("group", "dp"),
        P("group", "dp"),
        P("group", "dp"),
    )
    return jax.shard_map(
        on_device,
        mesh=mesh,
        in_specs=placed,
        out_specs=(
            P(("group", "dp"), None, None),
            P(("group", "dp"), None, None),
            P("group", None, "dp"),
            P("group", None, "dp"),
            P("group", None, "dp"),
            P("group", "dp"),
            P("group", "dp"),
            P("group", "dp"),
        ),
        check_vma=False,
    )
```

```python
import jax
import jax.numpy as jnp
from jax import lax
from jax.experimental import pallas as pl
from jax.experimental.pallas import tpu as pltpu
from jax.sharding import PartitionSpec as P

HEADS = 6
FF = 1536
LAYERS = 2
NEWTON_STEPS = 5
STEP = 10
MATS = 8
VROWS = 24


norm_eps = 1e-06
ortho_eps = 1e-07
coef_a = 3.4445
coef_b = -4.775
coef_c = 2.0315
momentum_keep = 0.95
muon_rate = 0.25
muon_decay = 0.01
muon_shape = 0.5
adam_rate = 0.4
first_keep = 0.9
second_keep = 0.999
adam_eps = 1e-08
half_root = 0.7071067811865476
density = 0.3989422804014327


def normalize(values):
    center = values - jnp.mean(values, -1, keepdims=True)
    inv_std = lax.rsqrt(jnp.mean(center * center, -1, keepdims=True) + norm_eps)
    return (center * inv_std, inv_std)


def norm_back(upstream, normed, inv_std, gain):
    scaled = upstream * gain
    return inv_std * (
        scaled
        - jnp.mean(scaled, -1, keepdims=True)
        - normed * jnp.mean(scaled * normed, -1, keepdims=True)
    )


def gelu_slope(values):
    return (
        0.5 * (1.0 + lax.erf(values * half_root))
        + values * jnp.exp(-0.5 * values * values) * density
    )


def row_contract(left_op, right_op):
    return lax.dot_general(
        left_op, right_op, (((0,), (0,)), ((), ())), preferred_element_type=jnp.float32
    )


def col_contract(left_op, right_op):
    return lax.dot_general(
        left_op, right_op, (((1,), (1,)), ((), ())), preferred_element_type=jnp.float32
    )


BLK = 96
WIDE = 384
VPAD = 32
RINGX = 4
RINGZ = 4
STEPS = [(flip, hops) for flip in range(2) for hops in range(RINGZ)]


def half(part):
    return part.astype(jnp.bfloat16)


def full(part):
    return part.astype(jnp.float32)


def near(part, change):
    return lax.ppermute(part, "dp", [(at, change(at)) for at in range(16)])


def other_core(part):
    return near(part, lambda at: at ^ 1)


def other_row(part):
    return near(part, lambda at: at ^ 2)


def along_x(part, hops):
    return near(part, lambda at: (at + 4 * hops) % 16)


def along_group(part, flip, hops):
    pairs = [(at, (at ^ (4 * flip)) // 4 * 4 + (at + hops) % RINGZ) for at in range(8)]
    return lax.ppermute(part, "group", pairs)


def my_place():
    spot = lax.axis_index("dp")
    return spot >> 2, (spot >> 1) & 1, spot & 1


def my_group():
    group = lax.axis_index("group")
    return group >> 2, group & 3


def rows_at(start, count=BLK):
    return pl.ds(pl.multiple_of(start, 32), count)


def small_call(kernel, outs, ins, slot_first=False, scratch=(), name=None, vmem=32):
    specs = [pl.BlockSpec(memory_space=pltpu.VMEM)] * len(ins)
    if slot_first:
        specs[0] = pl.BlockSpec(memory_space=pltpu.SMEM)
    return pl.pallas_call(
        kernel,
        out_shape=[jax.ShapeDtypeStruct((rows, WIDE), kind) for rows, kind in outs],
        in_specs=specs,
        out_specs=[pl.BlockSpec(memory_space=pltpu.VMEM)] * len(outs),
        scratch_shapes=list(scratch),
        compiler_params=pltpu.CompilerParams(vmem_limit_bytes=vmem << 20),
        name=name,
    )(*ins)


def choose_kernel(slot_ref, *refs):
    pairs, (first_ref, third_ref), hold = refs[:4], refs[4:6], refs[6]
    flip, z = my_group()
    spread = None
    for turn, hops in STEPS:
        base = turn * (BLK + VPAD)
        hold[turn * RINGZ + hops] = pairs[hops][base : base + BLK]
        piece = full(pairs[hops][base + BLK : base + BLK + VPAD])
        spread = piece if spread is None else spread + piece

    def matrix(mat_index):
        slot = slot_ref[mat_index]
        return hold[((slot >> 2) ^ flip) * RINGZ + ((slot - z) & 3)]

    first_ref[4 * BLK :] = half(spread)
    for member in range(4):
        first_ref[member * BLK : (member + 1) * BLK] = matrix(member)
        third_ref[member * BLK : (member + 1) * BLK] = matrix(4 + member)


def merge_first_kernel(*refs):
    parts, head_ref, hidden_ref, hold = refs[:4], refs[4], refs[5], refs[6]
    merge_heads(parts, head_ref, hold)
    merge_hidden(parts, hidden_ref, 0)
    total = full(parts[0][4 * BLK :])
    for at in range(1, 4):
        total = total + full(parts[at][4 * BLK :])
    head_ref[4 * BLK :] = half(total)


def merge_third_kernel(*refs):
    parts, out_ref, hold = refs[:4], refs[4], refs[5]
    merge_heads(parts, out_ref, hold)
    merge_hidden(parts, out_ref, 4 * BLK)


def merge_heads(parts, out_ref, hold):
    x, _, _ = my_place()
    for at in range(4):
        hold[at] = parts[at][: 2 * BLK]
    for at in range(3):
        out_ref[at * BLK : (at + 1) * BLK] = hold[(at - x) & 3, :BLK]
    out_ref[3 * BLK : 4 * BLK] = hold[(0 - x) & 3, BLK:]


def merge_hidden(parts, out_ref, put):
    for member in (2, 3):
        for part in parts:
            out_ref[put : put + BLK] = part[member * BLK : (member + 1) * BLK]
            put += BLK


def final_kernel(heads, hidden, spread, *refs):
    parts, outs = refs[:4], list(refs[4:])
    _, row, core = my_place()
    base = 0
    if heads:
        qkv_ref, out_ref = outs[:2]
        outs = outs[2:]
        for at_part, part in enumerate(parts):
            piece = (row ^ (at_part & 1)) * 2 * BLK + (core ^ (at_part >> 1)) * BLK
            for at in range(3):
                qkv_ref[rows_at(at * WIDE + piece)] = part[at * BLK : (at + 1) * BLK]
            out_ref[rows_at(piece)] = part[3 * BLK : 4 * BLK]
        base = 4 * BLK
    if hidden:
        for member in range(2):
            for at_part, part in enumerate(parts):
                start = base + member * WIDE
                outs[member][at_part * WIDE : (at_part + 1) * WIDE] = part[start : start + WIDE]
        base += 2 * WIDE
        outs = outs[2:]
    if spread:
        total = full(parts[0][base:])
        for part in parts[1:]:
            total = total + full(part[base:])
        outs[0][...] = total


def from_x(part):
    return [part] + [along_x(part, -hops) for hops in (1, 2, 3)]


HOLD_HEADS = pltpu.VMEM((4, 2 * BLK, WIDE), jnp.bfloat16)


def all_four(own):
    beside = other_row(own)
    return [own, beside, other_core(own), other_core(beside)]


def whole(parts, heads, hidden, spread, name):
    outs = []
    if heads:
        outs += [(3 * WIDE, jnp.bfloat16), (WIDE, jnp.bfloat16)]
    if hidden:
        outs += [(FF, jnp.bfloat16)] * 2
    if spread:
        outs += [(VPAD, jnp.float32)]
    return small_call(
        lambda *refs: final_kernel(heads, hidden, spread, *refs), outs, parts, name=name + "_whole"
    )


def put_vec(ref, start, value):
    high = half(value)
    ref[start : start + VPAD] = high
    ref[start + VPAD : start + 2 * VPAD] = half(value - full(high))


def get_vec(ref, start):
    return full(ref[start : start + VPAD]) + full(ref[start + VPAD : start + 2 * VPAD])


def split_core_kernel(heads, hidden, spread, *refs):
    refs = list(refs)
    keep_ref, sent_ref = refs[-2:]
    _, _, core = my_place()
    put = 0
    if heads:
        qkv_ref, out_ref = refs[:2]
        refs = refs[2:]
        for row in range(2):
            for at in range(4):
                source = out_ref if at == 3 else qkv_ref
                start = (0 if at == 3 else at * WIDE) + row * 2 * BLK
                keep_ref[put : put + BLK] = source[rows_at(start + core * BLK)]
                sent_ref[put : put + BLK] = source[rows_at(start + (1 - core) * BLK)]
                put += BLK
    if hidden:
        for source in refs[:2]:
            keep_ref[put : put + 2 * WIDE] = source[: 2 * WIDE]
            sent_ref[put : put + 2 * WIDE] = source[2 * WIDE :]
            put += 2 * WIDE
        refs = refs[2:]
    if spread:
        *pieces, vec_ref = refs[:-2]
        vec_ref[VROWS:] = jnp.zeros((VPAD - VROWS, WIDE), jnp.float32)
        for layer_at in range(LAYERS):
            base = layer_at * (VROWS // LAYERS)
            one, two, three = pieces[3 * layer_at : 3 * layer_at + 3]
            vec_ref[base : base + 5] = one[:5]
            vec_ref[base + 5 : base + 8] = two[:3]
            vec_ref[base + 8 : base + 12] = three[...]
        put_vec(sent_ref, put, vec_ref[...])


def split_row_kernel(heads, hidden, spread, *refs):
    had_ref, came_ref = refs[:2]
    keep_ref, sent_ref = refs[2 + spread : 4 + spread]
    _, row, _ = my_place()

    def total(start):
        at = rows_at(start, WIDE)
        return full(had_ref[at]) + full(came_ref[at])

    put, base = 0, 0
    if heads:
        keep_ref[:WIDE] = total(row * WIDE)
        sent_ref[:WIDE] = half(total((1 - row) * WIDE))
        put, base = WIDE, 2 * WIDE
    if hidden:
        for _ in range(2):
            keep_ref[put : put + WIDE] = total(base)
            sent_ref[put : put + WIDE] = half(total(base + WIDE))
            put, base = put + WIDE, base + 2 * WIDE
    if spread:
        value = refs[2][...] + get_vec(came_ref, base)
        refs[-1][...] = value
        put_vec(sent_ref, put, value)


def split_x_kernel(heads, hidden, spread, *refs):
    had_ref, came_ref = refs[:2]
    keep_ref, *sent_refs = refs[2 + spread : 6 + spread]
    hold = refs[-1]
    x, _, _ = my_place()
    count = had_ref.shape[0]
    hold[...] = had_ref[...] + full(came_ref[:count])
    for hops, target in enumerate([keep_ref] + sent_refs):
        kind = target.dtype
        put, base = 0, 0
        if heads:
            at = (x + hops) & 3
            piece = hold[rows_at(at * BLK)]
            target[:BLK] = jnp.where(at == 3, 0.0, piece).astype(kind)
            target[BLK : 2 * BLK] = hold[3 * BLK : 4 * BLK].astype(kind)
            put, base = 2 * BLK, WIDE
        if hidden:
            for _ in range(2):
                start = base + hops * BLK
                target[put : put + BLK] = hold[start : start + BLK].astype(kind)
                put, base = put + BLK, base + WIDE
        if spread and hops:
            value = refs[2][...] + get_vec(came_ref, base)
            refs[-2][...] = value
            put_vec(target, put, value)


def sum_x_kernel(heads, keep_ref, *refs):
    parts, out_ref = refs[:3], refs[3]
    x, _, _ = my_place()
    total = keep_ref[...]
    for part in parts:
        total = total + full(part[...])
    out_ref[...] = total
    if heads:
        out_ref[BLK : 2 * BLK] = jnp.where(x == 0, total[BLK : 2 * BLK], 0.0)


def scatter_core(grads, heads, hidden, spread, name):
    rows = 8 * BLK * heads + 16 * BLK * hidden
    return small_call(
        lambda *refs: split_core_kernel(heads, hidden, spread, *refs),
        [(VPAD, jnp.float32)] * spread
        + [(rows, jnp.bfloat16), (rows + 2 * VPAD * spread, jnp.bfloat16)],
        grads,
        name=name + "_split_core",
    )


def scatter_row(keep, came, heads, hidden, spread, name, vec_sum=None):
    rows = 4 * BLK * heads + 8 * BLK * hidden
    return small_call(
        lambda *refs: split_row_kernel(heads, hidden, spread, *refs),
        [(rows, jnp.float32), (rows + 2 * VPAD * spread, jnp.bfloat16)]
        + [(VPAD, jnp.float32)] * spread,
        [keep, came] + [vec_sum] * spread,
        name=name + "_split_row",
    )


def scatter_x(keep, came, heads, hidden, spread, name, vec_sum=None):
    rows = 2 * BLK * heads + 2 * BLK * hidden
    return small_call(
        lambda *refs: split_x_kernel(heads, hidden, spread, *refs),
        [(rows, jnp.float32)]
        + [(rows + 2 * VPAD * spread, jnp.bfloat16)] * 3
        + [(VPAD, jnp.float32)] * spread,
        [keep, came] + [vec_sum] * spread,
        scratch=[pltpu.VMEM(keep.shape, jnp.float32)],
        name=name + "_split_x",
    )


def spread_x(sent):
    return [along_x(part, hops + 1) for hops, part in enumerate(sent)]


def split_group_kernel(slot_ref, *refs):
    second_ref, third_ref, keep_ref, *parts = refs[:6]
    vec_ref, own_ref = refs[6], refs[7]
    sent_refs, vec_out, hold = refs[8:15], refs[15], refs[16]
    flip, z = my_group()
    x, _, _ = my_place()
    total = keep_ref[...]
    value = vec_ref[...]
    for part in parts:
        total = total + full(part[: 2 * BLK])
        value = value + get_vec(part, 2 * BLK)
    vec_out[...] = value
    hold[0] = total[:BLK]
    hold[1] = jnp.where(x == 0, total[BLK:], 0.0)
    for member in range(2):
        hold[2 + member] = second_ref[member * BLK : (member + 1) * BLK]
    for member in range(4):
        hold[4 + member] = third_ref[member * BLK : (member + 1) * BLK]
    for at, (turn, hops) in enumerate(STEPS):
        slot = (flip ^ turn) * RINGZ + ((z + hops) & 3)
        mat_index = jnp.int32(0)
        for member in range(1, MATS):
            mat_index = jnp.where(slot_ref[member] == slot, member, mat_index)
        if at == 0:
            own_ref[...] = hold[mat_index]
        else:
            sent_refs[at - 1][:BLK] = half(hold[mat_index])
            put_vec(sent_refs[at - 1], BLK, value)


def renew_kernel(own_ref, *refs):
    parts, (vec_ref, moment_ref) = refs[:7], refs[7:9]
    grad_ref, new_ref, low_ref, vec_out = refs[9:]
    total, value = own_ref[...], vec_ref[...]
    for part in parts:
        total = total + full(part[:BLK])
        value = value + get_vec(part, BLK)
    grad_ref[...] = total
    vec_out[...] = value
    renewed = momentum_keep * moment_ref[...] + total
    new_ref[...] = renewed
    low_ref[...] = half(renewed)


def parts_of(value):
    high = half(value)
    return high, half(value - full(high))


def as_left(value):
    high, low = parts_of(value)
    return jnp.concatenate([high, high, low], 1)


def as_right(value):
    high, low = parts_of(value)
    return jnp.concatenate([high, low, high], 0)


def product(left, right):
    return jnp.dot(left, right, preferred_element_type=jnp.float32)


def newton_kernel(slot_ref, *refs):
    parts, own_ref, weight_ref, out_ref = refs[:4], refs[4], refs[5], refs[6]
    size = WIDE
    gram = None
    for part in parts:
        piece = row_contract(part[...], part[...])
        gram = piece if gram is None else gram + piece
    diagonal = lax.broadcasted_iota(jnp.int32, (size, size), 0) == lax.broadcasted_iota(
        jnp.int32, (size, size), 1
    )
    trace = jnp.sum(jnp.where(diagonal, gram, 0.0), keepdims=True)
    inverse = 1.0 / (jnp.sqrt(trace) + ortho_eps)
    gram = gram * inverse * inverse
    total = None
    for iteration in range(NEWTON_STEPS):
        squared = product(as_left(gram), as_right(gram))
        step = jnp.where(diagonal, coef_a, 0.0) + coef_b * gram + coef_c * squared
        left = as_left(step)
        if iteration == 0:
            total = step
            gram = product(left, as_right(product(left, as_right(gram))))
        elif iteration < NEWTON_STEPS - 1:
            both = product(left, as_right(jnp.concatenate([gram, total], 1)))
            total = both[:, size:]
            gram = product(left, as_right(both[:, :size]))
        else:
            total = product(left, as_right(total))
    high, low = parts_of(total * inverse)
    own = own_ref[...]
    ortho = product(own, high) + product(own, low)
    group = lax.axis_index("group")
    widths = [3 * WIDE, WIDE, FF, FF] * LAYERS
    scale = jnp.float32(0.0)
    for member in range(MATS):
        rate = muon_rate * muon_shape * widths[member] ** 0.5
        scale = jnp.where(slot_ref[member] == group, jnp.float32(rate), scale)
    out_ref[...] = weight_ref[...] * (1.0 - muon_rate * muon_decay) - scale * ortho


def turned(part):
    return half(full(part).T)


def column(index):
    return pl.ds(pl.multiple_of(index * 128, 128), 128)


def row_of(vec_ref, layer_at, index):
    at = layer_at * (VROWS // LAYERS) + index
    return vec_ref[at : at + 1]


def attend_kernel(layer_at, in_ref, qkv_w, out_w, vec_ref, mid_ref, qkv_ref, attn_ref, prob_ref):
    at = pl.program_id(0)

    @pl.when(at == 0)
    def _():
        normed, _ = normalize(in_ref[...])
        normed_low = half(normed * row_of(vec_ref, layer_at, 0) + row_of(vec_ref, layer_at, 1))
        for third in range(3):
            rows = slice(third * WIDE, (third + 1) * WIDE)
            value = col_contract(normed_low, qkv_w[rows])
            if third != 1:
                value = value + row_of(vec_ref, layer_at, 2 if third == 0 else 3)
            qkv_ref[:, rows] = half(value)

    queries = qkv_ref[:, column(at)] * jnp.bfloat16(0.125)
    keys, values = qkv_ref[:, column(3 + at)], qkv_ref[:, column(6 + at)]
    lane = lax.broadcasted_iota(jnp.int32, keys.shape, 1)
    values_t = turned(values)
    sums = []
    for head in range(2):
        mine = half(jnp.where((lane >> 6) == head, 1.0, 0.0))
        scores = col_contract(keys * mine, queries)
        exponent = jnp.exp(scores - jnp.max(scores, 0, keepdims=True))
        probs = half(exponent * (1.0 / jnp.sum(exponent, 0, keepdims=True)))
        prob_ref[head] = probs
        sums.append(product(values_t, probs))
    row = lax.broadcasted_iota(jnp.int32, sums[0].shape, 0)
    attn_ref[:, column(at)] = half(jnp.where(row < 64, sums[0], sums[1]).T)

    @pl.when(at == HEADS // 2 - 1)
    def _():
        mid_ref[...] = in_ref[...] + (
            col_contract(attn_ref[...], out_w[...]) + row_of(vec_ref, layer_at, 4)
        )


def attend_back_kernel(layer_at, up_ref, in_ref, qkv_ref, attn_ref, prob_ref, qkv_w, out_w, vec_ref, grad_ref, gqkv_ref, gout_ref, sum_ref, upstream_ref, back_ref):
    at = pl.program_id(0)

    @pl.when(at == 0)
    def _():
        out_low = half(up_ref[...])
        gout_ref[...] = half(row_contract(out_low, attn_ref[...]))
        upstream_ref[...] = half(product(out_low, out_w[...]))
        sum_ref[4:5] = jnp.sum(full(out_low), 0, keepdims=True)

    queries, keys, values = (qkv_ref[:, column(3 * third + at)] for third in range(3))
    upstream = upstream_ref[:, column(at)]
    lane = lax.broadcasted_iota(jnp.int32, keys.shape, 1)
    keys_t = turned(keys)
    got = []
    for head in range(2):
        mine = half(jnp.where((lane >> 6) == head, 1.0, 0.0))
        probs_low = prob_ref[head]
        probs = full(probs_low)
        prob_grad = col_contract(values * mine, upstream)
        inner = jnp.sum(prob_grad * probs, 0, keepdims=True)
        score_low = half(probs * (prob_grad - inner))
        got.append(
            (product(keys_t, score_low), product(score_low, queries), product(probs_low, upstream))
        )
    row = lax.broadcasted_iota(jnp.int32, got[0][0].shape, 0)
    back_ref[:, column(at)] = half(jnp.where(row < 64, got[0][0], got[1][0]).T * 0.125)
    back_ref[:, column(3 + at)] = half(jnp.where(lane < 64, got[0][1], got[1][1]) * 0.125)
    back_ref[:, column(6 + at)] = half(jnp.where(lane < 64, got[0][2], got[1][2]))

    @pl.when(at == HEADS // 2 - 1)
    def _():
        normed, inv_std = normalize(in_ref[...])
        gain = row_of(vec_ref, layer_at, 0)
        normed_low = half(normed * gain + row_of(vec_ref, layer_at, 1))
        back_normed = jnp.zeros(normed.shape, jnp.float32)
        for third in range(3):
            rows = slice(third * WIDE, (third + 1) * WIDE)
            piece = back_ref[:, rows]
            gqkv_ref[rows] = half(row_contract(piece, normed_low))
            back_normed = back_normed + product(piece, qkv_w[rows])
            if third != 1:
                put = 2 if third == 0 else 3
                sum_ref[put : put + 1] = jnp.sum(full(piece), 0, keepdims=True)
        sum_ref[0:1] = jnp.sum(back_normed * normed, 0, keepdims=True)
        sum_ref[1:2] = jnp.sum(back_normed, 0, keepdims=True)
        grad_ref[...] = up_ref[...] + norm_back(back_normed, normed, inv_std, gain)


def hidden_kernel(layer_at, mid_ref, up_w, down_w, vec_ref, bias_ref, out_ref, act_ref, slope_ref):
    normed, _ = normalize(mid_ref[...])
    hidden_low = half(normed * row_of(vec_ref, layer_at, 5) + row_of(vec_ref, layer_at, 6))
    total = mid_ref[...] + row_of(vec_ref, layer_at, 7)
    for chunk in range(4):
        rows = slice(chunk * WIDE, (chunk + 1) * WIDE)
        hidden = col_contract(hidden_low, up_w[rows]) + bias_ref[chunk : chunk + 1]
        share = 0.5 * (1.0 + lax.erf(hidden * half_root))
        active_low = half(hidden * share)
        act_ref[:, rows] = active_low
        slope_ref[:, rows] = share + hidden * jnp.exp(-0.5 * hidden * hidden) * density
        total = total + product(active_low, down_w[rows])
    out_ref[...] = total


def hidden_back_kernel(layer_at, up_ref, mid_ref, act_ref, slope_ref, up_w, down_w, vec_ref, grad_ref, gup_ref, gdown_ref, sum_ref, bias_ref):
    down_low = half(up_ref[...])
    normed, inv_std = normalize(mid_ref[...])
    gain = row_of(vec_ref, layer_at, 5)
    hidden_low = half(normed * gain + row_of(vec_ref, layer_at, 6))
    back_hidden = jnp.zeros(normed.shape, jnp.float32)
    for chunk in range(4):
        rows = slice(chunk * WIDE, (chunk + 1) * WIDE)
        up_low = half(col_contract(down_low, down_w[rows]) * slope_ref[:, rows])
        gdown_ref[rows] = half(row_contract(act_ref[:, rows], down_low))
        gup_ref[rows] = half(row_contract(up_low, hidden_low))
        bias_ref[chunk : chunk + 1] = jnp.sum(full(up_low), 0, keepdims=True)
        back_hidden = back_hidden + product(up_low, up_w[rows])
    sum_ref[0:1] = jnp.sum(back_hidden * normed, 0, keepdims=True)
    sum_ref[1:2] = jnp.sum(back_hidden, 0, keepdims=True)
    sum_ref[2:3] = jnp.sum(full(down_low), 0, keepdims=True)
    grad_ref[...] = up_ref[...] + norm_back(back_hidden, normed, inv_std, gain)


def layer_call(kernel, layer_at, ins, outs, steps=1, prob_in=None, prob_out=None, scratch=(), name=None):
    def spec(shape, in_steps):
        if in_steps:
            return pl.BlockSpec((2, *shape[1:]), lambda at: (at, 0, 0))
        return pl.BlockSpec(shape, lambda at: (0, 0))

    def body(*refs):
        kernel(layer_at, *refs)

    return pl.pallas_call(
        body,
        grid=(steps,),
        out_shape=[jax.ShapeDtypeStruct(shape, kind) for shape, kind in outs],
        in_specs=[spec(part.shape, at == prob_in) for at, part in enumerate(ins)],
        out_specs=[spec(shape, at == prob_out) for at, (shape, _) in enumerate(outs)],
        scratch_shapes=list(scratch),
        compiler_params=pltpu.CompilerParams(vmem_limit_bytes=44 << 20),
        cost_estimate=pl.CostEstimate(flops=1 << 20, bytes_accessed=1 << 16, transcendentals=0),
        name=name,
    )(*ins)


def attention_forward(layer_at, inputs, w_qkv, w_out, vec_full):
    length = inputs.shape[0]
    return layer_call(
        attend_kernel,
        layer_at,
        [inputs, w_qkv, w_out, vec_full],
        [
            (inputs.shape, jnp.float32),
            ((length, 3 * WIDE), jnp.bfloat16),
            (inputs.shape, jnp.bfloat16),
            ((HEADS, length, length), jnp.bfloat16),
        ],
        steps=HEADS // 2,
        prob_out=3,
        name="attend",
    )


def attention_backward(layer_at, upstream, inputs, stored, w_qkv, w_out, vec_full):
    qkv_low, attn_low, probs = stored
    return layer_call(
        attend_back_kernel,
        layer_at,
        [upstream, inputs, qkv_low, attn_low, probs, w_qkv, w_out, vec_full],
        [
            (inputs.shape, jnp.float32),
            (w_qkv.shape, jnp.bfloat16),
            (w_out.shape, jnp.bfloat16),
            ((8, WIDE), jnp.float32),
        ],
        steps=HEADS // 2,
        prob_in=4,
        scratch=[
            pltpu.VMEM(attn_low.shape, jnp.bfloat16),
            pltpu.VMEM(qkv_low.shape, jnp.bfloat16),
        ],
        name="attend_back",
    )


def hidden_forward(layer_at, middle, w_up, w_down, vec_full, bias_up):
    wide = (middle.shape[0], FF)
    return layer_call(
        hidden_kernel,
        layer_at,
        [middle, w_up, w_down, vec_full, bias_up],
        [(middle.shape, jnp.float32), (wide, jnp.bfloat16), (wide, jnp.float32)],
        name="hidden",
    )


def hidden_backward(layer_at, upstream, middle, stored, w_up, w_down, vec_full):
    return layer_call(
        hidden_back_kernel,
        layer_at,
        [upstream, middle, *stored, w_up, w_down, vec_full],
        [
            (middle.shape, jnp.float32),
            (w_up.shape, jnp.bfloat16),
            (w_up.shape, jnp.bfloat16),
            ((8, WIDE), jnp.float32),
            ((4, WIDE), jnp.float32),
        ],
        name="hidden_back",
    )


def turn(parts, count):
    turned_parts = [jnp.roll(parts, -by, 0) for by in range(RINGX)]
    low = jnp.where((count & 1) == 0, turned_parts[0], turned_parts[1])
    high = jnp.where((count & 1) == 0, turned_parts[2], turned_parts[3])
    return jnp.where((count & 2) == 0, low, high)


def swap(parts, flag, axis):
    return jnp.where(flag == 0, parts, jnp.flip(parts, axis))


def to_own_order(row, place):
    cube = row.reshape(RINGX, 2, 2, BLK)
    cube = turn(swap(swap(cube, place[2], 2), place[1], 1), place[0])
    return cube.transpose(2, 1, 0, 3).reshape(4, WIDE)


def from_own_order(row, place):
    cube = row.reshape(2, 2, RINGX, BLK).transpose(2, 1, 0, 3)
    cube = swap(swap(turn(cube, (4 - place[0]) & 3), place[2], 2), place[1], 1)
    return cube.reshape(4, WIDE)


def on_device(tokens, cotangent, live, slot_of, weights, momentum, vec, vec_first, vec_second):
    place = my_place()
    group_at = lax.axis_index("group")
    data_at = lax.axis_index("dp")
    vec_here, vec_cols = vec.shape
    per_layer = VROWS // LAYERS
    tie = lax.optimization_barrier
    spread = lax.dynamic_update_slice(
        jnp.zeros((VPAD, WIDE), jnp.bfloat16),
        half(vec),
        (group_at * vec_here, data_at * vec_cols),
    )
    own_block = jnp.concatenate([half(weights[0].T), spread], 0)
    pair = jnp.concatenate([own_block, along_group(own_block, 1, 0)], 0)
    slots = [pair] + [along_group(pair, 0, -hops) for hops in (1, 2, 3)]
    first, third = small_call(
        choose_kernel,
        [(4 * BLK + VPAD, jnp.bfloat16), (4 * BLK, jnp.bfloat16)],
        [slot_of] + slots,
        slot_first=True,
        scratch=[pltpu.VMEM((MATS, BLK, WIDE), jnp.bfloat16)],
        name="choose",
    )
    first_x, second_x = small_call(
        merge_first_kernel,
        [(4 * BLK + VPAD, jnp.bfloat16), (8 * BLK, jnp.bfloat16)],
        from_x(first),
        scratch=[HOLD_HEADS],
        name="first_merge_x",
    )
    second_x, third, first_x = tie((second_x, third, first_x))
    first_parts = all_four(first_x)
    beside_second, core_second = other_row(second_x), other_core(second_x)
    third_parts = from_x(third)
    w_qkv0, w_out0, vec_full = whole(first_parts, True, False, True, "first")
    third_parts, w_qkv0 = tie((third_parts, w_qkv0))
    (third_x,) = small_call(
        merge_third_kernel,
        [(12 * BLK, jnp.bfloat16)],
        third_parts,
        scratch=[HOLD_HEADS],
        name="third_merge_x",
    )
    third_x, w_qkv0 = tie((third_x, w_qkv0))
    beside = other_row(third_x)
    core_third = other_core(third_x)
    bias0 = to_own_order(vec_full[8:12].reshape(-1), place)
    bias1 = to_own_order(vec_full[20:24].reshape(-1), place)

    inputs0 = tokens[0]
    middle0, *attn0 = attention_forward(0, inputs0, w_qkv0, w_out0, vec_full)
    beside_second, middle0 = tie((beside_second, middle0))
    second_parts = [second_x, beside_second, core_second, other_core(beside_second)]
    w_up0, w_down0 = whole(second_parts, False, True, False, "second")
    inputs1, *mlp0 = hidden_forward(0, middle0, w_up0, w_down0, vec_full, bias0)
    beside, inputs1 = tie((beside, inputs1))
    third_parts = [third_x, beside, core_third, other_core(beside)]
    w_qkv1, w_out1, w_up1, w_down1 = whole(third_parts, True, True, False, "third")
    middle1, *attn1 = attention_forward(1, inputs1, w_qkv1, w_out1, vec_full)
    stream, *mlp1 = hidden_forward(1, middle1, w_up1, w_down1, vec_full, bias1)

    upstream = cotangent[0] * full(live)[0]
    mid_grad, grad_up, grad_down, sums_two1, sums_up1 = hidden_backward(
        1, upstream, middle1, mlp1, w_up1, w_down1, vec_full
    )
    upstream, grad_qkv, grad_out, sums_one1 = attention_backward(
        1, mid_grad, inputs1, attn1, w_qkv1, w_out1, vec_full
    )
    keep, sent = scatter_core([grad_qkv, grad_out, grad_up, grad_down], True, True, False, "third")
    upstream, sent = tie((upstream, sent))
    came = other_core(sent)
    mid_grad, grad_up, grad_down, sums_two0, sums_up0 = hidden_backward(
        0, upstream, middle0, mlp0, w_up0, w_down0, vec_full
    )
    keep_f, sent_f = scatter_core([grad_up, grad_down], False, True, False, "second")
    mid_grad, sent_f, came = tie((mid_grad, sent_f, came))
    came_f = other_core(sent_f)
    keep, sent = scatter_row(keep, came, True, True, False, "third")
    mid_grad, sent = tie((mid_grad, sent))
    came = other_row(sent)
    token_grad, grad_qkv, grad_out, sums_one0 = attention_backward(
        0, mid_grad, inputs0, attn0, w_qkv0, w_out0, vec_full
    )
    grad_qkv, came_f = tie((grad_qkv, came_f))
    keep_f, sent_f = scatter_row(keep_f, came_f, False, True, False, "second")
    grad_qkv, sent_f, came = tie((grad_qkv, sent_f, came))
    came_f = other_row(sent_f)
    bias_sum0, bias_sum1 = (from_own_order(part, place) for part in (sums_up0, sums_up1))
    vec_sum, keep_h, sent_h = scatter_core(
        [grad_qkv, grad_out, sums_one0, sums_two0, bias_sum0, sums_one1, sums_two1, bias_sum1],
        True,
        False,
        True,
        "first",
    )
    came_h = other_core(sent_h)
    came_h, came = tie((came_h, came))
    keep, *sent_x = scatter_x(keep, came, True, True, False, "third")
    came_x = spread_x(sent_x)
    came_f, came_x = tie((came_f, came_x))
    keep_h, sent_h, vec_sum = scatter_row(keep_h, came_h, True, False, True, "first", vec_sum)
    came_h = other_row(sent_h)
    keep_f, *sent_f = scatter_x(keep_f, came_f, False, True, False, "second")
    (third_sum,) = small_call(
        lambda *refs: sum_x_kernel(True, *refs),
        [(4 * BLK, jnp.float32)],
        [keep] + came_x,
        name="third_sum_x",
    )
    came_f = spread_x(sent_f)
    (second_sum,) = small_call(
        lambda *refs: sum_x_kernel(False, *refs),
        [(2 * BLK, jnp.float32)],
        [keep_f] + came_f,
        name="second_sum_x",
    )
    keep_h, *sent_h, vec_sum = scatter_x(keep_h, came_h, True, False, True, "first", vec_sum)
    came_h = spread_x(sent_h)
    own, *sent_g, vec_sum = small_call(
        split_group_kernel,
        [(BLK, jnp.float32)]
        + [(BLK + 2 * VPAD, jnp.bfloat16)] * 7
        + [(VPAD, jnp.float32)],
        [slot_of, second_sum, third_sum, keep_h] + came_h + [vec_sum],
        slot_first=True,
        scratch=[pltpu.VMEM((MATS, BLK, WIDE), jnp.float32)],
        name="split_group",
    )
    came_g = [along_group(part, flip, hops) for part, (flip, hops) in zip(sent_g, STEPS[1:])]
    grad_rows, moment_rows, moment_low, vec_sum = small_call(
        renew_kernel,
        [(BLK, jnp.float32), (BLK, jnp.float32), (BLK, jnp.bfloat16), (VPAD, jnp.float32)],
        [own] + came_g + [vec_sum, momentum[0].T],
        name="renew",
    )
    ring = jnp.concatenate([moment_low] + [along_x(moment_low, -hops) for hops in (1, 2, 3)], 0)
    beside = other_row(ring)
    (weight_rows,) = small_call(
        newton_kernel,
        [(BLK, jnp.float32)],
        [slot_of, ring, beside, other_core(ring), other_core(beside), moment_low, weights[0].T],
        slot_first=True,
        name="newton",
    )
    shard_vec = lax.dynamic_slice(
        vec_sum, (group_at * vec_here, data_at * vec_cols), (vec_here, vec_cols)
    )
    first_new = first_keep * vec_first + (1.0 - first_keep) * shard_vec
    second_new = second_keep * vec_second + (1.0 - second_keep) * shard_vec * shard_vec
    vec_new = vec - adam_rate * (
        first_new
        / (1.0 - first_keep**STEP)
        / (jnp.sqrt(second_new / (1.0 - second_keep**STEP)) + adam_eps)
    )
    return (
        stream[None],
        token_grad[None],
        grad_rows.T[None],
        moment_rows.T[None],
        weight_rows.T[None],
        first_new,
        second_new,
        vec_new,
    )


def solution(mesh):
    placed = (
        P(("group", "dp"), None, None),
        P(("group", "dp"), None, None),
        P(("group", "dp")),
        P(),
        P("group", None, "dp"),
        P("group", None, "dp"),
        P("group", "dp"),
        P("group", "dp"),
        P("group", "dp"),
    )
    return jax.shard_map(
        on_device,
        mesh=mesh,
        in_specs=placed,
        out_specs=(
            P(("group", "dp"), None, None),
            P(("group", "dp"), None, None),
            P("group", None, "dp"),
            P("group", None, "dp"),
            P("group", None, "dp"),
            P("group", "dp"),
            P("group", "dp"),
            P("group", "dp"),
        ),
        check_vma=False,
    )
```

```python
import jax
import jax.numpy as jnp
from jax import lax
from jax.experimental import pallas as pl
from jax.experimental.pallas import tpu as pltpu
from jax.sharding import PartitionSpec as P

HEADS = 6
FF = 1536
LAYERS = 2
NEWTON_STEPS = 5
STEP = 10
MATS = 8
VROWS = 24


norm_eps = 1e-06
ortho_eps = 1e-07
coef_a = 3.4445
coef_b = -4.775
coef_c = 2.0315
momentum_keep = 0.95
muon_rate = 0.25
muon_decay = 0.01
muon_shape = 0.5
adam_rate = 0.4
first_keep = 0.9
second_keep = 0.999
adam_eps = 1e-08
half_root = 0.7071067811865476
density = 0.3989422804014327


def normalize(values):
    center = values - jnp.mean(values, -1, keepdims=True)
    inv_std = lax.rsqrt(jnp.mean(center * center, -1, keepdims=True) + norm_eps)
    return (center * inv_std, inv_std)


def norm_back(upstream, normed, inv_std, gain):
    scaled = upstream * gain
    return inv_std * (
        scaled
        - jnp.mean(scaled, -1, keepdims=True)
        - normed * jnp.mean(scaled * normed, -1, keepdims=True)
    )


def gelu_slope(values):
    return (
        0.5 * (1.0 + lax.erf(values * half_root))
        + values * jnp.exp(-0.5 * values * values) * density
    )


def row_contract(left_op, right_op):
    return lax.dot_general(
        left_op, right_op, (((0,), (0,)), ((), ())), preferred_element_type=jnp.float32
    )


def col_contract(left_op, right_op):
    return lax.dot_general(
        left_op, right_op, (((1,), (1,)), ((), ())), preferred_element_type=jnp.float32
    )


BLK = 96
WIDE = 384
VPAD = 32
RINGX = 4
RINGZ = 4
STEPS = [(flip, hops) for flip in range(2) for hops in range(RINGZ)]


def half(part):
    return part.astype(jnp.bfloat16)


def full(part):
    return part.astype(jnp.float32)


def near(part, change):
    return lax.ppermute(part, "dp", [(at, change(at)) for at in range(16)])


def other_core(part):
    return near(part, lambda at: at ^ 1)


def other_row(part):
    return near(part, lambda at: at ^ 2)


def along_x(part, hops):
    return near(part, lambda at: (at + 4 * hops) % 16)


def along_group(part, flip, hops):
    pairs = [(at, (at ^ (4 * flip)) // 4 * 4 + (at + hops) % RINGZ) for at in range(8)]
    return lax.ppermute(part, "group", pairs)


def my_place():
    spot = lax.axis_index("dp")
    return spot >> 2, (spot >> 1) & 1, spot & 1


def my_group():
    group = lax.axis_index("group")
    return group >> 2, group & 3


def rows_at(start, count=BLK):
    return pl.ds(pl.multiple_of(start, 32), count)


def small_call(kernel, outs, ins, slot_first=False, scratch=(), name=None, vmem=12):
    specs = [pl.BlockSpec(memory_space=pltpu.VMEM)] * len(ins)
    if slot_first:
        specs[0] = pl.BlockSpec(memory_space=pltpu.SMEM)
    return pl.pallas_call(
        kernel,
        out_shape=[jax.ShapeDtypeStruct((rows, WIDE), kind) for rows, kind in outs],
        in_specs=specs,
        out_specs=[pl.BlockSpec(memory_space=pltpu.VMEM)] * len(outs),
        scratch_shapes=list(scratch),
        compiler_params=pltpu.CompilerParams(vmem_limit_bytes=vmem << 20),
        name=name,
    )(*ins)


def choose_kernel(slot_ref, *refs):
    pairs, (first_ref, third_ref), hold = refs[:4], refs[4:6], refs[6]
    flip, z = my_group()
    spread = None
    for turn, hops in STEPS:
        base = turn * (BLK + VPAD)
        hold[turn * RINGZ + hops] = pairs[hops][base : base + BLK]
        piece = full(pairs[hops][base + BLK : base + BLK + VPAD])
        spread = piece if spread is None else spread + piece

    def matrix(mat_index):
        slot = slot_ref[mat_index]
        return hold[((slot >> 2) ^ flip) * RINGZ + ((slot - z) & 3)]

    first_ref[4 * BLK :] = half(spread)
    for member in range(4):
        first_ref[member * BLK : (member + 1) * BLK] = matrix(member)
        third_ref[member * BLK : (member + 1) * BLK] = matrix(4 + member)


def merge_first_kernel(*refs):
    parts, head_ref, hidden_ref, hold = refs[:4], refs[4], refs[5], refs[6]
    merge_heads(parts, head_ref, hold)
    merge_hidden(parts, hidden_ref, 0)
    total = full(parts[0][4 * BLK :])
    for at in range(1, 4):
        total = total + full(parts[at][4 * BLK :])
    head_ref[4 * BLK :] = half(total)


def merge_third_kernel(*refs):
    parts, out_ref, hold = refs[:4], refs[4], refs[5]
    merge_heads(parts, out_ref, hold)
    merge_hidden(parts, out_ref, 4 * BLK)


def merge_heads(parts, out_ref, hold):
    x, _, _ = my_place()
    for at in range(4):
        hold[at] = parts[at][: 2 * BLK]
    for at in range(3):
        out_ref[at * BLK : (at + 1) * BLK] = hold[(at - x) & 3, :BLK]
    out_ref[3 * BLK : 4 * BLK] = hold[(0 - x) & 3, BLK:]


def merge_hidden(parts, out_ref, put):
    for member in (2, 3):
        for part in parts:
            out_ref[put : put + BLK] = part[member * BLK : (member + 1) * BLK]
            put += BLK


def final_kernel(heads, hidden, spread, *refs):
    parts, outs = refs[:4], list(refs[4:])
    _, row, core = my_place()
    base = 0
    if heads:
        qkv_ref, out_ref = outs[:2]
        outs = outs[2:]
        for at_part, part in enumerate(parts):
            piece = (row ^ (at_part & 1)) * 2 * BLK + (core ^ (at_part >> 1)) * BLK
            for at in range(3):
                qkv_ref[rows_at(at * WIDE + piece)] = part[at * BLK : (at + 1) * BLK]
            out_ref[rows_at(piece)] = part[3 * BLK : 4 * BLK]
        base = 4 * BLK
    if hidden:
        for member in range(2):
            for at_part, part in enumerate(parts):
                start = base + member * WIDE
                outs[member][at_part * WIDE : (at_part + 1) * WIDE] = part[start : start + WIDE]
        base += 2 * WIDE
        outs = outs[2:]
    if spread:
        total = full(parts[0][base:])
        for part in parts[1:]:
            total = total + full(part[base:])
        outs[0][...] = total


def from_x(part):
    return [part] + [along_x(part, -hops) for hops in (1, 2, 3)]


HOLD_HEADS = pltpu.VMEM((4, 2 * BLK, WIDE), jnp.bfloat16)


def all_four(own):
    beside = other_row(own)
    return [own, beside, other_core(own), other_core(beside)]


def whole(parts, heads, hidden, spread, name):
    outs = []
    if heads:
        outs += [(3 * WIDE, jnp.bfloat16), (WIDE, jnp.bfloat16)]
    if hidden:
        outs += [(FF, jnp.bfloat16)] * 2
    if spread:
        outs += [(VPAD, jnp.float32)]
    return small_call(
        lambda *refs: final_kernel(heads, hidden, spread, *refs), outs, parts, name=name + "_whole"
    )


def put_vec(ref, start, value):
    high = half(value)
    ref[start : start + VPAD] = high
    ref[start + VPAD : start + 2 * VPAD] = half(value - full(high))


def get_vec(ref, start):
    return full(ref[start : start + VPAD]) + full(ref[start + VPAD : start + 2 * VPAD])


def split_core_kernel(heads, hidden, spread, *refs):
    refs = list(refs)
    keep_ref, sent_ref = refs[-2:]
    _, _, core = my_place()
    put = 0
    if heads:
        qkv_ref, out_ref = refs[:2]
        refs = refs[2:]
        for row in range(2):
            for at in range(4):
                source = out_ref if at == 3 else qkv_ref
                start = (0 if at == 3 else at * WIDE) + row * 2 * BLK
                keep_ref[put : put + BLK] = source[rows_at(start + core * BLK)]
                sent_ref[put : put + BLK] = source[rows_at(start + (1 - core) * BLK)]
                put += BLK
    if hidden:
        for source in refs[:2]:
            keep_ref[put : put + 2 * WIDE] = source[: 2 * WIDE]
            sent_ref[put : put + 2 * WIDE] = source[2 * WIDE :]
            put += 2 * WIDE
        refs = refs[2:]
    if spread:
        *pieces, vec_ref = refs[:-2]
        vec_ref[VROWS:] = jnp.zeros((VPAD - VROWS, WIDE), jnp.float32)
        for layer_at in range(LAYERS):
            base = layer_at * (VROWS // LAYERS)
            one, two, three = pieces[3 * layer_at : 3 * layer_at + 3]
            vec_ref[base : base + 5] = one[:5]
            vec_ref[base + 5 : base + 8] = two[:3]
            vec_ref[base + 8 : base + 12] = three[...]
        put_vec(sent_ref, put, vec_ref[...])


def split_row_kernel(heads, hidden, spread, *refs):
    had_ref, came_ref = refs[:2]
    keep_ref, sent_ref = refs[2 + spread : 4 + spread]
    _, row, _ = my_place()

    def total(start):
        at = rows_at(start, WIDE)
        return full(had_ref[at]) + full(came_ref[at])

    put, base = 0, 0
    if heads:
        keep_ref[:WIDE] = total(row * WIDE)
        sent_ref[:WIDE] = half(total((1 - row) * WIDE))
        put, base = WIDE, 2 * WIDE
    if hidden:
        for _ in range(2):
            keep_ref[put : put + WIDE] = total(base)
            sent_ref[put : put + WIDE] = half(total(base + WIDE))
            put, base = put + WIDE, base + 2 * WIDE
    if spread:
        value = refs[2][...] + get_vec(came_ref, base)
        refs[-1][...] = value
        put_vec(sent_ref, put, value)


def split_x_kernel(heads, hidden, spread, *refs):
    had_ref, came_ref = refs[:2]
    keep_ref, *sent_refs = refs[2 + spread : 6 + spread]
    hold = refs[-1]
    x, _, _ = my_place()
    count = had_ref.shape[0]
    hold[...] = had_ref[...] + full(came_ref[:count])
    for hops, target in enumerate([keep_ref] + sent_refs):
        kind = target.dtype
        put, base = 0, 0
        if heads:
            at = (x + hops) & 3
            piece = hold[rows_at(at * BLK)]
            target[:BLK] = jnp.where(at == 3, 0.0, piece).astype(kind)
            target[BLK : 2 * BLK] = hold[3 * BLK : 4 * BLK].astype(kind)
            put, base = 2 * BLK, WIDE
        if hidden:
            for _ in range(2):
                start = base + hops * BLK
                target[put : put + BLK] = hold[start : start + BLK].astype(kind)
                put, base = put + BLK, base + WIDE
        if spread and hops:
            value = refs[2][...] + get_vec(came_ref, base)
            refs[-2][...] = value
            put_vec(target, put, value)


def sum_x_kernel(heads, keep_ref, *refs):
    parts, out_ref = refs[:3], refs[3]
    x, _, _ = my_place()
    total = keep_ref[...]
    for part in parts:
        total = total + full(part[...])
    out_ref[...] = total
    if heads:
        out_ref[BLK : 2 * BLK] = jnp.where(x == 0, total[BLK : 2 * BLK], 0.0)


def scatter_core(grads, heads, hidden, spread, name):
    rows = 8 * BLK * heads + 16 * BLK * hidden
    return small_call(
        lambda *refs: split_core_kernel(heads, hidden, spread, *refs),
        [(VPAD, jnp.float32)] * spread
        + [(rows, jnp.bfloat16), (rows + 2 * VPAD * spread, jnp.bfloat16)],
        grads,
        name=name + "_split_core",
    )


def scatter_row(keep, came, heads, hidden, spread, name, vec_sum=None):
    rows = 4 * BLK * heads + 8 * BLK * hidden
    return small_call(
        lambda *refs: split_row_kernel(heads, hidden, spread, *refs),
        [(rows, jnp.float32), (rows + 2 * VPAD * spread, jnp.bfloat16)]
        + [(VPAD, jnp.float32)] * spread,
        [keep, came] + [vec_sum] * spread,
        name=name + "_split_row",
    )


def scatter_x(keep, came, heads, hidden, spread, name, vec_sum=None):
    rows = 2 * BLK * heads + 2 * BLK * hidden
    return small_call(
        lambda *refs: split_x_kernel(heads, hidden, spread, *refs),
        [(rows, jnp.float32)]
        + [(rows + 2 * VPAD * spread, jnp.bfloat16)] * 3
        + [(VPAD, jnp.float32)] * spread,
        [keep, came] + [vec_sum] * spread,
        scratch=[pltpu.VMEM(keep.shape, jnp.float32)],
        name=name + "_split_x",
    )


def spread_x(sent):
    return [along_x(part, hops + 1) for hops, part in enumerate(sent)]


def split_group_kernel(slot_ref, *refs):
    second_ref, third_ref, keep_ref, *parts = refs[:6]
    vec_ref, own_ref = refs[6], refs[7]
    sent_refs, vec_out, hold = refs[8:15], refs[15], refs[16]
    flip, z = my_group()
    x, _, _ = my_place()
    total = keep_ref[...]
    value = vec_ref[...]
    for part in parts:
        total = total + full(part[: 2 * BLK])
        value = value + get_vec(part, 2 * BLK)
    vec_out[...] = value
    hold[0] = total[:BLK]
    hold[1] = jnp.where(x == 0, total[BLK:], 0.0)
    for member in range(2):
        hold[2 + member] = second_ref[member * BLK : (member + 1) * BLK]
    for member in range(4):
        hold[4 + member] = third_ref[member * BLK : (member + 1) * BLK]
    for at, (turn, hops) in enumerate(STEPS):
        slot = (flip ^ turn) * RINGZ + ((z + hops) & 3)
        mat_index = jnp.int32(0)
        for member in range(1, MATS):
            mat_index = jnp.where(slot_ref[member] == slot, member, mat_index)
        if at == 0:
            own_ref[...] = hold[mat_index]
        else:
            sent_refs[at - 1][:BLK] = half(hold[mat_index])
            put_vec(sent_refs[at - 1], BLK, value)


def renew_kernel(own_ref, *refs):
    parts, (vec_ref, moment_ref) = refs[:7], refs[7:9]
    grad_ref, new_ref, low_ref, vec_out = refs[9:]
    total, value = own_ref[...], vec_ref[...]
    for part in parts:
        total = total + full(part[:BLK])
        value = value + get_vec(part, BLK)
    grad_ref[...] = total
    vec_out[...] = value
    renewed = momentum_keep * moment_ref[...] + total
    new_ref[...] = renewed
    low_ref[...] = half(renewed)


def parts_of(value):
    high = half(value)
    return high, half(value - full(high))


def as_left(value):
    high, low = parts_of(value)
    return jnp.concatenate([high, high, low], 1)


def as_right(value):
    high, low = parts_of(value)
    return jnp.concatenate([high, low, high], 0)


def product(left, right):
    return jnp.dot(left, right, preferred_element_type=jnp.float32)


def newton_kernel(slot_ref, *refs):
    parts, own_ref, weight_ref, out_ref = refs[:4], refs[4], refs[5], refs[6]
    size = WIDE
    gram = None
    for part in parts:
        piece = row_contract(part[...], part[...])
        gram = piece if gram is None else gram + piece
    diagonal = lax.broadcasted_iota(jnp.int32, (size, size), 0) == lax.broadcasted_iota(
        jnp.int32, (size, size), 1
    )
    trace = jnp.sum(jnp.where(diagonal, gram, 0.0), keepdims=True)
    inverse = 1.0 / (jnp.sqrt(trace) + ortho_eps)
    gram = gram * inverse * inverse
    total = None
    for iteration in range(NEWTON_STEPS):
        squared = product(as_left(gram), as_right(gram))
        step = jnp.where(diagonal, coef_a, 0.0) + coef_b * gram + coef_c * squared
        left = as_left(step)
        if iteration == 0:
            total = step
            gram = product(left, as_right(product(left, as_right(gram))))
        elif iteration < NEWTON_STEPS - 1:
            both = product(left, as_right(jnp.concatenate([gram, total], 1)))
            total = both[:, size:]
            gram = product(left, as_right(both[:, :size]))
        else:
            total = product(left, as_right(total))
    high, low = parts_of(total * inverse)
    own = own_ref[...]
    ortho = product(own, high) + product(own, low)
    group = lax.axis_index("group")
    widths = [3 * WIDE, WIDE, FF, FF] * LAYERS
    scale = jnp.float32(0.0)
    for member in range(MATS):
        rate = muon_rate * muon_shape * widths[member] ** 0.5
        scale = jnp.where(slot_ref[member] == group, jnp.float32(rate), scale)
    out_ref[...] = weight_ref[...] * (1.0 - muon_rate * muon_decay) - scale * ortho


def turned(part):
    return half(full(part).T)


def column(index):
    return slice(index * 128, (index + 1) * 128)


def row_of(vec_ref, layer_at, index):
    at = layer_at * (VROWS // LAYERS) + index
    return vec_ref[at : at + 1]


def attend_kernel(layer_at, in_ref, qkv_w, out_w, vec_ref, mid_ref, qkv_ref, attn_ref, prob_ref):
    normed, _ = normalize(in_ref[...])
    normed_low = half(normed * row_of(vec_ref, layer_at, 0) + row_of(vec_ref, layer_at, 1))
    for third in range(3):
        rows = slice(third * WIDE, (third + 1) * WIDE)
        value = col_contract(normed_low, qkv_w[rows])
        if third != 1:
            value = value + row_of(vec_ref, layer_at, 2 if third == 0 else 3)
        qkv_ref[:, rows] = half(value)
    for at in range(HEADS // 2):
        attend_pair(at, qkv_ref, attn_ref, prob_ref)
    mid_ref[...] = in_ref[...] + (
        col_contract(attn_ref[...], out_w[...]) + row_of(vec_ref, layer_at, 4)
    )


def attend_pair(at, qkv_ref, attn_ref, prob_ref):
    queries = qkv_ref[:, column(at)] * jnp.bfloat16(0.125)
    keys, values = qkv_ref[:, column(3 + at)], qkv_ref[:, column(6 + at)]
    lane = lax.broadcasted_iota(jnp.int32, keys.shape, 1)
    values_t = turned(values)
    sums = []
    for head in range(2):
        mine = half(jnp.where((lane >> 6) == head, 1.0, 0.0))
        scores = col_contract(keys * mine, queries)
        exponent = jnp.exp(scores - jnp.max(scores, 0, keepdims=True))
        probs = half(exponent * (1.0 / jnp.sum(exponent, 0, keepdims=True)))
        prob_ref[2 * at + head] = probs
        sums.append(product(values_t, probs))
    row = lax.broadcasted_iota(jnp.int32, sums[0].shape, 0)
    attn_ref[:, column(at)] = half(jnp.where(row < 64, sums[0], sums[1]).T)


def attend_back_kernel(layer_at, up_ref, in_ref, qkv_ref, attn_ref, prob_ref, qkv_w, out_w, vec_ref, grad_ref, gqkv_ref, gout_ref, sum_ref, upstream_ref, back_ref):
    out_low = half(up_ref[...])
    gout_ref[...] = half(row_contract(out_low, attn_ref[...]))
    upstream_ref[...] = half(product(out_low, out_w[...]))
    sum_ref[4:5] = jnp.sum(full(out_low), 0, keepdims=True)
    for at in range(HEADS // 2):
        attend_back_pair(at, qkv_ref, upstream_ref, prob_ref, back_ref)
    normed, inv_std = normalize(in_ref[...])
    gain = row_of(vec_ref, layer_at, 0)
    normed_low = half(normed * gain + row_of(vec_ref, layer_at, 1))
    back_normed = jnp.zeros(normed.shape, jnp.float32)
    for third in range(3):
        rows = slice(third * WIDE, (third + 1) * WIDE)
        piece = back_ref[:, rows]
        gqkv_ref[rows] = half(row_contract(piece, normed_low))
        back_normed = back_normed + product(piece, qkv_w[rows])
        if third != 1:
            put = 2 if third == 0 else 3
            sum_ref[put : put + 1] = jnp.sum(full(piece), 0, keepdims=True)
    sum_ref[0:1] = jnp.sum(back_normed * normed, 0, keepdims=True)
    sum_ref[1:2] = jnp.sum(back_normed, 0, keepdims=True)
    grad_ref[...] = up_ref[...] + norm_back(back_normed, normed, inv_std, gain)


def attend_back_pair(at, qkv_ref, upstream_ref, prob_ref, back_ref):
    queries, keys, values = (qkv_ref[:, column(3 * third + at)] for third in range(3))
    upstream = upstream_ref[:, column(at)]
    lane = lax.broadcasted_iota(jnp.int32, keys.shape, 1)
    keys_t = turned(keys)
    got = []
    for head in range(2):
        mine = half(jnp.where((lane >> 6) == head, 1.0, 0.0))
        probs_low = prob_ref[2 * at + head]
        probs = full(probs_low)
        prob_grad = col_contract(values * mine, upstream)
        inner = jnp.sum(prob_grad * probs, 0, keepdims=True)
        score_low = half(probs * (prob_grad - inner))
        got.append(
            (product(keys_t, score_low), product(score_low, queries), product(probs_low, upstream))
        )
    row = lax.broadcasted_iota(jnp.int32, got[0][0].shape, 0)
    back_ref[:, column(at)] = half(jnp.where(row < 64, got[0][0], got[1][0]).T * 0.125)
    back_ref[:, column(3 + at)] = half(jnp.where(lane < 64, got[0][1], got[1][1]) * 0.125)
    back_ref[:, column(6 + at)] = half(jnp.where(lane < 64, got[0][2], got[1][2]))


def hidden_kernel(layer_at, mid_ref, up_w, down_w, vec_ref, bias_ref, out_ref, act_ref, slope_ref):
    normed, _ = normalize(mid_ref[...])
    hidden_low = half(normed * row_of(vec_ref, layer_at, 5) + row_of(vec_ref, layer_at, 6))
    total = mid_ref[...] + row_of(vec_ref, layer_at, 7)
    for chunk in range(4):
        rows = slice(chunk * WIDE, (chunk + 1) * WIDE)
        hidden = col_contract(hidden_low, up_w[rows]) + bias_ref[chunk : chunk + 1]
        share = 0.5 * (1.0 + lax.erf(hidden * half_root))
        active_low = half(hidden * share)
        act_ref[:, rows] = active_low
        slope_ref[:, rows] = share + hidden * jnp.exp(-0.5 * hidden * hidden) * density
        total = total + product(active_low, down_w[rows])
    out_ref[...] = total


def hidden_back_kernel(layer_at, up_ref, mid_ref, act_ref, slope_ref, up_w, down_w, vec_ref, grad_ref, gup_ref, gdown_ref, sum_ref, bias_ref):
    down_low = half(up_ref[...])
    normed, inv_std = normalize(mid_ref[...])
    gain = row_of(vec_ref, layer_at, 5)
    hidden_low = half(normed * gain + row_of(vec_ref, layer_at, 6))
    back_hidden = jnp.zeros(normed.shape, jnp.float32)
    for chunk in range(4):
        rows = slice(chunk * WIDE, (chunk + 1) * WIDE)
        up_low = half(col_contract(down_low, down_w[rows]) * slope_ref[:, rows])
        gdown_ref[rows] = half(row_contract(act_ref[:, rows], down_low))
        gup_ref[rows] = half(row_contract(up_low, hidden_low))
        bias_ref[chunk : chunk + 1] = jnp.sum(full(up_low), 0, keepdims=True)
        back_hidden = back_hidden + product(up_low, up_w[rows])
    sum_ref[0:1] = jnp.sum(back_hidden * normed, 0, keepdims=True)
    sum_ref[1:2] = jnp.sum(back_hidden, 0, keepdims=True)
    sum_ref[2:3] = jnp.sum(full(down_low), 0, keepdims=True)
    grad_ref[...] = up_ref[...] + norm_back(back_hidden, normed, inv_std, gain)


def layer_call(kernel, layer_at, ins, outs, scratch=(), name=None, vmem=24):
    def body(*refs):
        kernel(layer_at, *refs)

    return pl.pallas_call(
        body,
        out_shape=[jax.ShapeDtypeStruct(shape, kind) for shape, kind in outs],
        in_specs=[pl.BlockSpec(memory_space=pltpu.VMEM)] * len(ins),
        out_specs=[pl.BlockSpec(memory_space=pltpu.VMEM)] * len(outs),
        scratch_shapes=list(scratch),
        compiler_params=pltpu.CompilerParams(vmem_limit_bytes=vmem << 20),
        cost_estimate=pl.CostEstimate(flops=1 << 20, bytes_accessed=1 << 16, transcendentals=0),
        name=name,
    )(*ins)


def attention_forward(layer_at, inputs, w_qkv, w_out, vec_full):
    length = inputs.shape[0]
    return layer_call(
        attend_kernel,
        layer_at,
        [inputs, w_qkv, w_out, vec_full],
        [
            (inputs.shape, jnp.float32),
            ((length, 3 * WIDE), jnp.bfloat16),
            (inputs.shape, jnp.bfloat16),
            ((HEADS, length, length), jnp.bfloat16),
        ],
        name="attend",
    )


def attention_backward(layer_at, upstream, inputs, stored, w_qkv, w_out, vec_full):
    qkv_low, attn_low, probs = stored
    return layer_call(
        attend_back_kernel,
        layer_at,
        [upstream, inputs, qkv_low, attn_low, probs, w_qkv, w_out, vec_full],
        [
            (inputs.shape, jnp.float32),
            (w_qkv.shape, jnp.bfloat16),
            (w_out.shape, jnp.bfloat16),
            ((8, WIDE), jnp.float32),
        ],
        scratch=[
            pltpu.VMEM(attn_low.shape, jnp.bfloat16),
            pltpu.VMEM(qkv_low.shape, jnp.bfloat16),
        ],
        name="attend_back",
    )


def hidden_forward(layer_at, middle, w_up, w_down, vec_full, bias_up):
    wide = (middle.shape[0], FF)
    return layer_call(
        hidden_kernel,
        layer_at,
        [middle, w_up, w_down, vec_full, bias_up],
        [(middle.shape, jnp.float32), (wide, jnp.bfloat16), (wide, jnp.float32)],
        name="hidden",
    )


def hidden_backward(layer_at, upstream, middle, stored, w_up, w_down, vec_full):
    return layer_call(
        hidden_back_kernel,
        layer_at,
        [upstream, middle, *stored, w_up, w_down, vec_full],
        [
            (middle.shape, jnp.float32),
            (w_up.shape, jnp.bfloat16),
            (w_up.shape, jnp.bfloat16),
            ((8, WIDE), jnp.float32),
            ((4, WIDE), jnp.float32),
        ],
        name="hidden_back",
    )


def turn(parts, count):
    turned_parts = [jnp.roll(parts, -by, 0) for by in range(RINGX)]
    low = jnp.where((count & 1) == 0, turned_parts[0], turned_parts[1])
    high = jnp.where((count & 1) == 0, turned_parts[2], turned_parts[3])
    return jnp.where((count & 2) == 0, low, high)


def swap(parts, flag, axis):
    return jnp.where(flag == 0, parts, jnp.flip(parts, axis))


def to_own_order(row, place):
    cube = row.reshape(RINGX, 2, 2, BLK)
    cube = turn(swap(swap(cube, place[2], 2), place[1], 1), place[0])
    return cube.transpose(2, 1, 0, 3).reshape(4, WIDE)


def from_own_order(row, place):
    cube = row.reshape(2, 2, RINGX, BLK).transpose(2, 1, 0, 3)
    cube = swap(swap(turn(cube, (4 - place[0]) & 3), place[2], 2), place[1], 1)
    return cube.reshape(4, WIDE)


def on_device(tokens, cotangent, live, slot_of, weights, momentum, vec, vec_first, vec_second):
    place = my_place()
    group_at = lax.axis_index("group")
    data_at = lax.axis_index("dp")
    vec_here, vec_cols = vec.shape
    per_layer = VROWS // LAYERS
    tie = lax.optimization_barrier
    spread = lax.dynamic_update_slice(
        jnp.zeros((VPAD, WIDE), jnp.bfloat16),
        half(vec),
        (group_at * vec_here, data_at * vec_cols),
    )
    own_block = jnp.concatenate([half(weights[0].T), spread], 0)
    pair = jnp.concatenate([own_block, along_group(own_block, 1, 0)], 0)
    slots = [pair] + [along_group(pair, 0, -hops) for hops in (1, 2, 3)]
    first, third = small_call(
        choose_kernel,
        [(4 * BLK + VPAD, jnp.bfloat16), (4 * BLK, jnp.bfloat16)],
        [slot_of] + slots,
        slot_first=True,
        scratch=[pltpu.VMEM((MATS, BLK, WIDE), jnp.bfloat16)],
        name="choose",
    )
    first_x, second_x = small_call(
        merge_first_kernel,
        [(4 * BLK + VPAD, jnp.bfloat16), (8 * BLK, jnp.bfloat16)],
        from_x(first),
        scratch=[HOLD_HEADS],
        name="first_merge_x",
    )
    second_x, third, first_x = tie((second_x, third, first_x))
    first_parts = all_four(first_x)
    beside_second, core_second = other_row(second_x), other_core(second_x)
    third_parts = from_x(third)
    first_parts, third_parts = tie((first_parts, third_parts))
    w_qkv0, w_out0, vec_full = whole(first_parts, True, False, True, "first")
    (third_x,) = small_call(
        merge_third_kernel,
        [(12 * BLK, jnp.bfloat16)],
        third_parts,
        scratch=[HOLD_HEADS],
        name="third_merge_x",
    )
    bias0 = to_own_order(vec_full[8:12].reshape(-1), place)
    bias1 = to_own_order(vec_full[20:24].reshape(-1), place)

    inputs0 = tokens[0]
    middle0, *attn0 = attention_forward(0, inputs0, w_qkv0, w_out0, vec_full)
    third_x, beside_second, middle0 = tie((third_x, beside_second, middle0))
    beside = other_row(third_x)
    core_third = other_core(third_x)
    second_parts = [second_x, beside_second, core_second, other_core(beside_second)]
    w_up0, w_down0 = whole(second_parts, False, True, False, "second")
    inputs1, *mlp0 = hidden_forward(0, middle0, w_up0, w_down0, vec_full, bias0)
    beside, inputs1 = tie((beside, inputs1))
    third_parts = [third_x, beside, core_third, other_core(beside)]
    w_qkv1, w_out1, w_up1, w_down1 = whole(third_parts, True, True, False, "third")
    middle1, *attn1 = attention_forward(1, inputs1, w_qkv1, w_out1, vec_full)
    stream, *mlp1 = hidden_forward(1, middle1, w_up1, w_down1, vec_full, bias1)

    upstream = cotangent[0] * full(live)[0]
    mid_grad, grad_up, grad_down, sums_two1, sums_up1 = hidden_backward(
        1, upstream, middle1, mlp1, w_up1, w_down1, vec_full
    )
    upstream, grad_qkv, grad_out, sums_one1 = attention_backward(
        1, mid_grad, inputs1, attn1, w_qkv1, w_out1, vec_full
    )
    keep, sent = scatter_core([grad_qkv, grad_out, grad_up, grad_down], True, True, False, "third")
    upstream, sent = tie((upstream, sent))
    came = other_core(sent)
    mid_grad, grad_up, grad_down, sums_two0, sums_up0 = hidden_backward(
        0, upstream, middle0, mlp0, w_up0, w_down0, vec_full
    )
    keep_f, sent_f = scatter_core([grad_up, grad_down], False, True, False, "second")
    mid_grad, sent_f, came = tie((mid_grad, sent_f, came))
    came_f = other_core(sent_f)
    keep, sent = scatter_row(keep, came, True, True, False, "third")
    mid_grad, sent = tie((mid_grad, sent))
    came = other_row(sent)
    token_grad, grad_qkv, grad_out, sums_one0 = attention_backward(
        0, mid_grad, inputs0, attn0, w_qkv0, w_out0, vec_full
    )
    grad_qkv, came_f = tie((grad_qkv, came_f))
    keep_f, sent_f = scatter_row(keep_f, came_f, False, True, False, "second")
    grad_qkv, sent_f, came = tie((grad_qkv, sent_f, came))
    came_f = other_row(sent_f)
    bias_sum0, bias_sum1 = (from_own_order(part, place) for part in (sums_up0, sums_up1))
    vec_sum, keep_h, sent_h = scatter_core(
        [grad_qkv, grad_out, sums_one0, sums_two0, bias_sum0, sums_one1, sums_two1, bias_sum1],
        True,
        False,
        True,
        "first",
    )
    came_h = other_core(sent_h)
    came_h, came = tie((came_h, came))
    keep, *sent_x = scatter_x(keep, came, True, True, False, "third")
    came_x = spread_x(sent_x)
    came_f, came_x = tie((came_f, came_x))
    keep_h, sent_h, vec_sum = scatter_row(keep_h, came_h, True, False, True, "first", vec_sum)
    came_h = other_row(sent_h)
    keep_f, *sent_f = scatter_x(keep_f, came_f, False, True, False, "second")
    (third_sum,) = small_call(
        lambda *refs: sum_x_kernel(True, *refs),
        [(4 * BLK, jnp.float32)],
        [keep] + came_x,
        name="third_sum_x",
    )
    came_f = spread_x(sent_f)
    (second_sum,) = small_call(
        lambda *refs: sum_x_kernel(False, *refs),
        [(2 * BLK, jnp.float32)],
        [keep_f] + came_f,
        name="second_sum_x",
    )
    keep_h, *sent_h, vec_sum = scatter_x(keep_h, came_h, True, False, True, "first", vec_sum)
    came_h = spread_x(sent_h)
    own, *sent_g, vec_sum = small_call(
        split_group_kernel,
        [(BLK, jnp.float32)]
        + [(BLK + 2 * VPAD, jnp.bfloat16)] * 7
        + [(VPAD, jnp.float32)],
        [slot_of, second_sum, third_sum, keep_h] + came_h + [vec_sum],
        slot_first=True,
        scratch=[pltpu.VMEM((MATS, BLK, WIDE), jnp.float32)],
        name="split_group",
    )
    came_g = [along_group(part, flip, hops) for part, (flip, hops) in zip(sent_g, STEPS[1:])]
    grad_rows, moment_rows, moment_low, vec_sum = small_call(
        renew_kernel,
        [(BLK, jnp.float32), (BLK, jnp.float32), (BLK, jnp.bfloat16), (VPAD, jnp.float32)],
        [own] + came_g + [vec_sum, momentum[0].T],
        name="renew",
    )
    ring = jnp.concatenate([moment_low] + [along_x(moment_low, -hops) for hops in (1, 2, 3)], 0)
    beside = other_row(ring)
    (weight_rows,) = small_call(
        newton_kernel,
        [(BLK, jnp.float32)],
        [slot_of, ring, beside, other_core(ring), other_core(beside), moment_low, weights[0].T],
        slot_first=True,
        name="newton",
    )
    shard_vec = lax.dynamic_slice(
        vec_sum, (group_at * vec_here, data_at * vec_cols), (vec_here, vec_cols)
    )
    first_new = first_keep * vec_first + (1.0 - first_keep) * shard_vec
    second_new = second_keep * vec_second + (1.0 - second_keep) * shard_vec * shard_vec
    vec_new = vec - adam_rate * (
        first_new
        / (1.0 - first_keep**STEP)
        / (jnp.sqrt(second_new / (1.0 - second_keep**STEP)) + adam_eps)
    )
    return (
        stream[None],
        token_grad[None],
        grad_rows.T[None],
        moment_rows.T[None],
        weight_rows.T[None],
        first_new,
        second_new,
        vec_new,
    )


def solution(mesh):
    placed = (
        P(("group", "dp"), None, None),
        P(("group", "dp"), None, None),
        P(("group", "dp")),
        P(),
        P("group", None, "dp"),
        P("group", None, "dp"),
        P("group", "dp"),
        P("group", "dp"),
        P("group", "dp"),
    )
    return jax.shard_map(
        on_device,
        mesh=mesh,
        in_specs=placed,
        out_specs=(
            P(("group", "dp"), None, None),
            P(("group", "dp"), None, None),
            P("group", None, "dp"),
            P("group", None, "dp"),
            P("group", None, "dp"),
            P("group", "dp"),
            P("group", "dp"),
            P("group", "dp"),
        ),
        check_vma=False,
    )
```

```python
import jax
import jax.numpy as jnp
from jax import lax
from jax.experimental import pallas as pl
from jax.experimental.pallas import tpu as pltpu
from jax.sharding import PartitionSpec as P

HEADS = 6
FF = 1536
LAYERS = 2
NEWTON_STEPS = 5
STEP = 10
MATS = 8
VROWS = 24


norm_eps = 1e-06
ortho_eps = 1e-07
coef_a = 3.4445
coef_b = -4.775
coef_c = 2.0315
momentum_keep = 0.95
muon_rate = 0.25
muon_decay = 0.01
muon_shape = 0.5
adam_rate = 0.4
first_keep = 0.9
second_keep = 0.999
adam_eps = 1e-08
half_root = 0.7071067811865476
density = 0.3989422804014327


def normalize(values):
    center = values - jnp.mean(values, -1, keepdims=True)
    inv_std = lax.rsqrt(jnp.mean(center * center, -1, keepdims=True) + norm_eps)
    return (center * inv_std, inv_std)


def norm_back(upstream, normed, inv_std, gain):
    scaled = upstream * gain
    return inv_std * (
        scaled
        - jnp.mean(scaled, -1, keepdims=True)
        - normed * jnp.mean(scaled * normed, -1, keepdims=True)
    )


def gelu_slope(values):
    return (
        0.5 * (1.0 + lax.erf(values * half_root))
        + values * jnp.exp(-0.5 * values * values) * density
    )


def row_contract(left_op, right_op):
    return lax.dot_general(
        left_op, right_op, (((0,), (0,)), ((), ())), preferred_element_type=jnp.float32
    )


def col_contract(left_op, right_op):
    return lax.dot_general(
        left_op, right_op, (((1,), (1,)), ((), ())), preferred_element_type=jnp.float32
    )


BLK = 96
WIDE = 384
VPAD = 32
RINGX = 4
RINGZ = 4
STEPS = [(flip, hops) for flip in range(2) for hops in range(RINGZ)]


def half(part):
    return part.astype(jnp.bfloat16)


def full(part):
    return part.astype(jnp.float32)


def near(part, change):
    return lax.ppermute(part, "dp", [(at, change(at)) for at in range(16)])


def other_core(part):
    return near(part, lambda at: at ^ 1)


def other_row(part):
    return near(part, lambda at: at ^ 2)


def along_x(part, hops):
    return near(part, lambda at: (at + 4 * hops) % 16)


def along_group(part, flip, hops):
    pairs = [(at, (at ^ (4 * flip)) // 4 * 4 + (at + hops) % RINGZ) for at in range(8)]
    return lax.ppermute(part, "group", pairs)


def my_place():
    spot = lax.axis_index("dp")
    return spot >> 2, (spot >> 1) & 1, spot & 1


def my_group():
    group = lax.axis_index("group")
    return group >> 2, group & 3


def rows_at(start, count=BLK):
    return pl.ds(pl.multiple_of(start, 32), count)


def far_spec():
    return pl.BlockSpec(memory_space=pltpu.HBM)


def small_call(kernel, outs, ins, slot_first=False, scratch=(), name=None, vmem=64):
    lead, count, total = int(slot_first), len(ins) - int(slot_first), len(outs)

    def body(*refs):
        far, near = refs[lead : lead + count + total], refs[lead + count + total :]
        sems, rest = near[count + total], near[count + total + 1 :]
        come = [
            pltpu.make_async_copy(far[at], near[at], sems.at[at]) for at in range(count)
        ]
        for copy in come:
            copy.start()
        for copy in come:
            copy.wait()
        kernel(*refs[:lead], *near[: count + total], *rest)
        leave = [
            pltpu.make_async_copy(near[at], far[at], sems.at[at])
            for at in range(count, count + total)
        ]
        for copy in leave:
            copy.start()
        for copy in leave:
            copy.wait()

    return pl.pallas_call(
        body,
        out_shape=[jax.ShapeDtypeStruct((rows, WIDE), kind) for rows, kind in outs],
        in_specs=[pl.BlockSpec(memory_space=pltpu.SMEM)] * lead + [far_spec()] * count,
        out_specs=[far_spec()] * total,
        scratch_shapes=[pltpu.VMEM(part.shape, part.dtype) for part in ins[lead:]]
        + [pltpu.VMEM((rows, WIDE), kind) for rows, kind in outs]
        + [pltpu.SemaphoreType.DMA((count + total,))]
        + list(scratch),
        compiler_params=pltpu.CompilerParams(vmem_limit_bytes=vmem << 20),
        cost_estimate=pl.CostEstimate(flops=1 << 20, bytes_accessed=1 << 16, transcendentals=0),
        name=name,
    )(*ins)


def choose_kernel(slot_ref, *refs):
    pairs, (first_ref, third_ref), hold = refs[:4], refs[4:6], refs[6]
    flip, z = my_group()
    spread = None
    for turn, hops in STEPS:
        base = turn * (BLK + VPAD)
        hold[turn * RINGZ + hops] = pairs[hops][base : base + BLK]
        piece = full(pairs[hops][base + BLK : base + BLK + VPAD])
        spread = piece if spread is None else spread + piece

    def matrix(mat_index):
        slot = slot_ref[mat_index]
        return hold[((slot >> 2) ^ flip) * RINGZ + ((slot - z) & 3)]

    first_ref[4 * BLK :] = half(spread)
    for member in range(4):
        first_ref[member * BLK : (member + 1) * BLK] = matrix(member)
        third_ref[member * BLK : (member + 1) * BLK] = matrix(4 + member)


def merge_first_kernel(*refs):
    parts, head_ref, hidden_ref, hold = refs[:4], refs[4], refs[5], refs[6]
    merge_heads(parts, head_ref, hold)
    merge_hidden(parts, hidden_ref, 0)
    total = full(parts[0][4 * BLK :])
    for at in range(1, 4):
        total = total + full(parts[at][4 * BLK :])
    head_ref[4 * BLK :] = half(total)


def merge_third_kernel(*refs):
    parts, out_ref, hold = refs[:4], refs[4], refs[5]
    merge_heads(parts, out_ref, hold)
    merge_hidden(parts, out_ref, 4 * BLK)


def merge_heads(parts, out_ref, hold):
    x, _, _ = my_place()
    for at in range(4):
        hold[at] = parts[at][: 2 * BLK]
    for at in range(3):
        out_ref[at * BLK : (at + 1) * BLK] = hold[(at - x) & 3, :BLK]
    out_ref[3 * BLK : 4 * BLK] = hold[(0 - x) & 3, BLK:]


def merge_hidden(parts, out_ref, put):
    for member in (2, 3):
        for part in parts:
            out_ref[put : put + BLK] = part[member * BLK : (member + 1) * BLK]
            put += BLK


def final_kernel(heads, hidden, spread, *refs):
    parts, outs = refs[:4], list(refs[4:])
    _, row, core = my_place()
    base = 0
    if heads:
        qkv_ref, out_ref = outs[:2]
        outs = outs[2:]
        for at_part, part in enumerate(parts):
            piece = (row ^ (at_part & 1)) * 2 * BLK + (core ^ (at_part >> 1)) * BLK
            for at in range(3):
                qkv_ref[rows_at(at * WIDE + piece)] = part[at * BLK : (at + 1) * BLK]
            out_ref[rows_at(piece)] = part[3 * BLK : 4 * BLK]
        base = 4 * BLK
    if hidden:
        for member in range(2):
            for at_part, part in enumerate(parts):
                start = base + member * WIDE
                outs[member][at_part * WIDE : (at_part + 1) * WIDE] = part[start : start + WIDE]
        base += 2 * WIDE
        outs = outs[2:]
    if spread:
        total = full(parts[0][base:])
        for part in parts[1:]:
            total = total + full(part[base:])
        outs[0][...] = total


def from_x(part):
    return [part] + [along_x(part, -hops) for hops in (1, 2, 3)]


HOLD_HEADS = pltpu.VMEM((4, 2 * BLK, WIDE), jnp.bfloat16)


def all_four(own):
    beside = other_row(own)
    return [own, beside, other_core(own), other_core(beside)]


def whole(parts, heads, hidden, spread, name):
    outs = []
    if heads:
        outs += [(3 * WIDE, jnp.bfloat16), (WIDE, jnp.bfloat16)]
    if hidden:
        outs += [(FF, jnp.bfloat16)] * 2
    if spread:
        outs += [(VPAD, jnp.float32)]
    return small_call(
        lambda *refs: final_kernel(heads, hidden, spread, *refs), outs, parts, name=name + "_whole"
    )


def put_vec(ref, start, value):
    high = half(value)
    ref[start : start + VPAD] = high
    ref[start + VPAD : start + 2 * VPAD] = half(value - full(high))


def get_vec(ref, start):
    return full(ref[start : start + VPAD]) + full(ref[start + VPAD : start + 2 * VPAD])


def split_heads(grads, keep_ref, sent_ref):
    _, _, core = my_place()
    put = 0
    for row in range(2):
        for at in range(4):
            start = at * WIDE + row * 2 * BLK
            keep_ref[put : put + BLK] = grads[rows_at(start + core * BLK)]
            sent_ref[put : put + BLK] = grads[rows_at(start + (1 - core) * BLK)]
            put += BLK


def split_row_kernel(heads, spread, *refs):
    had_ref, came_ref = refs[:2]
    keep_ref, sent_ref = refs[2 + spread : 4 + spread]
    _, row, _ = my_place()

    def total(start):
        at = rows_at(start, WIDE)
        return full(had_ref[at]) + full(came_ref[at])

    if heads:
        keep_ref[...] = total(row * WIDE)
        sent_ref[:WIDE] = half(total((1 - row) * WIDE))
    else:
        for member in range(2):
            rows = slice(member * WIDE, (member + 1) * WIDE)
            keep_ref[rows] = total(2 * member * WIDE)
            sent_ref[rows] = half(total((2 * member + 1) * WIDE))
    if spread:
        value = refs[2][...] + get_vec(came_ref, 2 * WIDE)
        refs[-1][...] = value
        put_vec(sent_ref, WIDE, value)


def split_x_kernel(heads, hidden, spread, *refs):
    pairs = 2 * (heads + hidden)
    sources = refs[:pairs]
    keep_ref, *sent_refs = refs[pairs + spread : pairs + spread + 4]
    x, _, _ = my_place()
    put = 0
    if heads:
        hold = refs[-1]
        hold[...] = sources[0][...] + full(sources[1][:WIDE])
        for hops, target in enumerate([keep_ref] + sent_refs):
            kind = target.dtype
            at = (x + hops) & 3
            piece = hold[rows_at(at * BLK)]
            target[:BLK] = jnp.where(at == 3, 0.0, piece).astype(kind)
            target[BLK : 2 * BLK] = hold[3 * BLK : 4 * BLK].astype(kind)
        put = 2 * BLK
    if hidden:
        had_ref, came_ref = sources[-2:]
        for member in range(2):
            for hops, target in enumerate([keep_ref] + sent_refs):
                rows = slice(member * WIDE + hops * BLK, member * WIDE + (hops + 1) * BLK)
                value = had_ref[rows] + full(came_ref[rows])
                target[put : put + BLK] = value.astype(target.dtype)
            put += BLK
    if spread:
        value = refs[pairs][...] + get_vec(sources[1], WIDE)
        refs[-2][...] = value
        for target in sent_refs:
            put_vec(target, put, value)


def sum_x_kernel(heads, keep_ref, *refs):
    parts, out_ref = refs[:3], refs[3]
    x, _, _ = my_place()
    total = keep_ref[...]
    for part in parts:
        total = total + full(part[...])
    out_ref[...] = total
    if heads:
        out_ref[BLK : 2 * BLK] = jnp.where(x == 0, total[BLK : 2 * BLK], 0.0)


def scatter_row(keep, came, heads, spread, name, vec_sum=None):
    rows = 4 * BLK if heads else 8 * BLK
    return small_call(
        lambda *refs: split_row_kernel(heads, spread, *refs),
        [(rows, jnp.float32), (rows + 2 * VPAD * spread, jnp.bfloat16)]
        + [(VPAD, jnp.float32)] * spread,
        [keep, came] + [vec_sum] * spread,
        name=name + "_split_row",
    )


def scatter_x(sources, heads, hidden, spread, name, vec_sum=None):
    rows = 2 * BLK * heads + 2 * BLK * hidden
    return small_call(
        lambda *refs: split_x_kernel(heads, hidden, spread, *refs),
        [(rows, jnp.float32)]
        + [(rows + 2 * VPAD * spread, jnp.bfloat16)] * 3
        + [(VPAD, jnp.float32)] * spread,
        list(sources) + [vec_sum] * spread,
        scratch=[pltpu.VMEM((WIDE, WIDE), jnp.float32)],
        name=name + "_split_x",
    )


def spread_x(sent):
    return [along_x(part, hops + 1) for hops, part in enumerate(sent)]


def split_group_kernel(slot_ref, *refs):
    second_ref, third_ref, keep_ref, *parts = refs[:6]
    vec_ref, own_ref = refs[6], refs[7]
    sent_refs, vec_out, hold = refs[8:15], refs[15], refs[16]
    flip, z = my_group()
    x, _, _ = my_place()
    total = keep_ref[...]
    value = vec_ref[...]
    for part in parts:
        total = total + full(part[: 2 * BLK])
        value = value + get_vec(part, 2 * BLK)
    vec_out[...] = value
    hold[0] = total[:BLK]
    hold[1] = jnp.where(x == 0, total[BLK:], 0.0)
    for member in range(2):
        hold[2 + member] = second_ref[member * BLK : (member + 1) * BLK]
    for member in range(4):
        hold[4 + member] = third_ref[member * BLK : (member + 1) * BLK]
    for at, (turn, hops) in enumerate(STEPS):
        slot = (flip ^ turn) * RINGZ + ((z + hops) & 3)
        mat_index = jnp.int32(0)
        for member in range(1, MATS):
            mat_index = jnp.where(slot_ref[member] == slot, member, mat_index)
        if at == 0:
            own_ref[...] = hold[mat_index]
        else:
            sent_refs[at - 1][:BLK] = half(hold[mat_index])
            put_vec(sent_refs[at - 1], BLK, value)


def renew_kernel(own_ref, *refs):
    parts, (vec_ref, moment_ref) = refs[:7], refs[7:9]
    grad_ref, new_ref, low_ref, vec_out = refs[9:]
    total, value = own_ref[...], vec_ref[...]
    for part in parts:
        total = total + full(part[:BLK])
        value = value + get_vec(part, BLK)
    grad_ref[...] = total
    vec_out[...] = value
    renewed = momentum_keep * moment_ref[...] + total
    new_ref[...] = renewed
    low_ref[...] = half(renewed)


def parts_of(value):
    high = half(value)
    return high, half(value - full(high))


def as_left(value):
    high, low = parts_of(value)
    return jnp.concatenate([high, high, low], 1)


def as_right(value):
    high, low = parts_of(value)
    return jnp.concatenate([high, low, high], 0)


def product(left, right):
    return jnp.dot(left, right, preferred_element_type=jnp.float32)


def newton_kernel(slot_ref, *refs):
    parts, own_ref, weight_ref, out_ref = refs[:4], refs[4], refs[5], refs[6]
    size = WIDE
    gram = None
    for part in parts:
        piece = row_contract(part[...], part[...])
        gram = piece if gram is None else gram + piece
    diagonal = lax.broadcasted_iota(jnp.int32, (size, size), 0) == lax.broadcasted_iota(
        jnp.int32, (size, size), 1
    )
    trace = jnp.sum(jnp.where(diagonal, gram, 0.0), keepdims=True)
    inverse = 1.0 / (jnp.sqrt(trace) + ortho_eps)
    gram = gram * inverse * inverse
    total = None
    for iteration in range(NEWTON_STEPS):
        squared = product(as_left(gram), as_right(gram))
        step = jnp.where(diagonal, coef_a, 0.0) + coef_b * gram + coef_c * squared
        left = as_left(step)
        if iteration == 0:
            total = step
            gram = product(left, as_right(product(left, as_right(gram))))
        elif iteration < NEWTON_STEPS - 1:
            both = product(left, as_right(jnp.concatenate([gram, total], 1)))
            total = both[:, size:]
            gram = product(left, as_right(both[:, :size]))
        else:
            total = product(left, as_right(total))
    high, low = parts_of(total * inverse)
    own = own_ref[...]
    ortho = product(own, high) + product(own, low)
    group = lax.axis_index("group")
    widths = [3 * WIDE, WIDE, FF, FF] * LAYERS
    scale = jnp.float32(0.0)
    for member in range(MATS):
        rate = muon_rate * muon_shape * widths[member] ** 0.5
        scale = jnp.where(slot_ref[member] == group, jnp.float32(rate), scale)
    out_ref[...] = weight_ref[...] * (1.0 - muon_rate * muon_decay) - scale * ortho


def turned(part):
    return half(full(part).T)


def column(index):
    return slice(index * 128, (index + 1) * 128)


def row_of(vec_ref, layer_at, index):
    at = layer_at * (VROWS // LAYERS) + index
    return vec_ref[at : at + 1]


def attend_kernel(layer_at, need, flush, in_ref, qkv_w, out_w, vec_ref, mid_ref, qkv_ref, attn_ref, prob_ref):
    normed, _ = normalize(in_ref[...])
    normed_low = half(normed * row_of(vec_ref, layer_at, 0) + row_of(vec_ref, layer_at, 1))
    for third in range(3):
        rows = slice(third * WIDE, (third + 1) * WIDE)
        value = col_contract(normed_low, qkv_w[rows])
        if third != 1:
            value = value + row_of(vec_ref, layer_at, 2 if third == 0 else 3)
        qkv_ref[:, rows] = half(value)
    flush(1)
    for at in range(HEADS // 2):
        attend_pair(at, qkv_ref, attn_ref, prob_ref)
        flush(3, at)
    flush(2)
    mid_ref[...] = in_ref[...] + (
        col_contract(attn_ref[...], out_w[...]) + row_of(vec_ref, layer_at, 4)
    )


def attend_pair(at, qkv_ref, attn_ref, prob_ref):
    queries = qkv_ref[:, column(at)] * jnp.bfloat16(0.125)
    keys, values = qkv_ref[:, column(3 + at)], qkv_ref[:, column(6 + at)]
    lane = lax.broadcasted_iota(jnp.int32, keys.shape, 1)
    values_t = turned(values)
    sums = []
    for head in range(2):
        mine = half(jnp.where((lane >> 6) == head, 1.0, 0.0))
        scores = col_contract(keys * mine, queries)
        exponent = jnp.exp(scores - jnp.max(scores, 0, keepdims=True))
        probs = half(exponent * (1.0 / jnp.sum(exponent, 0, keepdims=True)))
        prob_ref[2 * at + head] = probs
        sums.append(product(values_t, probs))
    row = lax.broadcasted_iota(jnp.int32, sums[0].shape, 0)
    attn_ref[:, column(at)] = half(jnp.where(row < 64, sums[0], sums[1]).T)


def attend_back_kernel(layer_at, need, flush, up_ref, in_ref, qkv_ref, attn_ref, prob_ref, qkv_w, out_w, vec_ref, *refs):
    spread = len(refs) > 8
    others = refs[:5] if spread else ()
    grad_ref, keep_ref, sent_ref, total_ref, upstream_ref, back_ref, grads_ref, sum_ref = refs[-8:]
    sum_ref[...] = jnp.zeros_like(sum_ref)
    out_low = half(up_ref[...])
    grads_ref[3 * WIDE :] = half(row_contract(out_low, attn_ref[...]))
    upstream_ref[...] = half(product(out_low, out_w[...]))
    sum_ref[4:5] = jnp.sum(full(out_low), 0, keepdims=True)
    for at in range(HEADS // 2):
        need(at)
        attend_back_pair(at, qkv_ref, upstream_ref, prob_ref, back_ref)
    normed, inv_std = normalize(in_ref[...])
    gain = row_of(vec_ref, layer_at, 0)
    normed_low = half(normed * gain + row_of(vec_ref, layer_at, 1))
    back_normed = jnp.zeros(normed.shape, jnp.float32)
    for third in range(3):
        rows = slice(third * WIDE, (third + 1) * WIDE)
        piece = back_ref[:, rows]
        grads_ref[rows] = half(row_contract(piece, normed_low))
        back_normed = back_normed + product(piece, qkv_w[rows])
        if third != 1:
            put = 2 if third == 0 else 3
            sum_ref[put : put + 1] = jnp.sum(full(piece), 0, keepdims=True)
    sum_ref[0:1] = jnp.sum(back_normed * normed, 0, keepdims=True)
    sum_ref[1:2] = jnp.sum(back_normed, 0, keepdims=True)
    grad_ref[...] = up_ref[...] + norm_back(back_normed, normed, inv_std, gain)
    flush(0)
    split_heads(grads_ref, keep_ref, sent_ref)
    if not spread:
        total_ref[...] = sum_ref[...]
        return
    total_ref[VROWS:] = jnp.zeros((VPAD - VROWS, WIDE), jnp.float32)
    pieces = (sum_ref, *others)
    for layer in range(LAYERS):
        base = layer * (VROWS // LAYERS)
        one, two, three = pieces[3 * layer : 3 * layer + 3]
        total_ref[base : base + 5] = one[:5]
        total_ref[base + 5 : base + 8] = two[:3]
        total_ref[base + 8 : base + 12] = three[:4]
    put_vec(sent_ref, 2 * WIDE, total_ref[...])


def attend_back_pair(at, qkv_ref, upstream_ref, prob_ref, back_ref):
    queries, keys, values = (qkv_ref[:, column(3 * third + at)] for third in range(3))
    upstream = upstream_ref[:, column(at)]
    lane = lax.broadcasted_iota(jnp.int32, keys.shape, 1)
    keys_t = turned(keys)
    got = []
    for head in range(2):
        mine = half(jnp.where((lane >> 6) == head, 1.0, 0.0))
        probs_low = prob_ref[2 * at + head]
        probs = full(probs_low)
        prob_grad = col_contract(values * mine, upstream)
        inner = jnp.sum(prob_grad * probs, 0, keepdims=True)
        score_low = half(probs * (prob_grad - inner))
        got.append(
            (product(keys_t, score_low), product(score_low, queries), product(probs_low, upstream))
        )
    row = lax.broadcasted_iota(jnp.int32, got[0][0].shape, 0)
    back_ref[:, column(at)] = half(jnp.where(row < 64, got[0][0], got[1][0]).T * 0.125)
    back_ref[:, column(3 + at)] = half(jnp.where(lane < 64, got[0][1], got[1][1]) * 0.125)
    back_ref[:, column(6 + at)] = half(jnp.where(lane < 64, got[0][2], got[1][2]))


def hidden_kernel(layer_at, need, flush, mid_ref, up_w, down_w, vec_ref, bias_ref, out_ref, act_ref, slope_ref):
    normed, _ = normalize(mid_ref[...])
    hidden_low = half(normed * row_of(vec_ref, layer_at, 5) + row_of(vec_ref, layer_at, 6))
    total = mid_ref[...] + row_of(vec_ref, layer_at, 7)
    for chunk in range(4):
        need(chunk)
        rows = slice(chunk * WIDE, (chunk + 1) * WIDE)
        hidden = col_contract(hidden_low, up_w[rows]) + bias_ref[chunk : chunk + 1]
        share = 0.5 * (1.0 + lax.erf(hidden * half_root))
        active_low = half(hidden * share)
        act_ref[:, rows] = active_low
        slope_ref[:, rows] = share + hidden * jnp.exp(-0.5 * hidden * hidden) * density
        total = total + product(active_low, down_w[rows])
        flush(1, chunk)
        flush(2, chunk)
    out_ref[...] = total


def hidden_back_kernel(layer_at, need, flush, up_ref, mid_ref, act_ref, slope_ref, up_w, down_w, vec_ref, grad_ref, keep_ref, sent_ref, sum_ref, bias_ref):
    down_low = half(up_ref[...])
    normed, inv_std = normalize(mid_ref[...])
    gain = row_of(vec_ref, layer_at, 5)
    hidden_low = half(normed * gain + row_of(vec_ref, layer_at, 6))
    back_hidden = jnp.zeros(normed.shape, jnp.float32)
    sum_ref[...] = jnp.zeros_like(sum_ref)
    bias_ref[...] = jnp.zeros_like(bias_ref)
    for chunk in range(4):
        need(chunk)
        rows = slice(chunk * WIDE, (chunk + 1) * WIDE)
        up_low = half(col_contract(down_low, down_w[rows]) * slope_ref[:, rows])
        target, turn_at = (keep_ref, sent_ref)[chunk // 2], chunk % 2
        for member, value in enumerate(
            (row_contract(up_low, hidden_low), row_contract(act_ref[:, rows], down_low))
        ):
            put = (2 * member + turn_at) * WIDE
            target[put : put + WIDE] = half(value)
            flush(1 + chunk // 2, 2 * member + turn_at)
        bias_ref[chunk : chunk + 1] = jnp.sum(full(up_low), 0, keepdims=True)
        back_hidden = back_hidden + product(up_low, up_w[rows])
    sum_ref[0:1] = jnp.sum(back_hidden * normed, 0, keepdims=True)
    sum_ref[1:2] = jnp.sum(back_hidden, 0, keepdims=True)
    sum_ref[2:3] = jnp.sum(full(down_low), 0, keepdims=True)
    grad_ref[...] = up_ref[...] + norm_back(back_hidden, normed, inv_std, gain)


def cut_piece(ref, how, at):
    if how is None:
        return ref
    dimension, pieces = how
    size = ref.shape[dimension] // pieces
    return ref.at[(slice(None),) * dimension + (pl.ds(at * size, size),)]


def layer_call(kernel, layer_at, ins, outs, in_cut, out_cut, scratch=(), name=None):
    count, total = len(ins), len(outs)
    pieces = max([how[1] for how in in_cut.values()] + [1])
    in_plan = [(at, None, 0) for at in range(count) if at not in in_cut]
    in_plan += [(at, in_cut[at], piece) for piece in range(pieces) for at in sorted(in_cut)]
    out_plan = []
    for at in range(total):
        how = out_cut.get(at)
        out_plan += [(at, how, piece) for piece in range(how[1] if how else 1)]

    def body(*refs):
        far, near = refs[: count + total], refs[count + total : 2 * (count + total)]
        come_sems, leave_sems = refs[2 * (count + total) : 2 * (count + total) + 2]
        rest = refs[2 * (count + total) + 2 :]
        come = [
            pltpu.make_async_copy(
                cut_piece(far[at], how, piece), cut_piece(near[at], how, piece), come_sems.at[index]
            )
            for index, (at, how, piece) in enumerate(in_plan)
        ]
        leave = [
            pltpu.make_async_copy(
                cut_piece(near[count + at], how, piece),
                cut_piece(far[count + at], how, piece),
                leave_sems.at[index],
            )
            for index, (at, how, piece) in enumerate(out_plan)
        ]
        started = []

        def need(wanted):
            for (_, how, piece), copy in zip(in_plan, come):
                if (how is None and wanted is None) or (how is not None and piece == wanted):
                    copy.wait()

        def flush(out_at, wanted=0):
            index = [(at, piece) for at, _, piece in out_plan].index((out_at, wanted))
            leave[index].start()
            started.append(index)

        for copy in come:
            copy.start()
        need(None)
        kernel(layer_at, need, flush, *near, *rest)
        for index, copy in enumerate(leave):
            if index not in started:
                copy.start()
        for copy in leave:
            copy.wait()

    return pl.pallas_call(
        body,
        out_shape=[jax.ShapeDtypeStruct(shape, kind) for shape, kind in outs],
        in_specs=[far_spec()] * count,
        out_specs=[far_spec()] * total,
        scratch_shapes=[pltpu.VMEM(part.shape, part.dtype) for part in ins]
        + [pltpu.VMEM(shape, kind) for shape, kind in outs]
        + [pltpu.SemaphoreType.DMA((len(in_plan),)), pltpu.SemaphoreType.DMA((len(out_plan),))]
        + list(scratch),
        compiler_params=pltpu.CompilerParams(vmem_limit_bytes=64 << 20),
        cost_estimate=pl.CostEstimate(flops=1 << 20, bytes_accessed=1 << 16, transcendentals=0),
        name=name,
    )(*ins)


def attention_forward(layer_at, inputs, w_qkv, w_out, vec_full):
    length = inputs.shape[0]
    return layer_call(
        attend_kernel,
        layer_at,
        [inputs, w_qkv, w_out, vec_full],
        [
            (inputs.shape, jnp.float32),
            ((length, 3 * WIDE), jnp.bfloat16),
            (inputs.shape, jnp.bfloat16),
            ((HEADS, length, length), jnp.bfloat16),
        ],
        {},
        {3: (0, HEADS // 2)},
        name="attend",
    )


def attention_backward(layer_at, upstream, inputs, stored, w_qkv, w_out, vec_full, others=()):
    qkv_low, attn_low, probs = stored
    spread = len(others) > 0
    return layer_call(
        attend_back_kernel,
        layer_at,
        [upstream, inputs, qkv_low, attn_low, probs, w_qkv, w_out, vec_full, *others],
        [
            (inputs.shape, jnp.float32),
            ((2 * WIDE, WIDE), jnp.bfloat16),
            ((2 * WIDE + 2 * VPAD * spread, WIDE), jnp.bfloat16),
            ((VPAD if spread else 8, WIDE), jnp.float32),
        ],
        {4: (0, HEADS // 2)},
        {},
        scratch=[
            pltpu.VMEM(attn_low.shape, jnp.bfloat16),
            pltpu.VMEM(qkv_low.shape, jnp.bfloat16),
            pltpu.VMEM((4 * WIDE, WIDE), jnp.bfloat16),
            pltpu.VMEM((8, WIDE), jnp.float32),
        ],
        name="attend_back",
    )


def hidden_forward(layer_at, middle, w_up, w_down, vec_full, bias_up):
    wide = (middle.shape[0], FF)
    return layer_call(
        hidden_kernel,
        layer_at,
        [middle, w_up, w_down, vec_full, bias_up],
        [(middle.shape, jnp.float32), (wide, jnp.bfloat16), (wide, jnp.float32)],
        {1: (0, 4), 2: (0, 4)},
        {1: (1, 4), 2: (1, 4)},
        name="hidden",
    )


def hidden_backward(layer_at, upstream, middle, stored, w_up, w_down, vec_full):
    return layer_call(
        hidden_back_kernel,
        layer_at,
        [upstream, middle, *stored, w_up, w_down, vec_full],
        [
            (middle.shape, jnp.float32),
            (w_up.shape, jnp.bfloat16),
            (w_up.shape, jnp.bfloat16),
            ((8, WIDE), jnp.float32),
            ((8, WIDE), jnp.float32),
        ],
        {2: (1, 4), 3: (1, 4), 4: (0, 4), 5: (0, 4)},
        {1: (0, 4), 2: (0, 4)},
        name="hidden_back",
    )


def turn(parts, count):
    turned_parts = [jnp.roll(parts, -by, 0) for by in range(RINGX)]
    low = jnp.where((count & 1) == 0, turned_parts[0], turned_parts[1])
    high = jnp.where((count & 1) == 0, turned_parts[2], turned_parts[3])
    return jnp.where((count & 2) == 0, low, high)


def swap(parts, flag, axis):
    return jnp.where(flag == 0, parts, jnp.flip(parts, axis))


def to_own_order(row, place):
    cube = row.reshape(RINGX, 2, 2, BLK)
    cube = turn(swap(swap(cube, place[2], 2), place[1], 1), place[0])
    return jnp.pad(cube.transpose(2, 1, 0, 3).reshape(4, WIDE), ((0, 4), (0, 0)))


def from_own_order(row, place):
    cube = row[:4].reshape(2, 2, RINGX, BLK).transpose(2, 1, 0, 3)
    cube = swap(swap(turn(cube, (4 - place[0]) & 3), place[2], 2), place[1], 1)
    return jnp.pad(cube.reshape(4, WIDE), ((0, 4), (0, 0)))


def on_device(tokens, cotangent, live, slot_of, weights, momentum, vec, vec_first, vec_second):
    place = my_place()
    group_at = lax.axis_index("group")
    data_at = lax.axis_index("dp")
    vec_here, vec_cols = vec.shape
    per_layer = VROWS // LAYERS
    tie = lax.optimization_barrier
    spread = lax.dynamic_update_slice(
        jnp.zeros((VPAD, WIDE), jnp.bfloat16),
        half(vec),
        (group_at * vec_here, data_at * vec_cols),
    )
    own_block = jnp.concatenate([half(weights[0].T), spread], 0)
    pair = jnp.concatenate([own_block, along_group(own_block, 1, 0)], 0)
    slots = [pair] + [along_group(pair, 0, -hops) for hops in (1, 2, 3)]
    first, third = small_call(
        choose_kernel,
        [(4 * BLK + VPAD, jnp.bfloat16), (4 * BLK, jnp.bfloat16)],
        [slot_of] + slots,
        slot_first=True,
        scratch=[pltpu.VMEM((MATS, BLK, WIDE), jnp.bfloat16)],
        name="choose",
    )
    first_x, second_x = small_call(
        merge_first_kernel,
        [(4 * BLK + VPAD, jnp.bfloat16), (8 * BLK, jnp.bfloat16)],
        from_x(first),
        scratch=[HOLD_HEADS],
        name="first_merge_x",
    )
    second_x, third, first_x = tie((second_x, third, first_x))
    beside_first, core_first = other_row(first_x), other_core(first_x)
    beside_second, core_second = other_row(second_x), other_core(second_x)
    third_parts = from_x(third)
    beside_first, third_parts = tie((beside_first, third_parts))
    first_parts = [first_x, beside_first, core_first, other_core(beside_first)]
    w_qkv0, w_out0, vec_full = whole(first_parts, True, False, True, "first")
    (third_x,) = small_call(
        merge_third_kernel,
        [(12 * BLK, jnp.bfloat16)],
        third_parts,
        scratch=[HOLD_HEADS],
        name="third_merge_x",
    )
    bias0 = to_own_order(vec_full[8:12].reshape(-1), place)
    bias1 = to_own_order(vec_full[20:24].reshape(-1), place)

    inputs0 = tokens[0]
    middle0, *attn0 = attention_forward(0, inputs0, w_qkv0, w_out0, vec_full)
    third_x, beside_second, middle0 = tie((third_x, beside_second, middle0))
    beside = other_row(third_x)
    core_third = other_core(third_x)
    second_parts = [second_x, beside_second, core_second, other_core(beside_second)]
    w_up0, w_down0 = whole(second_parts, False, True, False, "second")
    inputs1, *mlp0 = hidden_forward(0, middle0, w_up0, w_down0, vec_full, bias0)
    beside, inputs1 = tie((beside, inputs1))
    third_parts = [third_x, beside, core_third, other_core(beside)]
    w_qkv1, w_out1, w_up1, w_down1 = whole(third_parts, True, True, False, "third")
    middle1, *attn1 = attention_forward(1, inputs1, w_qkv1, w_out1, vec_full)
    stream, *mlp1 = hidden_forward(1, middle1, w_up1, w_down1, vec_full, bias1)

    upstream = cotangent[0] * full(live)[0]
    mid_grad, keep_f1, sent, sums_two1, sums_up1 = hidden_backward(
        1, upstream, middle1, mlp1, w_up1, w_down1, vec_full
    )
    came_f1 = other_core(sent)
    upstream, keep_h1, sent, sums_one1 = attention_backward(
        1, mid_grad, inputs1, attn1, w_qkv1, w_out1, vec_full
    )
    came_h1 = other_core(sent)
    upstream, came_f1 = tie((upstream, came_f1))
    keep_f1, sent = scatter_row(keep_f1, came_f1, False, False, "third")
    upstream, sent = tie((upstream, sent))
    came_f1 = other_row(sent)
    mid_grad, keep_f, sent, sums_two0, sums_up0 = hidden_backward(
        0, upstream, middle0, mlp0, w_up0, w_down0, vec_full
    )
    came_f = other_core(sent)
    mid_grad, came_h1 = tie((mid_grad, came_h1))
    keep_h1, sent = scatter_row(keep_h1, came_h1, True, False, "fourth")
    mid_grad, sent = tie((mid_grad, sent))
    came_h1 = other_row(sent)
    bias_sum0, bias_sum1 = (from_own_order(part, place) for part in (sums_up0, sums_up1))
    token_grad, keep_h, sent_h, vec_sum = attention_backward(
        0,
        mid_grad,
        inputs0,
        attn0,
        w_qkv0,
        w_out0,
        vec_full,
        (sums_two0, bias_sum0, sums_one1, sums_two1, bias_sum1),
    )
    sent_h, came_f = tie((sent_h, came_f))
    keep_f, sent_f = scatter_row(keep_f, came_f, False, False, "second")
    sent_h, sent_f, came_f1, came_h1 = tie((sent_h, sent_f, came_f1, came_h1))
    came_f = other_row(sent_f)
    came_h = other_core(sent_h)
    keep, *sent_x = scatter_x([keep_h1, came_h1, keep_f1, came_f1], True, True, False, "third")
    came_x = spread_x(sent_x)
    came_f, came_x = tie((came_f, came_x))
    keep_h, sent_h, vec_sum = scatter_row(keep_h, came_h, True, True, "first", vec_sum)
    came_h = other_row(sent_h)
    keep_f, *sent_f = scatter_x([keep_f, came_f], False, True, False, "second")
    (third_sum,) = small_call(
        lambda *refs: sum_x_kernel(True, *refs),
        [(4 * BLK, jnp.float32)],
        [keep] + came_x,
        name="third_sum_x",
    )
    came_f = spread_x(sent_f)
    (second_sum,) = small_call(
        lambda *refs: sum_x_kernel(False, *refs),
        [(2 * BLK, jnp.float32)],
        [keep_f] + came_f,
        name="second_sum_x",
    )
    keep_h, *sent_h, vec_sum = scatter_x([keep_h, came_h], True, False, True, "first", vec_sum)
    came_h = spread_x(sent_h)
    own, *sent_g, vec_sum = small_call(
        split_group_kernel,
        [(BLK, jnp.float32)]
        + [(BLK + 2 * VPAD, jnp.bfloat16)] * 7
        + [(VPAD, jnp.float32)],
        [slot_of, second_sum, third_sum, keep_h] + came_h + [vec_sum],
        slot_first=True,
        scratch=[pltpu.VMEM((MATS, BLK, WIDE), jnp.float32)],
        name="split_group",
    )
    came_g = [along_group(part, flip, hops) for part, (flip, hops) in zip(sent_g, STEPS[1:])]
    grad_rows, moment_rows, moment_low, vec_sum = small_call(
        renew_kernel,
        [(BLK, jnp.float32), (BLK, jnp.float32), (BLK, jnp.bfloat16), (VPAD, jnp.float32)],
        [own] + came_g + [vec_sum, momentum[0].T],
        name="renew",
    )
    ring = jnp.concatenate([moment_low] + [along_x(moment_low, -hops) for hops in (1, 2, 3)], 0)
    beside = other_row(ring)
    (weight_rows,) = small_call(
        newton_kernel,
        [(BLK, jnp.float32)],
        [slot_of, ring, beside, other_core(ring), other_core(beside), moment_low, weights[0].T],
        slot_first=True,
        name="newton",
    )
    shard_vec = lax.dynamic_slice(
        vec_sum, (group_at * vec_here, data_at * vec_cols), (vec_here, vec_cols)
    )
    first_new = first_keep * vec_first + (1.0 - first_keep) * shard_vec
    second_new = second_keep * vec_second + (1.0 - second_keep) * shard_vec * shard_vec
    vec_new = vec - adam_rate * (
        first_new
        / (1.0 - first_keep**STEP)
        / (jnp.sqrt(second_new / (1.0 - second_keep**STEP)) + adam_eps)
    )
    return (
        stream[None],
        token_grad[None],
        grad_rows.T[None],
        moment_rows.T[None],
        weight_rows.T[None],
        first_new,
        second_new,
        vec_new,
    )


def solution(mesh):
    placed = (
        P(("group", "dp"), None, None),
        P(("group", "dp"), None, None),
        P(("group", "dp")),
        P(),
        P("group", None, "dp"),
        P("group", None, "dp"),
        P("group", "dp"),
        P("group", "dp"),
        P("group", "dp"),
    )
    return jax.shard_map(
        on_device,
        mesh=mesh,
        in_specs=placed,
        out_specs=(
            P(("group", "dp"), None, None),
            P(("group", "dp"), None, None),
            P("group", None, "dp"),
            P("group", None, "dp"),
            P("group", None, "dp"),
            P("group", "dp"),
            P("group", "dp"),
            P("group", "dp"),
        ),
        check_vma=False,
    )
```

```python
import jax
import jax.numpy as jnp
from jax import lax
from jax.experimental import pallas as pl
from jax.experimental.pallas import tpu as pltpu
from jax.sharding import PartitionSpec as P

HEADS = 6
FF = 1536
LAYERS = 2
NEWTON_STEPS = 5
STEP = 10
MATS = 8
VROWS = 24


norm_eps = 1e-06
ortho_eps = 1e-07
coef_a = 3.4445
coef_b = -4.775
coef_c = 2.0315
momentum_keep = 0.95
muon_rate = 0.25
muon_decay = 0.01
muon_shape = 0.5
adam_rate = 0.4
first_keep = 0.9
second_keep = 0.999
adam_eps = 1e-08
half_root = 0.7071067811865476
density = 0.3989422804014327


def normalize(values):
    center = values - jnp.mean(values, -1, keepdims=True)
    inv_std = lax.rsqrt(jnp.mean(center * center, -1, keepdims=True) + norm_eps)
    return (center * inv_std, inv_std)


def norm_back(upstream, normed, inv_std, gain):
    scaled = upstream * gain
    return inv_std * (
        scaled
        - jnp.mean(scaled, -1, keepdims=True)
        - normed * jnp.mean(scaled * normed, -1, keepdims=True)
    )


def gelu_slope(values):
    return (
        0.5 * (1.0 + lax.erf(values * half_root))
        + values * jnp.exp(-0.5 * values * values) * density
    )


def row_contract(left_op, right_op):
    return lax.dot_general(
        left_op, right_op, (((0,), (0,)), ((), ())), preferred_element_type=jnp.float32
    )


def col_contract(left_op, right_op):
    return lax.dot_general(
        left_op, right_op, (((1,), (1,)), ((), ())), preferred_element_type=jnp.float32
    )


BLK = 96
WIDE = 384
VPAD = 32
RINGX = 4
RINGZ = 4
STEPS = [(flip, hops) for flip in range(2) for hops in range(RINGZ)]


def half(part):
    return part.astype(jnp.bfloat16)


def full(part):
    return part.astype(jnp.float32)


def near(part, change):
    return lax.ppermute(part, "dp", [(at, change(at)) for at in range(16)])


def other_core(part):
    return near(part, lambda at: at ^ 1)


def other_row(part):
    return near(part, lambda at: at ^ 2)


def along_x(part, hops):
    return near(part, lambda at: (at + 4 * hops) % 16)


def along_group(part, flip, hops):
    pairs = [(at, (at ^ (4 * flip)) // 4 * 4 + (at + hops) % RINGZ) for at in range(8)]
    return lax.ppermute(part, "group", pairs)


def my_place():
    spot = lax.axis_index("dp")
    return spot >> 2, (spot >> 1) & 1, spot & 1


def my_group():
    group = lax.axis_index("group")
    return group >> 2, group & 3


def rows_at(start, count=BLK):
    return pl.ds(pl.multiple_of(start, 32), count)


def small_call(kernel, outs, ins, slot_first=False, scratch=(), name=None, vmem=12):
    specs = [pl.BlockSpec(memory_space=pltpu.VMEM)] * len(ins)
    if slot_first:
        specs[0] = pl.BlockSpec(memory_space=pltpu.SMEM)
    return pl.pallas_call(
        kernel,
        out_shape=[jax.ShapeDtypeStruct((rows, WIDE), kind) for rows, kind in outs],
        in_specs=specs,
        out_specs=[pl.BlockSpec(memory_space=pltpu.VMEM)] * len(outs),
        scratch_shapes=list(scratch),
        compiler_params=pltpu.CompilerParams(vmem_limit_bytes=vmem << 20),
        name=name,
    )(*ins)


def choose_kernel(slot_ref, *refs):
    pairs, (first_ref, third_ref), hold = refs[:4], refs[4:6], refs[6]
    flip, z = my_group()
    spread = None
    for turn, hops in STEPS:
        base = turn * (BLK + VPAD)
        hold[turn * RINGZ + hops] = pairs[hops][base : base + BLK]
        piece = full(pairs[hops][base + BLK : base + BLK + VPAD])
        spread = piece if spread is None else spread + piece

    def matrix(mat_index):
        slot = slot_ref[mat_index]
        return hold[((slot >> 2) ^ flip) * RINGZ + ((slot - z) & 3)]

    first_ref[4 * BLK :] = half(spread)
    for member in range(4):
        first_ref[member * BLK : (member + 1) * BLK] = matrix(member)
        third_ref[member * BLK : (member + 1) * BLK] = matrix(4 + member)


def merge_first_kernel(*refs):
    parts, head_ref, hidden_ref, hold = refs[:4], refs[4], refs[5], refs[6]
    merge_heads(parts, head_ref, hold)
    merge_hidden(parts, hidden_ref, 0)
    total = full(parts[0][4 * BLK :])
    for at in range(1, 4):
        total = total + full(parts[at][4 * BLK :])
    head_ref[4 * BLK :] = half(total)


def merge_third_kernel(*refs):
    parts, out_ref, hold = refs[:4], refs[4], refs[5]
    merge_heads(parts, out_ref, hold)
    merge_hidden(parts, out_ref, 4 * BLK)


def merge_heads(parts, out_ref, hold):
    x, _, _ = my_place()
    for at in range(4):
        hold[at] = parts[at][: 2 * BLK]
    for at in range(3):
        out_ref[at * BLK : (at + 1) * BLK] = hold[(at - x) & 3, :BLK]
    out_ref[3 * BLK : 4 * BLK] = hold[(0 - x) & 3, BLK:]


def merge_hidden(parts, out_ref, put):
    for member in (2, 3):
        for part in parts:
            out_ref[put : put + BLK] = part[member * BLK : (member + 1) * BLK]
            put += BLK


def final_kernel(heads, hidden, spread, *refs):
    if spread:
        rows = refs[0].shape[0] // 2
        parts = [ref.at[pl.ds(at * rows, rows)] for ref in refs[:2] for at in range(2)]
        outs = list(refs[2:])
    else:
        parts, outs = refs[:4], list(refs[4:])
    _, row, core = my_place()
    base = 0
    if heads:
        qkv_ref, out_ref = outs[:2]
        outs = outs[2:]
        for at_part, part in enumerate(parts):
            piece = (row ^ (at_part & 1)) * 2 * BLK + (core ^ (at_part >> 1)) * BLK
            for at in range(3):
                qkv_ref[rows_at(at * WIDE + piece)] = part[at * BLK : (at + 1) * BLK]
            out_ref[rows_at(piece)] = part[3 * BLK : 4 * BLK]
        base = 4 * BLK
    if hidden:
        for member in range(2):
            for at_part, part in enumerate(parts):
                start = base + member * WIDE
                outs[member][at_part * WIDE : (at_part + 1) * WIDE] = part[start : start + WIDE]
        base += 2 * WIDE
        outs = outs[2:]
    if spread:
        total = full(parts[0][base : base + VPAD])
        for part in parts[1:]:
            total = total + full(part[base : base + VPAD])
        outs[0][...] = total


def from_x(part):
    return [part] + [along_x(part, -hops) for hops in (1, 2, 3)]


HOLD_HEADS = pltpu.VMEM((4, 2 * BLK, WIDE), jnp.bfloat16)


def all_four(own):
    beside = other_row(own)
    return [own, beside, other_core(own), other_core(beside)]


def whole(parts, heads, hidden, spread, name):
    outs = []
    if heads:
        outs += [(3 * WIDE, jnp.bfloat16), (WIDE, jnp.bfloat16)]
    if hidden:
        outs += [(FF, jnp.bfloat16)] * 2
    if spread:
        outs += [(VPAD, jnp.float32)]
    return small_call(
        lambda *refs: final_kernel(heads, hidden, spread, *refs), outs, parts, name=name + "_whole"
    )


def put_vec(ref, start, value):
    high = half(value)
    ref[start : start + VPAD] = high
    ref[start + VPAD : start + 2 * VPAD] = half(value - full(high))


def get_vec(ref, start):
    return full(ref[start : start + VPAD]) + full(ref[start + VPAD : start + 2 * VPAD])


def split_heads(grads, keep_ref, sent_ref):
    _, _, core = my_place()
    put = 0
    for row in range(2):
        for at in range(4):
            start = at * WIDE + row * 2 * BLK
            keep_ref[put : put + BLK] = grads[rows_at(start + core * BLK)]
            sent_ref[put : put + BLK] = grads[rows_at(start + (1 - core) * BLK)]
            put += BLK


def split_row_kernel(heads, hidden, spread, *refs):
    had_ref, came_ref = refs[:2]
    keep_ref, sent_ref = refs[2 + spread : 4 + spread]
    _, row, _ = my_place()

    def total(start):
        at = rows_at(start, WIDE)
        return full(had_ref[at]) + full(came_ref[at])

    put, base = 0, 0
    if heads:
        keep_ref[:WIDE] = total(row * WIDE)
        sent_ref[:WIDE] = half(total((1 - row) * WIDE))
        put, base = WIDE, 2 * WIDE
    if hidden:
        for _ in range(2):
            keep_ref[put : put + WIDE] = total(base)
            sent_ref[put : put + WIDE] = half(total(base + WIDE))
            put, base = put + WIDE, base + 2 * WIDE
    if spread:
        value = refs[2][...] + get_vec(came_ref, base)
        refs[-1][...] = value
        put_vec(sent_ref, put, value)


def split_x_kernel(heads, hidden, spread, *refs):
    had_ref, came_ref = refs[:2]
    keep_ref, *sent_refs = refs[2 + spread : 6 + spread]
    hold = refs[-1]
    x, _, _ = my_place()
    count = had_ref.shape[0]
    hold[...] = had_ref[...] + full(came_ref[:count])
    for hops, target in enumerate([keep_ref] + sent_refs):
        kind = target.dtype
        put, base = 0, 0
        if heads:
            at = (x + hops) & 3
            piece = hold[rows_at(at * BLK)]
            target[:BLK] = jnp.where(at == 3, 0.0, piece).astype(kind)
            target[BLK : 2 * BLK] = hold[3 * BLK : 4 * BLK].astype(kind)
            put, base = 2 * BLK, WIDE
        if hidden:
            for _ in range(2):
                start = base + hops * BLK
                target[put : put + BLK] = hold[start : start + BLK].astype(kind)
                put, base = put + BLK, base + WIDE
        if spread and hops:
            value = refs[2][...] + get_vec(came_ref, base)
            refs[-2][...] = value
            put_vec(target, put, value)


def sum_x_kernel(heads, keep_ref, *refs):
    parts, out_ref = refs[:3], refs[3]
    x, _, _ = my_place()
    total = keep_ref[...]
    for part in parts:
        total = total + full(part[...])
    out_ref[...] = total
    if heads:
        out_ref[BLK : 2 * BLK] = jnp.where(x == 0, total[BLK : 2 * BLK], 0.0)


def scatter_row(keep, came, heads, hidden, spread, name, vec_sum=None):
    rows = 4 * BLK * heads + 8 * BLK * hidden
    return small_call(
        lambda *refs: split_row_kernel(heads, hidden, spread, *refs),
        [(rows, jnp.float32), (rows + 2 * VPAD * spread, jnp.bfloat16)]
        + [(VPAD, jnp.float32)] * spread,
        [keep, came] + [vec_sum] * spread,
        name=name + "_split_row",
    )


def scatter_x(keep, came, heads, hidden, spread, name, vec_sum=None):
    rows = 2 * BLK * heads + 2 * BLK * hidden
    return small_call(
        lambda *refs: split_x_kernel(heads, hidden, spread, *refs),
        [(rows, jnp.float32)]
        + [(rows + 2 * VPAD * spread, jnp.bfloat16)] * 3
        + [(VPAD, jnp.float32)] * spread,
        [keep, came] + [vec_sum] * spread,
        scratch=[pltpu.VMEM(keep.shape, jnp.float32)],
        name=name + "_split_x",
    )


def spread_x(sent):
    return [along_x(part, hops + 1) for hops, part in enumerate(sent)]


def split_group_kernel(slot_ref, *refs):
    second_ref, third_ref, keep_ref, *parts = refs[:6]
    vec_ref, own_ref = refs[6], refs[7]
    sent_refs, vec_out, hold = refs[8:15], refs[15], refs[16]
    flip, z = my_group()
    x, _, _ = my_place()
    total = keep_ref[...]
    value = vec_ref[...]
    for part in parts:
        total = total + full(part[: 2 * BLK])
        value = value + get_vec(part, 2 * BLK)
    vec_out[...] = value
    hold[0] = total[:BLK]
    hold[1] = jnp.where(x == 0, total[BLK:], 0.0)
    for member in range(2):
        hold[2 + member] = second_ref[member * BLK : (member + 1) * BLK]
    for member in range(4):
        hold[4 + member] = third_ref[member * BLK : (member + 1) * BLK]
    for at, (turn, hops) in enumerate(STEPS):
        slot = (flip ^ turn) * RINGZ + ((z + hops) & 3)
        mat_index = jnp.int32(0)
        for member in range(1, MATS):
            mat_index = jnp.where(slot_ref[member] == slot, member, mat_index)
        if at == 0:
            own_ref[...] = hold[mat_index]
        else:
            sent_refs[at - 1][:BLK] = half(hold[mat_index])
            put_vec(sent_refs[at - 1], BLK, value)


def renew_kernel(own_ref, *refs):
    parts, (vec_ref, moment_ref) = refs[:7], refs[7:9]
    grad_ref, new_ref, low_ref, vec_out = refs[9:]
    total, value = own_ref[...], vec_ref[...]
    for part in parts:
        total = total + full(part[:BLK])
        value = value + get_vec(part, BLK)
    grad_ref[...] = total
    vec_out[...] = value
    renewed = momentum_keep * moment_ref[...] + total
    new_ref[...] = renewed
    low_ref[...] = half(renewed)


def parts_of(value):
    high = half(value)
    return high, half(value - full(high))


def as_left(value):
    high, low = parts_of(value)
    return jnp.concatenate([high, high, low], 1)


def as_right(value):
    high, low = parts_of(value)
    return jnp.concatenate([high, low, high], 0)


def product(left, right):
    return jnp.dot(left, right, preferred_element_type=jnp.float32)


def newton_kernel(slot_ref, *refs):
    parts, own_ref, weight_ref, out_ref = refs[:4], refs[4], refs[5], refs[6]
    size = WIDE
    gram = None
    for part in parts:
        piece = row_contract(part[...], part[...])
        gram = piece if gram is None else gram + piece
    diagonal = lax.broadcasted_iota(jnp.int32, (size, size), 0) == lax.broadcasted_iota(
        jnp.int32, (size, size), 1
    )
    trace = jnp.sum(jnp.where(diagonal, gram, 0.0), keepdims=True)
    inverse = 1.0 / (jnp.sqrt(trace) + ortho_eps)
    gram = gram * inverse * inverse
    total = None
    for iteration in range(NEWTON_STEPS):
        squared = product(as_left(gram), as_right(gram))
        step = jnp.where(diagonal, coef_a, 0.0) + coef_b * gram + coef_c * squared
        left = as_left(step)
        if iteration == 0:
            total = step
            gram = product(left, as_right(product(left, as_right(gram))))
        elif iteration < NEWTON_STEPS - 1:
            both = product(left, as_right(jnp.concatenate([gram, total], 1)))
            total = both[:, size:]
            gram = product(left, as_right(both[:, :size]))
        else:
            total = product(left, as_right(total))
    high, low = parts_of(total * inverse)
    own = own_ref[...]
    ortho = product(own, high) + product(own, low)
    group = lax.axis_index("group")
    widths = [3 * WIDE, WIDE, FF, FF] * LAYERS
    scale = jnp.float32(0.0)
    for member in range(MATS):
        rate = muon_rate * muon_shape * widths[member] ** 0.5
        scale = jnp.where(slot_ref[member] == group, jnp.float32(rate), scale)
    out_ref[...] = weight_ref[...] * (1.0 - muon_rate * muon_decay) - scale * ortho


def turned(part):
    return half(full(part).T)


def column(index):
    return slice(index * 128, (index + 1) * 128)


def row_of(vec_ref, layer_at, index):
    at = layer_at * (VROWS // LAYERS) + index
    return vec_ref[at : at + 1]


def attend_kernel(layer_at, in_ref, qkv_w, out_w, vec_ref, mid_ref, qkv_ref, attn_ref, prob_ref):
    normed, _ = normalize(in_ref[...])
    normed_low = half(normed * row_of(vec_ref, layer_at, 0) + row_of(vec_ref, layer_at, 1))
    for third in range(3):
        rows = slice(third * WIDE, (third + 1) * WIDE)
        value = col_contract(normed_low, qkv_w[rows])
        if third != 1:
            value = value + row_of(vec_ref, layer_at, 2 if third == 0 else 3)
        qkv_ref[:, rows] = half(value)
    for at in range(HEADS // 2):
        attend_pair(at, qkv_ref, attn_ref, prob_ref)
    mid_ref[...] = in_ref[...] + (
        col_contract(attn_ref[...], out_w[...]) + row_of(vec_ref, layer_at, 4)
    )


def attend_pair(at, qkv_ref, attn_ref, prob_ref):
    queries = qkv_ref[:, column(at)] * jnp.bfloat16(0.125)
    keys, values = qkv_ref[:, column(3 + at)], qkv_ref[:, column(6 + at)]
    lane = lax.broadcasted_iota(jnp.int32, keys.shape, 1)
    values_t = turned(values)
    sums = []
    for head in range(2):
        mine = half(jnp.where((lane >> 6) == head, 1.0, 0.0))
        scores = col_contract(keys * mine, queries)
        exponent = jnp.exp(scores - jnp.max(scores, 0, keepdims=True))
        probs = half(exponent * (1.0 / jnp.sum(exponent, 0, keepdims=True)))
        prob_ref[2 * at + head] = probs
        sums.append(product(values_t, probs))
    row = lax.broadcasted_iota(jnp.int32, sums[0].shape, 0)
    attn_ref[:, column(at)] = half(jnp.where(row < 64, sums[0], sums[1]).T)


def attend_back_kernel(layer_at, up_ref, in_ref, qkv_ref, attn_ref, prob_ref, qkv_w, out_w, vec_ref, *refs):
    spread = len(refs) > 8
    others = refs[:5] if spread else ()
    grad_ref, keep_ref, sent_ref, total_ref, upstream_ref, back_ref, grads_ref, sum_ref = refs[-8:]
    sum_ref[...] = jnp.zeros_like(sum_ref)
    out_low = half(up_ref[...])
    grads_ref[3 * WIDE :] = half(row_contract(out_low, attn_ref[...]))
    upstream_ref[...] = half(product(out_low, out_w[...]))
    sum_ref[4:5] = jnp.sum(full(out_low), 0, keepdims=True)
    for at in range(HEADS // 2):
        attend_back_pair(at, qkv_ref, upstream_ref, prob_ref, back_ref)
    normed, inv_std = normalize(in_ref[...])
    gain = row_of(vec_ref, layer_at, 0)
    normed_low = half(normed * gain + row_of(vec_ref, layer_at, 1))
    back_normed = jnp.zeros(normed.shape, jnp.float32)
    for third in range(3):
        rows = slice(third * WIDE, (third + 1) * WIDE)
        piece = back_ref[:, rows]
        grads_ref[rows] = half(row_contract(piece, normed_low))
        back_normed = back_normed + product(piece, qkv_w[rows])
        if third != 1:
            put = 2 if third == 0 else 3
            sum_ref[put : put + 1] = jnp.sum(full(piece), 0, keepdims=True)
    sum_ref[0:1] = jnp.sum(back_normed * normed, 0, keepdims=True)
    sum_ref[1:2] = jnp.sum(back_normed, 0, keepdims=True)
    grad_ref[...] = up_ref[...] + norm_back(back_normed, normed, inv_std, gain)
    split_heads(grads_ref, keep_ref, sent_ref)
    if not spread:
        total_ref[...] = sum_ref[...]
        return
    total_ref[VROWS:] = jnp.zeros((VPAD - VROWS, WIDE), jnp.float32)
    pieces = (sum_ref, *others)
    for layer in range(LAYERS):
        base = layer * (VROWS // LAYERS)
        one, two, three = pieces[3 * layer : 3 * layer + 3]
        total_ref[base : base + 5] = one[:5]
        total_ref[base + 5 : base + 8] = two[:3]
        total_ref[base + 8 : base + 12] = three[...]
    put_vec(sent_ref, 2 * WIDE, total_ref[...])


def attend_back_pair(at, qkv_ref, upstream_ref, prob_ref, back_ref):
    queries, keys, values = (qkv_ref[:, column(3 * third + at)] for third in range(3))
    upstream = upstream_ref[:, column(at)]
    lane = lax.broadcasted_iota(jnp.int32, keys.shape, 1)
    keys_t = turned(keys)
    got = []
    for head in range(2):
        mine = half(jnp.where((lane >> 6) == head, 1.0, 0.0))
        probs_low = prob_ref[2 * at + head]
        probs = full(probs_low)
        prob_grad = col_contract(values * mine, upstream)
        inner = jnp.sum(prob_grad * probs, 0, keepdims=True)
        score_low = half(probs * (prob_grad - inner))
        got.append(
            (product(keys_t, score_low), product(score_low, queries), product(probs_low, upstream))
        )
    row = lax.broadcasted_iota(jnp.int32, got[0][0].shape, 0)
    back_ref[:, column(at)] = half(jnp.where(row < 64, got[0][0], got[1][0]).T * 0.125)
    back_ref[:, column(3 + at)] = half(jnp.where(lane < 64, got[0][1], got[1][1]) * 0.125)
    back_ref[:, column(6 + at)] = half(jnp.where(lane < 64, got[0][2], got[1][2]))


def hidden_kernel(layer_at, mid_ref, up_w, down_w, vec_ref, bias_ref, out_ref, act_ref, slope_ref):
    normed, _ = normalize(mid_ref[...])
    hidden_low = half(normed * row_of(vec_ref, layer_at, 5) + row_of(vec_ref, layer_at, 6))
    total = mid_ref[...] + row_of(vec_ref, layer_at, 7)
    for chunk in range(4):
        rows = slice(chunk * WIDE, (chunk + 1) * WIDE)
        hidden = col_contract(hidden_low, up_w[rows]) + bias_ref[chunk : chunk + 1]
        share = 0.5 * (1.0 + lax.erf(hidden * half_root))
        active_low = half(hidden * share)
        act_ref[:, rows] = active_low
        slope_ref[:, rows] = share + hidden * jnp.exp(-0.5 * hidden * hidden) * density
        total = total + product(active_low, down_w[rows])
    out_ref[...] = total


def hidden_back_kernel(layer_at, up_ref, mid_ref, act_ref, slope_ref, up_w, down_w, vec_ref, grad_ref, keep_ref, sent_ref, sum_ref, bias_ref):
    down_low = half(up_ref[...])
    normed, inv_std = normalize(mid_ref[...])
    gain = row_of(vec_ref, layer_at, 5)
    hidden_low = half(normed * gain + row_of(vec_ref, layer_at, 6))
    back_hidden = jnp.zeros(normed.shape, jnp.float32)
    sum_ref[...] = jnp.zeros_like(sum_ref)
    for chunk in range(4):
        rows = slice(chunk * WIDE, (chunk + 1) * WIDE)
        up_low = half(col_contract(down_low, down_w[rows]) * slope_ref[:, rows])
        target, turn_at = (keep_ref, sent_ref)[chunk // 2], chunk % 2
        for member, value in enumerate(
            (row_contract(up_low, hidden_low), row_contract(act_ref[:, rows], down_low))
        ):
            put = (2 * member + turn_at) * WIDE
            target[put : put + WIDE] = half(value)
        bias_ref[chunk : chunk + 1] = jnp.sum(full(up_low), 0, keepdims=True)
        back_hidden = back_hidden + product(up_low, up_w[rows])
    sum_ref[0:1] = jnp.sum(back_hidden * normed, 0, keepdims=True)
    sum_ref[1:2] = jnp.sum(back_hidden, 0, keepdims=True)
    sum_ref[2:3] = jnp.sum(full(down_low), 0, keepdims=True)
    grad_ref[...] = up_ref[...] + norm_back(back_hidden, normed, inv_std, gain)


def layer_one_kernel(layer_at, in_ref, cot_ref, qkv_w, out_w, up_w, down_w, vec_ref, bias_ref, *refs):
    stream_ref, grad_ref, keep_ref, sent_ref, one_ref, two_ref, bias_sum_ref = refs[:7]
    mid_ref, qkv_ref, attn_ref, prob_ref, act_ref, slope_ref, mid_grad_ref, *rest = refs[7:]
    heads, hidden = pl.ds(0, 2 * WIDE), pl.ds(2 * WIDE, 4 * WIDE)
    attend_kernel(layer_at, in_ref, qkv_w, out_w, vec_ref, mid_ref, qkv_ref, attn_ref, prob_ref)
    hidden_kernel(
        layer_at, mid_ref, up_w, down_w, vec_ref, bias_ref, stream_ref, act_ref, slope_ref
    )
    hidden_back_kernel(
        layer_at,
        cot_ref,
        mid_ref,
        act_ref,
        slope_ref,
        up_w,
        down_w,
        vec_ref,
        mid_grad_ref,
        keep_ref.at[hidden],
        sent_ref.at[hidden],
        two_ref,
        bias_sum_ref,
    )
    attend_back_kernel(
        layer_at,
        mid_grad_ref,
        in_ref,
        qkv_ref,
        attn_ref,
        prob_ref,
        qkv_w,
        out_w,
        vec_ref,
        grad_ref,
        keep_ref.at[heads],
        sent_ref.at[heads],
        one_ref,
        *rest,
    )


def layer_call(kernel, layer_at, ins, outs, scratch=(), name=None, vmem=24):
    def body(*refs):
        kernel(layer_at, *refs)

    return pl.pallas_call(
        body,
        out_shape=[jax.ShapeDtypeStruct(shape, kind) for shape, kind in outs],
        in_specs=[pl.BlockSpec(memory_space=pltpu.VMEM)] * len(ins),
        out_specs=[pl.BlockSpec(memory_space=pltpu.VMEM)] * len(outs),
        scratch_shapes=list(scratch),
        compiler_params=pltpu.CompilerParams(vmem_limit_bytes=vmem << 20),
        cost_estimate=pl.CostEstimate(flops=1 << 20, bytes_accessed=1 << 16, transcendentals=0),
        name=name,
    )(*ins)


def attention_forward(layer_at, inputs, w_qkv, w_out, vec_full):
    length = inputs.shape[0]
    return layer_call(
        attend_kernel,
        layer_at,
        [inputs, w_qkv, w_out, vec_full],
        [
            (inputs.shape, jnp.float32),
            ((length, 3 * WIDE), jnp.bfloat16),
            (inputs.shape, jnp.bfloat16),
            ((HEADS, length, length), jnp.bfloat16),
        ],
        name="attend",
    )


def back_scratch(length):
    return [
        pltpu.VMEM((length, WIDE), jnp.bfloat16),
        pltpu.VMEM((length, 3 * WIDE), jnp.bfloat16),
        pltpu.VMEM((4 * WIDE, WIDE), jnp.bfloat16),
        pltpu.VMEM((8, WIDE), jnp.float32),
    ]


def attention_backward(layer_at, upstream, inputs, stored, w_qkv, w_out, vec_full, others):
    qkv_low, attn_low, probs = stored
    return layer_call(
        attend_back_kernel,
        layer_at,
        [upstream, inputs, qkv_low, attn_low, probs, w_qkv, w_out, vec_full, *others],
        [
            (inputs.shape, jnp.float32),
            ((2 * WIDE, WIDE), jnp.bfloat16),
            ((2 * WIDE + 2 * VPAD, WIDE), jnp.bfloat16),
            ((VPAD, WIDE), jnp.float32),
        ],
        scratch=back_scratch(inputs.shape[0]),
        name="attend_back",
    )


def layer_one(inputs, cotangent, w_qkv, w_out, w_up, w_down, vec_full, bias_up):
    length = inputs.shape[0]
    return layer_call(
        layer_one_kernel,
        1,
        [inputs, cotangent, w_qkv, w_out, w_up, w_down, vec_full, bias_up],
        [
            (inputs.shape, jnp.float32),
            (inputs.shape, jnp.float32),
            ((6 * WIDE, WIDE), jnp.bfloat16),
            ((6 * WIDE, WIDE), jnp.bfloat16),
            ((8, WIDE), jnp.float32),
            ((8, WIDE), jnp.float32),
            ((4, WIDE), jnp.float32),
        ],
        scratch=[
            pltpu.VMEM(inputs.shape, jnp.float32),
            pltpu.VMEM((length, 3 * WIDE), jnp.bfloat16),
            pltpu.VMEM(inputs.shape, jnp.bfloat16),
            pltpu.VMEM((HEADS, length, length), jnp.bfloat16),
            pltpu.VMEM((length, FF), jnp.bfloat16),
            pltpu.VMEM((length, FF), jnp.float32),
            pltpu.VMEM(inputs.shape, jnp.float32),
            *back_scratch(length),
        ],
        name="layer_one",
        vmem=36,
    )


def hidden_forward(layer_at, middle, w_up, w_down, vec_full, bias_up):
    wide = (middle.shape[0], FF)
    return layer_call(
        hidden_kernel,
        layer_at,
        [middle, w_up, w_down, vec_full, bias_up],
        [(middle.shape, jnp.float32), (wide, jnp.bfloat16), (wide, jnp.float32)],
        name="hidden",
    )


def hidden_backward(layer_at, upstream, middle, stored, w_up, w_down, vec_full):
    return layer_call(
        hidden_back_kernel,
        layer_at,
        [upstream, middle, *stored, w_up, w_down, vec_full],
        [
            (middle.shape, jnp.float32),
            (w_up.shape, jnp.bfloat16),
            (w_up.shape, jnp.bfloat16),
            ((8, WIDE), jnp.float32),
            ((4, WIDE), jnp.float32),
        ],
        name="hidden_back",
    )


def turn(parts, count):
    turned_parts = [jnp.roll(parts, -by, 0) for by in range(RINGX)]
    low = jnp.where((count & 1) == 0, turned_parts[0], turned_parts[1])
    high = jnp.where((count & 1) == 0, turned_parts[2], turned_parts[3])
    return jnp.where((count & 2) == 0, low, high)


def swap(parts, flag, axis):
    return jnp.where(flag == 0, parts, jnp.flip(parts, axis))


def to_own_order(row, place):
    cube = row.reshape(RINGX, 2, 2, BLK)
    cube = turn(swap(swap(cube, place[2], 2), place[1], 1), place[0])
    return cube.transpose(2, 1, 0, 3).reshape(4, WIDE)


def from_own_order(row, place):
    cube = row.reshape(2, 2, RINGX, BLK).transpose(2, 1, 0, 3)
    cube = swap(swap(turn(cube, (4 - place[0]) & 3), place[2], 2), place[1], 1)
    return cube.reshape(4, WIDE)


def on_device(tokens, cotangent, live, slot_of, weights, momentum, vec, vec_first, vec_second):
    place = my_place()
    group_at = lax.axis_index("group")
    data_at = lax.axis_index("dp")
    vec_here, vec_cols = vec.shape
    per_layer = VROWS // LAYERS
    tie = lax.optimization_barrier
    spread = lax.dynamic_update_slice(
        jnp.zeros((VPAD, WIDE), jnp.bfloat16),
        half(vec),
        (group_at * vec_here, data_at * vec_cols),
    )
    own_block = jnp.concatenate([half(weights[0].T), spread], 0)
    pair = jnp.concatenate([own_block, along_group(own_block, 1, 0)], 0)
    slots = [pair] + [along_group(pair, 0, -hops) for hops in (1, 2, 3)]
    first, third = small_call(
        choose_kernel,
        [(4 * BLK + VPAD, jnp.bfloat16), (4 * BLK, jnp.bfloat16)],
        [slot_of] + slots,
        slot_first=True,
        scratch=[pltpu.VMEM((MATS, BLK, WIDE), jnp.bfloat16)],
        name="choose",
    )
    first_x, second_x = small_call(
        merge_first_kernel,
        [(4 * BLK + VPAD, jnp.bfloat16), (8 * BLK, jnp.bfloat16)],
        from_x(first),
        scratch=[HOLD_HEADS],
        name="first_merge_x",
    )
    second_x, third, first_x = tie((second_x, third, first_x))
    beside_first = other_row(first_x)
    pair_first = jnp.concatenate([first_x, beside_first], 0)
    first_parts = [pair_first, other_core(pair_first)]
    beside_second, core_second = other_row(second_x), other_core(second_x)
    third_parts = from_x(third)
    w_qkv0, w_out0, vec_full = whole(first_parts, True, False, True, "first")
    bias0 = to_own_order(vec_full[8:12].reshape(-1), place)
    bias1 = to_own_order(vec_full[20:24].reshape(-1), place)

    inputs0 = tokens[0]
    middle0, *attn0 = attention_forward(0, inputs0, w_qkv0, w_out0, vec_full)
    third_parts, beside_second, middle0 = tie((third_parts, beside_second, middle0))
    (third_x,) = small_call(
        merge_third_kernel,
        [(12 * BLK, jnp.bfloat16)],
        third_parts,
        scratch=[HOLD_HEADS],
        name="third_merge_x",
    )
    beside = other_row(third_x)
    core_third = other_core(third_x)
    second_parts = [second_x, beside_second, core_second, other_core(beside_second)]
    w_up0, w_down0 = whole(second_parts, False, True, False, "second")
    inputs1, *mlp0 = hidden_forward(0, middle0, w_up0, w_down0, vec_full, bias0)
    beside, inputs1 = tie((beside, inputs1))
    third_parts = [third_x, beside, core_third, other_core(beside)]
    w_qkv1, w_out1, w_up1, w_down1 = whole(third_parts, True, True, False, "third")
    upstream = cotangent[0] * full(live)[0]
    stream, upstream, keep, sent, sums_one1, sums_two1, sums_up1 = layer_one(
        inputs1, upstream, w_qkv1, w_out1, w_up1, w_down1, vec_full, bias1
    )
    came = other_core(sent)
    mid_grad, keep_f, sent_f, sums_two0, sums_up0 = hidden_backward(
        0, upstream, middle0, mlp0, w_up0, w_down0, vec_full
    )
    came_f = other_core(sent_f)
    vec_full, came = tie((vec_full, came))
    keep, sent = scatter_row(keep, came, True, True, False, "third")
    vec_full, sent = tie((vec_full, sent))
    came = other_row(sent)
    bias_sum0, bias_sum1 = (from_own_order(part, place) for part in (sums_up0, sums_up1))
    token_grad, keep_h, sent_h, vec_sum = attention_backward(
        0,
        mid_grad,
        inputs0,
        attn0,
        w_qkv0,
        w_out0,
        vec_full,
        (sums_two0, bias_sum0, sums_one1, sums_two1, bias_sum1),
    )
    vec_sum, came_f = tie((vec_sum, came_f))
    keep_f, sent_f = scatter_row(keep_f, came_f, False, True, False, "second")
    sent_h, sent_f, came = tie((sent_h, sent_f, came))
    came_f = other_row(sent_f)
    came_h = other_core(sent_h)
    keep, *sent_x = scatter_x(keep, came, True, True, False, "third")
    came_x = spread_x(sent_x)
    came_f, came_x = tie((came_f, came_x))
    keep_h, sent_h, vec_sum = scatter_row(keep_h, came_h, True, False, True, "first", vec_sum)
    came_h = other_row(sent_h)
    keep_f, *sent_f = scatter_x(keep_f, came_f, False, True, False, "second")
    (third_sum,) = small_call(
        lambda *refs: sum_x_kernel(True, *refs),
        [(4 * BLK, jnp.float32)],
        [keep] + came_x,
        name="third_sum_x",
    )
    came_f = spread_x(sent_f)
    (second_sum,) = small_call(
        lambda *refs: sum_x_kernel(False, *refs),
        [(2 * BLK, jnp.float32)],
        [keep_f] + came_f,
        name="second_sum_x",
    )
    keep_h, *sent_h, vec_sum = scatter_x(keep_h, came_h, True, False, True, "first", vec_sum)
    came_h = spread_x(sent_h)
    own, *sent_g, vec_sum = small_call(
        split_group_kernel,
        [(BLK, jnp.float32)]
        + [(BLK + 2 * VPAD, jnp.bfloat16)] * 7
        + [(VPAD, jnp.float32)],
        [slot_of, second_sum, third_sum, keep_h] + came_h + [vec_sum],
        slot_first=True,
        scratch=[pltpu.VMEM((MATS, BLK, WIDE), jnp.float32)],
        name="split_group",
    )
    came_g = [along_group(part, flip, hops) for part, (flip, hops) in zip(sent_g, STEPS[1:])]
    grad_rows, moment_rows, moment_low, vec_sum = small_call(
        renew_kernel,
        [(BLK, jnp.float32), (BLK, jnp.float32), (BLK, jnp.bfloat16), (VPAD, jnp.float32)],
        [own] + came_g + [vec_sum, momentum[0].T],
        name="renew",
    )
    ring = jnp.concatenate([moment_low] + [along_x(moment_low, -hops) for hops in (1, 2, 3)], 0)
    beside = other_row(ring)
    (weight_rows,) = small_call(
        newton_kernel,
        [(BLK, jnp.float32)],
        [slot_of, ring, beside, other_core(ring), other_core(beside), moment_low, weights[0].T],
        slot_first=True,
        name="newton",
    )
    shard_vec = lax.dynamic_slice(
        vec_sum, (group_at * vec_here, data_at * vec_cols), (vec_here, vec_cols)
    )
    first_new = first_keep * vec_first + (1.0 - first_keep) * shard_vec
    second_new = second_keep * vec_second + (1.0 - second_keep) * shard_vec * shard_vec
    vec_new = vec - adam_rate * (
        first_new
        / (1.0 - first_keep**STEP)
        / (jnp.sqrt(second_new / (1.0 - second_keep**STEP)) + adam_eps)
    )
    return (
        stream[None],
        token_grad[None],
        grad_rows.T[None],
        moment_rows.T[None],
        weight_rows.T[None],
        first_new,
        second_new,
        vec_new,
    )


def solution(mesh):
    placed = (
        P(("group", "dp"), None, None),
        P(("group", "dp"), None, None),
        P(("group", "dp")),
        P(),
        P("group", None, "dp"),
        P("group", None, "dp"),
        P("group", "dp"),
        P("group", "dp"),
        P("group", "dp"),
    )
    return jax.shard_map(
        on_device,
        mesh=mesh,
        in_specs=placed,
        out_specs=(
            P(("group", "dp"), None, None),
            P(("group", "dp"), None, None),
            P("group", None, "dp"),
            P("group", None, "dp"),
            P("group", None, "dp"),
            P("group", "dp"),
            P("group", "dp"),
            P("group", "dp"),
        ),
        check_vma=False,
    )
```

```python
import jax
import jax.numpy as jnp
from jax import lax
from jax.experimental import pallas as pl
from jax.experimental.pallas import tpu as pltpu
from jax.sharding import PartitionSpec as P

HEADS = 6
FF = 1536
LAYERS = 2
NEWTON_STEPS = 5
STEP = 10
MATS = 8
VROWS = 24


norm_eps = 1e-06
ortho_eps = 1e-07
coef_a = 3.4445
coef_b = -4.775
coef_c = 2.0315
momentum_keep = 0.95
muon_rate = 0.25
muon_decay = 0.01
muon_shape = 0.5
adam_rate = 0.4
first_keep = 0.9
second_keep = 0.999
adam_eps = 1e-08
half_root = 0.7071067811865476
density = 0.3989422804014327


def normalize(values):
    center = values - jnp.mean(values, -1, keepdims=True)
    inv_std = lax.rsqrt(jnp.mean(center * center, -1, keepdims=True) + norm_eps)
    return (center * inv_std, inv_std)


def norm_back(upstream, normed, inv_std, gain):
    scaled = upstream * gain
    return inv_std * (
        scaled
        - jnp.mean(scaled, -1, keepdims=True)
        - normed * jnp.mean(scaled * normed, -1, keepdims=True)
    )


def gelu_slope(values):
    return (
        0.5 * (1.0 + lax.erf(values * half_root))
        + values * jnp.exp(-0.5 * values * values) * density
    )


def row_contract(left_op, right_op):
    return lax.dot_general(
        left_op, right_op, (((0,), (0,)), ((), ())), preferred_element_type=jnp.float32
    )


def col_contract(left_op, right_op):
    return lax.dot_general(
        left_op, right_op, (((1,), (1,)), ((), ())), preferred_element_type=jnp.float32
    )


BLK = 96
WIDE = 384
VPAD = 32
RINGX = 4
RINGZ = 4
STEPS = [(flip, hops) for flip in range(2) for hops in range(RINGZ)]


def half(part):
    return part.astype(jnp.bfloat16)


def full(part):
    return part.astype(jnp.float32)


def near(part, change):
    return lax.ppermute(part, "dp", [(at, change(at)) for at in range(16)])


def other_core(part):
    return near(part, lambda at: at ^ 1)


def other_row(part):
    return near(part, lambda at: at ^ 2)


def along_x(part, hops):
    return near(part, lambda at: (at + 4 * hops) % 16)


def along_group(part, flip, hops):
    pairs = [(at, (at ^ (4 * flip)) // 4 * 4 + (at + hops) % RINGZ) for at in range(8)]
    return lax.ppermute(part, "group", pairs)


def my_place():
    spot = lax.axis_index("dp")
    return spot >> 2, (spot >> 1) & 1, spot & 1


def my_group():
    group = lax.axis_index("group")
    return group >> 2, group & 3


def rows_at(start, count=BLK):
    return pl.ds(pl.multiple_of(start, 32), count)


def small_call(kernel, outs, ins, slot_first=False, scratch=(), name=None, vmem=12):
    specs = [pl.BlockSpec(memory_space=pltpu.VMEM)] * len(ins)
    if slot_first:
        specs[0] = pl.BlockSpec(memory_space=pltpu.SMEM)
    return pl.pallas_call(
        kernel,
        out_shape=[jax.ShapeDtypeStruct((rows, WIDE), kind) for rows, kind in outs],
        in_specs=specs,
        out_specs=[pl.BlockSpec(memory_space=pltpu.VMEM)] * len(outs),
        scratch_shapes=list(scratch),
        compiler_params=pltpu.CompilerParams(vmem_limit_bytes=vmem << 20),
        name=name,
    )(*ins)


def choose_kernel(slot_ref, *refs):
    pairs, (first_ref, third_ref), hold = refs[:4], refs[4:6], refs[6]
    flip, z = my_group()
    spread = None
    for turn, hops in STEPS:
        base = turn * (BLK + VPAD)
        hold[turn * RINGZ + hops] = pairs[hops][base : base + BLK]
        piece = full(pairs[hops][base + BLK : base + BLK + VPAD])
        spread = piece if spread is None else spread + piece

    def matrix(mat_index):
        slot = slot_ref[mat_index]
        return hold[((slot >> 2) ^ flip) * RINGZ + ((slot - z) & 3)]

    first_ref[4 * BLK :] = half(spread)
    for member in range(4):
        first_ref[member * BLK : (member + 1) * BLK] = matrix(member)
        third_ref[member * BLK : (member + 1) * BLK] = matrix(4 + member)


def merge_first_kernel(*refs):
    parts, head_ref, hidden_ref, hold = refs[:4], refs[4], refs[5], refs[6]
    merge_heads(parts, head_ref, hold)
    merge_hidden(parts, hidden_ref, 0)
    total = full(parts[0][4 * BLK :])
    for at in range(1, 4):
        total = total + full(parts[at][4 * BLK :])
    head_ref[4 * BLK :] = half(total)


def merge_third_kernel(*refs):
    parts, out_ref, hold = refs[:4], refs[4], refs[5]
    merge_heads(parts, out_ref, hold)
    merge_hidden(parts, out_ref, 4 * BLK)


def merge_heads(parts, out_ref, hold):
    x, _, _ = my_place()
    for at in range(4):
        hold[at] = parts[at][: 2 * BLK]
    for at in range(3):
        out_ref[at * BLK : (at + 1) * BLK] = hold[(at - x) & 3, :BLK]
    out_ref[3 * BLK : 4 * BLK] = hold[(0 - x) & 3, BLK:]


def merge_hidden(parts, out_ref, put):
    for member in (2, 3):
        for part in parts:
            out_ref[put : put + BLK] = part[member * BLK : (member + 1) * BLK]
            put += BLK


def swap_four(parts, row, core):
    parts = [jnp.where(core == 0, parts[at], parts[at ^ 1]) for at in range(4)]
    return [jnp.where(row == 0, parts[at], parts[at ^ 2]) for at in range(4)]


def lanes(block):
    return slice(block * BLK, (block + 1) * BLK)


def rotate_four(parts, count):
    parts = [jnp.where((count & 1) == 0, parts[at], parts[(at + 1) & 3]) for at in range(4)]
    return [jnp.where((count & 2) == 0, parts[at], parts[(at + 2) & 3]) for at in range(4)]


def to_own_order(vec_ref, base, out_ref):
    x, row, core = my_place()
    cube = [
        swap_four([vec_ref[base + at : base + at + 1, lanes(part)] for part in range(4)], row, core)
        for at in range(RINGX)
    ]
    for part in range(4):
        put = (part & 1) * 2 + (part >> 1)
        for hops, value in enumerate(rotate_four([four[part] for four in cube], x)):
            out_ref[put : put + 1, lanes(hops)] = value


def from_own_order(own_ref, vec_ref, base):
    x, row, core = my_place()
    cube = []
    for hops in range(RINGX):
        got = [(at & 1) * 2 + (at >> 1) for at in range(4)]
        cube.append(swap_four([own_ref[at : at + 1, lanes(hops)] for at in got], row, core))
    for part in range(4):
        for at, value in enumerate(rotate_four([four[part] for four in cube], 4 - x)):
            vec_ref[base + at : base + at + 1, lanes(part)] = value


def final_kernel(heads, hidden, spread, *refs):
    if spread:
        rows = refs[0].shape[0] // 2
        parts = [ref.at[pl.ds(at * rows, rows)] for ref in refs[:2] for at in range(2)]
        outs = list(refs[2:])
    else:
        parts, outs = refs[:4], list(refs[4:])
    _, row, core = my_place()
    base = 0
    if heads:
        qkv_ref, out_ref = outs[:2]
        outs = outs[2:]
        for at_part, part in enumerate(parts):
            piece = (row ^ (at_part & 1)) * 2 * BLK + (core ^ (at_part >> 1)) * BLK
            for at in range(3):
                qkv_ref[rows_at(at * WIDE + piece)] = part[at * BLK : (at + 1) * BLK]
            out_ref[rows_at(piece)] = part[3 * BLK : 4 * BLK]
        base = 4 * BLK
    if hidden:
        for member in range(2):
            for at_part, part in enumerate(parts):
                start = base + member * WIDE
                outs[member][at_part * WIDE : (at_part + 1) * WIDE] = part[start : start + WIDE]
        base += 2 * WIDE
        outs = outs[2:]
    if spread:
        total = full(parts[0][base : base + VPAD])
        for part in parts[1:]:
            total = total + full(part[base : base + VPAD])
        outs[0][...] = total
        for layer_at in range(LAYERS):
            base = layer_at * (VROWS // LAYERS) + 8
            to_own_order(outs[0], base, outs[1 + layer_at])


def from_x(part):
    return [part] + [along_x(part, -hops) for hops in (1, 2, 3)]


HOLD_HEADS = pltpu.VMEM((4, 2 * BLK, WIDE), jnp.bfloat16)


def all_four(own):
    beside = other_row(own)
    return [own, beside, other_core(own), other_core(beside)]


def whole(parts, heads, hidden, spread, name):
    outs = []
    if heads:
        outs += [(3 * WIDE, jnp.bfloat16), (WIDE, jnp.bfloat16)]
    if hidden:
        outs += [(FF, jnp.bfloat16)] * 2
    if spread:
        outs += [(VPAD, jnp.float32)] + [(4, jnp.float32)] * LAYERS
    return small_call(
        lambda *refs: final_kernel(heads, hidden, spread, *refs), outs, parts, name=name + "_whole"
    )


def put_vec(ref, start, value):
    high = half(value)
    ref[start : start + VPAD] = high
    ref[start + VPAD : start + 2 * VPAD] = half(value - full(high))


def get_vec(ref, start):
    return full(ref[start : start + VPAD]) + full(ref[start + VPAD : start + 2 * VPAD])


def split_heads(grads, keep_ref, sent_ref):
    _, _, core = my_place()
    put = 0
    for row in range(2):
        for at in range(4):
            start = at * WIDE + row * 2 * BLK
            keep_ref[put : put + BLK] = grads[rows_at(start + core * BLK)]
            sent_ref[put : put + BLK] = grads[rows_at(start + (1 - core) * BLK)]
            put += BLK


def split_row_kernel(heads, hidden, spread, *refs):
    had_ref, came_ref = refs[:2]
    keep_ref, sent_ref = refs[2 + spread : 4 + spread]
    _, row, _ = my_place()

    def total(start):
        at = rows_at(start, WIDE)
        return full(had_ref[at]) + full(came_ref[at])

    put, base = 0, 0
    if heads:
        keep_ref[:WIDE] = total(row * WIDE)
        sent_ref[:WIDE] = half(total((1 - row) * WIDE))
        put, base = WIDE, 2 * WIDE
    if hidden:
        for _ in range(2):
            keep_ref[put : put + WIDE] = total(base)
            sent_ref[put : put + WIDE] = half(total(base + WIDE))
            put, base = put + WIDE, base + 2 * WIDE
    if spread:
        value = refs[2][...] + get_vec(came_ref, base)
        refs[-1][...] = value
        put_vec(sent_ref, put, value)


def split_x_kernel(heads, hidden, spread, *refs):
    had_ref, came_ref = refs[:2]
    keep_ref, *sent_refs = refs[2 + spread : 6 + spread]
    hold = refs[-1]
    x, _, _ = my_place()
    count = had_ref.shape[0]
    hold[...] = had_ref[...] + full(came_ref[:count])
    for hops, target in enumerate([keep_ref] + sent_refs):
        kind = target.dtype
        put, base = 0, 0
        if heads:
            at = (x + hops) & 3
            piece = hold[rows_at(at * BLK)]
            target[:BLK] = jnp.where(at == 3, 0.0, piece).astype(kind)
            target[BLK : 2 * BLK] = hold[3 * BLK : 4 * BLK].astype(kind)
            put, base = 2 * BLK, WIDE
        if hidden:
            for _ in range(2):
                start = base + hops * BLK
                target[put : put + BLK] = hold[start : start + BLK].astype(kind)
                put, base = put + BLK, base + WIDE
        if spread and hops:
            value = refs[2][...] + get_vec(came_ref, base)
            refs[-2][...] = value
            put_vec(target, put, value)


def sum_x_kernel(heads, keep_ref, *refs):
    parts, out_ref = refs[:3], refs[3]
    x, _, _ = my_place()
    total = keep_ref[...]
    for part in parts:
        total = total + full(part[...])
    out_ref[...] = total
    if heads:
        out_ref[BLK : 2 * BLK] = jnp.where(x == 0, total[BLK : 2 * BLK], 0.0)


def scatter_row(keep, came, heads, hidden, spread, name, vec_sum=None):
    rows = 4 * BLK * heads + 8 * BLK * hidden
    return small_call(
        lambda *refs: split_row_kernel(heads, hidden, spread, *refs),
        [(rows, jnp.float32), (rows + 2 * VPAD * spread, jnp.bfloat16)]
        + [(VPAD, jnp.float32)] * spread,
        [keep, came] + [vec_sum] * spread,
        name=name + "_split_row",
    )


def scatter_x(keep, came, heads, hidden, spread, name, vec_sum=None):
    rows = 2 * BLK * heads + 2 * BLK * hidden
    return small_call(
        lambda *refs: split_x_kernel(heads, hidden, spread, *refs),
        [(rows, jnp.float32)]
        + [(rows + 2 * VPAD * spread, jnp.bfloat16)] * 3
        + [(VPAD, jnp.float32)] * spread,
        [keep, came] + [vec_sum] * spread,
        scratch=[pltpu.VMEM(keep.shape, jnp.float32)],
        name=name + "_split_x",
    )


def spread_x(sent):
    return [along_x(part, hops + 1) for hops, part in enumerate(sent)]


def split_group_kernel(slot_ref, *refs):
    second_ref, third_ref, keep_ref, *parts = refs[:6]
    vec_ref, own_ref = refs[6], refs[7]
    sent_refs, vec_out, hold = refs[8:15], refs[15], refs[16]
    flip, z = my_group()
    x, _, _ = my_place()
    total = keep_ref[...]
    value = vec_ref[...]
    for part in parts:
        total = total + full(part[: 2 * BLK])
        value = value + get_vec(part, 2 * BLK)
    vec_out[...] = value
    hold[0] = total[:BLK]
    hold[1] = jnp.where(x == 0, total[BLK:], 0.0)
    for member in range(2):
        hold[2 + member] = second_ref[member * BLK : (member + 1) * BLK]
    for member in range(4):
        hold[4 + member] = third_ref[member * BLK : (member + 1) * BLK]
    for at, (turn, hops) in enumerate(STEPS):
        slot = (flip ^ turn) * RINGZ + ((z + hops) & 3)
        mat_index = jnp.int32(0)
        for member in range(1, MATS):
            mat_index = jnp.where(slot_ref[member] == slot, member, mat_index)
        if at == 0:
            own_ref[...] = hold[mat_index]
        else:
            sent_refs[at - 1][:BLK] = half(hold[mat_index])
            put_vec(sent_refs[at - 1], BLK, value)


def renew_kernel(own_ref, *refs):
    parts, (vec_ref, moment_ref) = refs[:7], refs[7:9]
    grad_ref, new_ref, low_ref, vec_out = refs[9:]
    total, value = own_ref[...], vec_ref[...]
    for part in parts:
        total = total + full(part[:BLK])
        value = value + get_vec(part, BLK)
    grad_ref[...] = total
    vec_out[...] = value
    renewed = momentum_keep * moment_ref[...] + total
    new_ref[...] = renewed
    low_ref[...] = half(renewed)


def parts_of(value):
    high = half(value)
    return high, half(value - full(high))


def as_left(value):
    high, low = parts_of(value)
    return jnp.concatenate([high, high, low], 1)


def as_right(value):
    high, low = parts_of(value)
    return jnp.concatenate([high, low, high], 0)


def product(left, right):
    return jnp.dot(left, right, preferred_element_type=jnp.float32)


def newton_kernel(slot_ref, *refs):
    parts, own_ref, weight_ref, out_ref = refs[:4], refs[4], refs[5], refs[6]
    size = WIDE
    gram = None
    for part in parts:
        piece = row_contract(part[...], part[...])
        gram = piece if gram is None else gram + piece
    diagonal = lax.broadcasted_iota(jnp.int32, (size, size), 0) == lax.broadcasted_iota(
        jnp.int32, (size, size), 1
    )
    trace = jnp.sum(jnp.where(diagonal, gram, 0.0), keepdims=True)
    inverse = 1.0 / (jnp.sqrt(trace) + ortho_eps)
    gram = gram * inverse * inverse
    total = None
    for iteration in range(NEWTON_STEPS):
        squared = product(as_left(gram), as_right(gram))
        step = jnp.where(diagonal, coef_a, 0.0) + coef_b * gram + coef_c * squared
        left = as_left(step)
        if iteration == 0:
            total = step
            gram = product(left, as_right(product(left, as_right(gram))))
        elif iteration < NEWTON_STEPS - 1:
            both = product(left, as_right(jnp.concatenate([gram, total], 1)))
            total = both[:, size:]
            gram = product(left, as_right(both[:, :size]))
        else:
            total = product(left, as_right(total))
    high, low = parts_of(total * inverse)
    own = own_ref[...]
    ortho = product(own, high) + product(own, low)
    group = lax.axis_index("group")
    widths = [3 * WIDE, WIDE, FF, FF] * LAYERS
    scale = jnp.float32(0.0)
    for member in range(MATS):
        rate = muon_rate * muon_shape * widths[member] ** 0.5
        scale = jnp.where(slot_ref[member] == group, jnp.float32(rate), scale)
    out_ref[...] = weight_ref[...] * (1.0 - muon_rate * muon_decay) - scale * ortho


def turned(part):
    return half(full(part).T)


def column(index):
    return slice(index * 128, (index + 1) * 128)


def row_of(vec_ref, layer_at, index):
    at = layer_at * (VROWS // LAYERS) + index
    return vec_ref[at : at + 1]


def attend_kernel(layer_at, need, flush, in_ref, qkv_w, out_w, vec_ref, mid_ref, qkv_ref, attn_ref, prob_ref):
    normed, _ = normalize(in_ref[...])
    normed_low = half(normed * row_of(vec_ref, layer_at, 0) + row_of(vec_ref, layer_at, 1))
    for third in range(3):
        rows = slice(third * WIDE, (third + 1) * WIDE)
        value = col_contract(normed_low, qkv_w[rows])
        if third != 1:
            value = value + row_of(vec_ref, layer_at, 2 if third == 0 else 3)
        qkv_ref[:, rows] = half(value)
    flush(1)
    for at in range(HEADS // 2):
        attend_pair(at, qkv_ref, attn_ref, prob_ref)
        flush(3, at)
    flush(2)
    need(0)
    mid_ref[...] = in_ref[...] + (
        col_contract(attn_ref[...], out_w[...]) + row_of(vec_ref, layer_at, 4)
    )


def attend_pair(at, qkv_ref, attn_ref, prob_ref):
    queries = qkv_ref[:, column(at)] * jnp.bfloat16(0.125)
    keys, values = qkv_ref[:, column(3 + at)], qkv_ref[:, column(6 + at)]
    lane = lax.broadcasted_iota(jnp.int32, keys.shape, 1)
    values_t = turned(values)
    sums = []
    for head in range(2):
        mine = half(jnp.where((lane >> 6) == head, 1.0, 0.0))
        scores = col_contract(keys * mine, queries)
        exponent = jnp.exp(scores - jnp.max(scores, 0, keepdims=True))
        probs = half(exponent * (1.0 / jnp.sum(exponent, 0, keepdims=True)))
        prob_ref[2 * at + head] = probs
        sums.append(product(values_t, probs))
    row = lax.broadcasted_iota(jnp.int32, sums[0].shape, 0)
    attn_ref[:, column(at)] = half(jnp.where(row < 64, sums[0], sums[1]).T)


def attend_back_kernel(layer_at, need, flush, up_ref, in_ref, qkv_ref, attn_ref, prob_ref, qkv_w, out_w, vec_ref, *refs):
    spread = len(refs) > 8
    others = refs[:5] if spread else ()
    grad_ref, keep_ref, sent_ref, total_ref, upstream_ref, back_ref, grads_ref, sum_ref = refs[-8:]
    sum_ref[...] = jnp.zeros_like(sum_ref)
    out_low = half(up_ref[...])
    grads_ref[3 * WIDE :] = half(row_contract(out_low, attn_ref[...]))
    upstream_ref[...] = half(product(out_low, out_w[...]))
    sum_ref[4:5] = jnp.sum(full(out_low), 0, keepdims=True)
    for at in range(HEADS // 2):
        need(at)
        attend_back_pair(at, qkv_ref, upstream_ref, prob_ref, back_ref)
    normed, inv_std = normalize(in_ref[...])
    gain = row_of(vec_ref, layer_at, 0)
    normed_low = half(normed * gain + row_of(vec_ref, layer_at, 1))
    back_normed = jnp.zeros(normed.shape, jnp.float32)
    for third in range(3):
        rows = slice(third * WIDE, (third + 1) * WIDE)
        piece = back_ref[:, rows]
        grads_ref[rows] = half(row_contract(piece, normed_low))
        back_normed = back_normed + product(piece, qkv_w[rows])
        if third != 1:
            put = 2 if third == 0 else 3
            sum_ref[put : put + 1] = jnp.sum(full(piece), 0, keepdims=True)
    sum_ref[0:1] = jnp.sum(back_normed * normed, 0, keepdims=True)
    sum_ref[1:2] = jnp.sum(back_normed, 0, keepdims=True)
    grad_ref[...] = up_ref[...] + norm_back(back_normed, normed, inv_std, gain)
    flush(0)
    split_heads(grads_ref, keep_ref, sent_ref)
    if not spread:
        total_ref[...] = sum_ref[...]
        return
    total_ref[VROWS:] = jnp.zeros((VPAD - VROWS, WIDE), jnp.float32)
    pieces = (sum_ref, *others)
    for layer in range(LAYERS):
        base = layer * (VROWS // LAYERS)
        one, two, three = pieces[3 * layer : 3 * layer + 3]
        total_ref[base : base + 5] = one[:5]
        total_ref[base + 5 : base + 8] = two[:3]
        from_own_order(three, total_ref, base + 8)
    put_vec(sent_ref, 2 * WIDE, total_ref[...])


def attend_back_pair(at, qkv_ref, upstream_ref, prob_ref, back_ref):
    queries, keys, values = (qkv_ref[:, column(3 * third + at)] for third in range(3))
    upstream = upstream_ref[:, column(at)]
    lane = lax.broadcasted_iota(jnp.int32, keys.shape, 1)
    keys_t = turned(keys)
    got = []
    for head in range(2):
        mine = half(jnp.where((lane >> 6) == head, 1.0, 0.0))
        probs_low = prob_ref[2 * at + head]
        probs = full(probs_low)
        prob_grad = col_contract(values * mine, upstream)
        inner = jnp.sum(prob_grad * probs, 0, keepdims=True)
        score_low = half(probs * (prob_grad - inner))
        got.append(
            (product(keys_t, score_low), product(score_low, queries), product(probs_low, upstream))
        )
    row = lax.broadcasted_iota(jnp.int32, got[0][0].shape, 0)
    back_ref[:, column(at)] = half(jnp.where(row < 64, got[0][0], got[1][0]).T * 0.125)
    back_ref[:, column(3 + at)] = half(jnp.where(lane < 64, got[0][1], got[1][1]) * 0.125)
    back_ref[:, column(6 + at)] = half(jnp.where(lane < 64, got[0][2], got[1][2]))


def hidden_kernel(layer_at, need, flush, mid_ref, up_w, down_w, vec_ref, bias_ref, out_ref, act_ref, slope_ref):
    normed, _ = normalize(mid_ref[...])
    hidden_low = half(normed * row_of(vec_ref, layer_at, 5) + row_of(vec_ref, layer_at, 6))
    total = mid_ref[...] + row_of(vec_ref, layer_at, 7)
    for chunk in range(4):
        need(chunk)
        rows = slice(chunk * WIDE, (chunk + 1) * WIDE)
        hidden = col_contract(hidden_low, up_w[rows]) + bias_ref[chunk : chunk + 1]
        share = 0.5 * (1.0 + lax.erf(hidden * half_root))
        active_low = half(hidden * share)
        act_ref[:, rows] = active_low
        slope_ref[:, rows] = share + hidden * jnp.exp(-0.5 * hidden * hidden) * density
        total = total + product(active_low, down_w[rows])
        flush(1, chunk)
        flush(2, chunk)
    out_ref[...] = total


def hidden_back_kernel(layer_at, need, flush, up_ref, mid_ref, act_ref, slope_ref, up_w, down_w, vec_ref, grad_ref, keep_ref, sent_ref, sum_ref, bias_ref):
    down_low = half(up_ref[...])
    normed, inv_std = normalize(mid_ref[...])
    gain = row_of(vec_ref, layer_at, 5)
    hidden_low = half(normed * gain + row_of(vec_ref, layer_at, 6))
    back_hidden = jnp.zeros(normed.shape, jnp.float32)
    sum_ref[...] = jnp.zeros_like(sum_ref)
    for chunk in range(4):
        need(chunk)
        rows = slice(chunk * WIDE, (chunk + 1) * WIDE)
        up_low = half(col_contract(down_low, down_w[rows]) * slope_ref[:, rows])
        target, turn_at = (keep_ref, sent_ref)[chunk // 2], chunk % 2
        for member, value in enumerate(
            (row_contract(up_low, hidden_low), row_contract(act_ref[:, rows], down_low))
        ):
            put = (2 * member + turn_at) * WIDE
            target[put : put + WIDE] = half(value)
            flush(1 + chunk // 2, 2 * member + turn_at)
        bias_ref[chunk : chunk + 1] = jnp.sum(full(up_low), 0, keepdims=True)
        back_hidden = back_hidden + product(up_low, up_w[rows])
    sum_ref[0:1] = jnp.sum(back_hidden * normed, 0, keepdims=True)
    sum_ref[1:2] = jnp.sum(back_hidden, 0, keepdims=True)
    sum_ref[2:3] = jnp.sum(full(down_low), 0, keepdims=True)
    grad_ref[...] = up_ref[...] + norm_back(back_hidden, normed, inv_std, gain)


def layer_one_kernel(layer_at, need, flush, in_ref, cot_ref, qkv_w, out_w, up_w, down_w, vec_ref, bias_ref, *refs):
    stream_ref, grad_ref, keep_ref, sent_ref, one_ref, two_ref, bias_sum_ref = refs[:7]
    mid_ref, qkv_ref, attn_ref, prob_ref, act_ref, slope_ref, mid_grad_ref, *rest = refs[7:]
    heads, hidden = pl.ds(0, 2 * WIDE), pl.ds(2 * WIDE, 4 * WIDE)

    def nothing(*_):
        pass

    attend_kernel(
        layer_at, need, nothing, in_ref, qkv_w, out_w, vec_ref, mid_ref, qkv_ref, attn_ref, prob_ref
    )
    hidden_kernel(
        layer_at,
        nothing,
        nothing,
        mid_ref,
        up_w,
        down_w,
        vec_ref,
        bias_ref,
        stream_ref,
        act_ref,
        slope_ref,
    )
    flush(0)
    hidden_back_kernel(
        layer_at,
        nothing,
        nothing,
        cot_ref,
        mid_ref,
        act_ref,
        slope_ref,
        up_w,
        down_w,
        vec_ref,
        mid_grad_ref,
        keep_ref.at[hidden],
        sent_ref.at[hidden],
        two_ref,
        bias_sum_ref,
    )
    for piece in (1, 2):
        flush(2, piece)
        flush(3, piece)
    attend_back_kernel(
        layer_at,
        nothing,
        nothing,
        mid_grad_ref,
        in_ref,
        qkv_ref,
        attn_ref,
        prob_ref,
        qkv_w,
        out_w,
        vec_ref,
        grad_ref,
        keep_ref.at[heads],
        sent_ref.at[heads],
        one_ref,
        *rest,
    )


def far_spec():
    return pl.BlockSpec(memory_space=pltpu.HBM)


def cut_piece(ref, how, at):
    if how is None:
        return ref
    dimension, pieces = how
    size = ref.shape[dimension] // pieces
    return ref.at[(slice(None),) * dimension + (pl.ds(at * size, size),)]


def layer_call(kernel, layer_at, ins, outs, in_cut, out_cut, scratch=(), name=None):
    count, total = len(ins), len(outs)
    pieces = max([how[1] for how in in_cut.values()] + [1])
    in_plan = [(at, None, 0) for at in range(count) if at not in in_cut]
    in_plan += [(at, in_cut[at], piece) for piece in range(pieces) for at in sorted(in_cut)]
    out_plan = []
    for at in range(total):
        how = out_cut.get(at)
        out_plan += [(at, how, piece) for piece in range(how[1] if how else 1)]

    def body(*refs):
        far, near = refs[: count + total], refs[count + total : 2 * (count + total)]
        come_sems, leave_sems = refs[2 * (count + total) : 2 * (count + total) + 2]
        rest = refs[2 * (count + total) + 2 :]
        come = [
            pltpu.make_async_copy(
                cut_piece(far[at], how, piece), cut_piece(near[at], how, piece), come_sems.at[index]
            )
            for index, (at, how, piece) in enumerate(in_plan)
        ]
        leave = [
            pltpu.make_async_copy(
                cut_piece(near[count + at], how, piece),
                cut_piece(far[count + at], how, piece),
                leave_sems.at[index],
            )
            for index, (at, how, piece) in enumerate(out_plan)
        ]
        started = []

        def need(wanted):
            for (_, how, piece), copy in zip(in_plan, come):
                if (how is None and wanted is None) or (how is not None and piece == wanted):
                    copy.wait()

        def flush(out_at, wanted=0):
            index = [(at, piece) for at, _, piece in out_plan].index((out_at, wanted))
            leave[index].start()
            started.append(index)

        for copy in come:
            copy.start()
        need(None)
        kernel(layer_at, need, flush, *near, *rest)
        for index, copy in enumerate(leave):
            if index not in started:
                copy.start()
        for copy in leave:
            copy.wait()

    return pl.pallas_call(
        body,
        out_shape=[jax.ShapeDtypeStruct(shape, kind) for shape, kind in outs],
        in_specs=[far_spec()] * count,
        out_specs=[far_spec()] * total,
        scratch_shapes=[pltpu.VMEM(part.shape, part.dtype) for part in ins]
        + [pltpu.VMEM(shape, kind) for shape, kind in outs]
        + [pltpu.SemaphoreType.DMA((len(in_plan),)), pltpu.SemaphoreType.DMA((len(out_plan),))]
        + list(scratch),
        compiler_params=pltpu.CompilerParams(vmem_limit_bytes=64 << 20),
        cost_estimate=pl.CostEstimate(flops=1 << 20, bytes_accessed=1 << 16, transcendentals=0),
        name=name,
    )(*ins)


def attention_forward(layer_at, inputs, w_qkv, w_out, vec_full):
    length = inputs.shape[0]
    return layer_call(
        attend_kernel,
        layer_at,
        [inputs, w_qkv, w_out, vec_full],
        [
            (inputs.shape, jnp.float32),
            ((length, 3 * WIDE), jnp.bfloat16),
            (inputs.shape, jnp.bfloat16),
            ((HEADS, length, length), jnp.bfloat16),
        ],
        {2: (0, 1)},
        {3: (0, HEADS // 2)},
        name="attend",
    )


def back_scratch(length):
    return [
        pltpu.VMEM((length, WIDE), jnp.bfloat16),
        pltpu.VMEM((length, 3 * WIDE), jnp.bfloat16),
        pltpu.VMEM((4 * WIDE, WIDE), jnp.bfloat16),
        pltpu.VMEM((8, WIDE), jnp.float32),
    ]


def attention_backward(layer_at, upstream, inputs, stored, w_qkv, w_out, vec_full, others):
    qkv_low, attn_low, probs = stored
    return layer_call(
        attend_back_kernel,
        layer_at,
        [upstream, inputs, qkv_low, attn_low, probs, w_qkv, w_out, vec_full, *others],
        [
            (inputs.shape, jnp.float32),
            ((2 * WIDE, WIDE), jnp.bfloat16),
            ((2 * WIDE + 2 * VPAD, WIDE), jnp.bfloat16),
            ((VPAD, WIDE), jnp.float32),
        ],
        {4: (0, HEADS // 2)},
        {},
        scratch=back_scratch(inputs.shape[0]),
        name="attend_back",
    )


def layer_one(inputs, cotangent, w_qkv, w_out, w_up, w_down, vec_full, bias_up):
    length = inputs.shape[0]
    return layer_call(
        layer_one_kernel,
        1,
        [inputs, cotangent, w_qkv, w_out, w_up, w_down, vec_full, bias_up],
        [
            (inputs.shape, jnp.float32),
            (inputs.shape, jnp.float32),
            ((6 * WIDE, WIDE), jnp.bfloat16),
            ((6 * WIDE, WIDE), jnp.bfloat16),
            ((8, WIDE), jnp.float32),
            ((8, WIDE), jnp.float32),
            ((4, WIDE), jnp.float32),
        ],
        {1: (0, 1), 3: (0, 1), 4: (0, 1), 5: (0, 1)},
        {2: (0, 3), 3: (0, 3)},
        scratch=[
            pltpu.VMEM(inputs.shape, jnp.float32),
            pltpu.VMEM((length, 3 * WIDE), jnp.bfloat16),
            pltpu.VMEM(inputs.shape, jnp.bfloat16),
            pltpu.VMEM((HEADS, length, length), jnp.bfloat16),
            pltpu.VMEM((length, FF), jnp.bfloat16),
            pltpu.VMEM((length, FF), jnp.float32),
            pltpu.VMEM(inputs.shape, jnp.float32),
            *back_scratch(length),
        ],
        name="layer_one",
    )


def hidden_forward(layer_at, middle, w_up, w_down, vec_full, bias_up):
    wide = (middle.shape[0], FF)
    return layer_call(
        hidden_kernel,
        layer_at,
        [middle, w_up, w_down, vec_full, bias_up],
        [(middle.shape, jnp.float32), (wide, jnp.bfloat16), (wide, jnp.float32)],
        {1: (0, 4), 2: (0, 4)},
        {1: (1, 4), 2: (1, 4)},
        name="hidden",
    )


def hidden_backward(layer_at, upstream, middle, stored, w_up, w_down, vec_full):
    return layer_call(
        hidden_back_kernel,
        layer_at,
        [upstream, middle, *stored, w_up, w_down, vec_full],
        [
            (middle.shape, jnp.float32),
            (w_up.shape, jnp.bfloat16),
            (w_up.shape, jnp.bfloat16),
            ((8, WIDE), jnp.float32),
            ((4, WIDE), jnp.float32),
        ],
        {2: (1, 4), 3: (1, 4), 4: (0, 4), 5: (0, 4)},
        {1: (0, 4), 2: (0, 4)},
        name="hidden_back",
    )


def on_device(tokens, cotangent, live, slot_of, weights, momentum, vec, vec_first, vec_second):
    group_at = lax.axis_index("group")
    data_at = lax.axis_index("dp")
    vec_here, vec_cols = vec.shape
    per_layer = VROWS // LAYERS
    tie = lax.optimization_barrier
    spread = lax.dynamic_update_slice(
        jnp.zeros((VPAD, WIDE), jnp.bfloat16),
        half(vec),
        (group_at * vec_here, data_at * vec_cols),
    )
    own_block = jnp.concatenate([half(weights[0].T), spread], 0)
    pair = jnp.concatenate([own_block, along_group(own_block, 1, 0)], 0)
    slots = [pair] + [along_group(pair, 0, -hops) for hops in (1, 2, 3)]
    first, third = small_call(
        choose_kernel,
        [(4 * BLK + VPAD, jnp.bfloat16), (4 * BLK, jnp.bfloat16)],
        [slot_of] + slots,
        slot_first=True,
        scratch=[pltpu.VMEM((MATS, BLK, WIDE), jnp.bfloat16)],
        name="choose",
    )
    first_x, second_x = small_call(
        merge_first_kernel,
        [(4 * BLK + VPAD, jnp.bfloat16), (8 * BLK, jnp.bfloat16)],
        from_x(first),
        scratch=[HOLD_HEADS],
        name="first_merge_x",
    )
    second_x, third, first_x = tie((second_x, third, first_x))
    beside_first = other_row(first_x)
    pair_first = jnp.concatenate([first_x, beside_first], 0)
    first_parts = [pair_first, other_core(pair_first)]
    beside_second, core_second = other_row(second_x), other_core(second_x)
    third_parts = from_x(third)
    w_qkv0, w_out0, vec_full, bias0, bias1 = whole(first_parts, True, False, True, "first")
    inputs0 = tokens[0]
    middle0, *attn0 = attention_forward(0, inputs0, w_qkv0, w_out0, vec_full)
    third_parts, beside_second, middle0 = tie((third_parts, beside_second, middle0))
    (third_x,) = small_call(
        merge_third_kernel,
        [(12 * BLK, jnp.bfloat16)],
        third_parts,
        scratch=[HOLD_HEADS],
        name="third_merge_x",
    )
    beside = other_row(third_x)
    core_third = other_core(third_x)
    second_parts = [second_x, beside_second, core_second, other_core(beside_second)]
    w_up0, w_down0 = whole(second_parts, False, True, False, "second")
    inputs1, *mlp0 = hidden_forward(0, middle0, w_up0, w_down0, vec_full, bias0)
    beside, inputs1 = tie((beside, inputs1))
    third_parts = [third_x, beside, core_third, other_core(beside)]
    w_qkv1, w_out1, w_up1, w_down1 = whole(third_parts, True, True, False, "third")
    upstream = cotangent[0] * full(live)[0]
    stream, upstream, keep, sent, sums_one1, sums_two1, sums_up1 = layer_one(
        inputs1, upstream, w_qkv1, w_out1, w_up1, w_down1, vec_full, bias1
    )
    came = other_core(sent)
    mid_grad, keep_f, sent_f, sums_two0, sums_up0 = hidden_backward(
        0, upstream, middle0, mlp0, w_up0, w_down0, vec_full
    )
    came_f = other_core(sent_f)
    vec_full, came = tie((vec_full, came))
    keep, sent = scatter_row(keep, came, True, True, False, "third")
    vec_full, sent = tie((vec_full, sent))
    came = other_row(sent)
    token_grad, keep_h, sent_h, vec_sum = attention_backward(
        0,
        mid_grad,
        inputs0,
        attn0,
        w_qkv0,
        w_out0,
        vec_full,
        (sums_two0, sums_up0, sums_one1, sums_two1, sums_up1),
    )
    vec_sum, came_f = tie((vec_sum, came_f))
    keep_f, sent_f = scatter_row(keep_f, came_f, False, True, False, "second")
    sent_h, sent_f, came = tie((sent_h, sent_f, came))
    came_f = other_row(sent_f)
    came_h = other_core(sent_h)
    keep, *sent_x = scatter_x(keep, came, True, True, False, "third")
    came_x = spread_x(sent_x)
    came_f, came_x = tie((came_f, came_x))
    keep_h, sent_h, vec_sum = scatter_row(keep_h, came_h, True, False, True, "first", vec_sum)
    came_h = other_row(sent_h)
    keep_f, *sent_f = scatter_x(keep_f, came_f, False, True, False, "second")
    (third_sum,) = small_call(
        lambda *refs: sum_x_kernel(True, *refs),
        [(4 * BLK, jnp.float32)],
        [keep] + came_x,
        name="third_sum_x",
    )
    came_f = spread_x(sent_f)
    (second_sum,) = small_call(
        lambda *refs: sum_x_kernel(False, *refs),
        [(2 * BLK, jnp.float32)],
        [keep_f] + came_f,
        name="second_sum_x",
    )
    keep_h, *sent_h, vec_sum = scatter_x(keep_h, came_h, True, False, True, "first", vec_sum)
    came_h = spread_x(sent_h)
    own, *sent_g, vec_sum = small_call(
        split_group_kernel,
        [(BLK, jnp.float32)]
        + [(BLK + 2 * VPAD, jnp.bfloat16)] * 7
        + [(VPAD, jnp.float32)],
        [slot_of, second_sum, third_sum, keep_h] + came_h + [vec_sum],
        slot_first=True,
        scratch=[pltpu.VMEM((MATS, BLK, WIDE), jnp.float32)],
        name="split_group",
    )
    came_g = [along_group(part, flip, hops) for part, (flip, hops) in zip(sent_g, STEPS[1:])]
    grad_rows, moment_rows, moment_low, vec_sum = small_call(
        renew_kernel,
        [(BLK, jnp.float32), (BLK, jnp.float32), (BLK, jnp.bfloat16), (VPAD, jnp.float32)],
        [own] + came_g + [vec_sum, momentum[0].T],
        name="renew",
    )
    ring = jnp.concatenate([moment_low] + [along_x(moment_low, -hops) for hops in (1, 2, 3)], 0)
    beside = other_row(ring)
    (weight_rows,) = small_call(
        newton_kernel,
        [(BLK, jnp.float32)],
        [slot_of, ring, beside, other_core(ring), other_core(beside), moment_low, weights[0].T],
        slot_first=True,
        name="newton",
    )
    shard_vec = lax.dynamic_slice(
        vec_sum, (group_at * vec_here, data_at * vec_cols), (vec_here, vec_cols)
    )
    first_new = first_keep * vec_first + (1.0 - first_keep) * shard_vec
    second_new = second_keep * vec_second + (1.0 - second_keep) * shard_vec * shard_vec
    vec_new = vec - adam_rate * (
        first_new
        / (1.0 - first_keep**STEP)
        / (jnp.sqrt(second_new / (1.0 - second_keep**STEP)) + adam_eps)
    )
    return (
        stream[None],
        token_grad[None],
        grad_rows.T[None],
        moment_rows.T[None],
        weight_rows.T[None],
        first_new,
        second_new,
        vec_new,
    )


def solution(mesh):
    placed = (
        P(("group", "dp"), None, None),
        P(("group", "dp"), None, None),
        P(("group", "dp")),
        P(),
        P("group", None, "dp"),
        P("group", None, "dp"),
        P("group", "dp"),
        P("group", "dp"),
        P("group", "dp"),
    )
    return jax.shard_map(
        on_device,
        mesh=mesh,
        in_specs=placed,
        out_specs=(
            P(("group", "dp"), None, None),
            P(("group", "dp"), None, None),
            P("group", None, "dp"),
            P("group", None, "dp"),
            P("group", None, "dp"),
            P("group", "dp"),
            P("group", "dp"),
            P("group", "dp"),
        ),
        check_vma=False,
    )
```

```python
import jax
import jax.numpy as jnp
from jax import lax
from jax.experimental import pallas as pl
from jax.experimental.pallas import tpu as pltpu
from jax.sharding import PartitionSpec as P

HEADS = 6
FF = 1536
LAYERS = 2
NEWTON_STEPS = 5
STEP = 10
MATS = 8
VROWS = 24


norm_eps = 1e-06
ortho_eps = 1e-07
coef_a = 3.4445
coef_b = -4.775
coef_c = 2.0315
momentum_keep = 0.95
muon_rate = 0.25
muon_decay = 0.01
muon_shape = 0.5
adam_rate = 0.4
first_keep = 0.9
second_keep = 0.999
adam_eps = 1e-08
half_root = 0.7071067811865476
density = 0.3989422804014327


def normalize(values):
    center = values - jnp.mean(values, -1, keepdims=True)
    inv_std = lax.rsqrt(jnp.mean(center * center, -1, keepdims=True) + norm_eps)
    return (center * inv_std, inv_std)


def norm_back(upstream, normed, inv_std, gain):
    scaled = upstream * gain
    return inv_std * (
        scaled
        - jnp.mean(scaled, -1, keepdims=True)
        - normed * jnp.mean(scaled * normed, -1, keepdims=True)
    )


def gelu_slope(values):
    return (
        0.5 * (1.0 + lax.erf(values * half_root))
        + values * jnp.exp(-0.5 * values * values) * density
    )


def row_contract(left_op, right_op):
    return lax.dot_general(
        left_op, right_op, (((0,), (0,)), ((), ())), preferred_element_type=jnp.float32
    )


def col_contract(left_op, right_op):
    return lax.dot_general(
        left_op, right_op, (((1,), (1,)), ((), ())), preferred_element_type=jnp.float32
    )


BLK = 96
WIDE = 384
VPAD = 32
RINGX = 4
RINGZ = 4
STEPS = [(flip, hops) for flip in range(2) for hops in range(RINGZ)]


def half(part):
    return part.astype(jnp.bfloat16)


def full(part):
    return part.astype(jnp.float32)


def near(part, change):
    return lax.ppermute(part, "dp", [(at, change(at)) for at in range(16)])


def other_core(part):
    return near(part, lambda at: at ^ 1)


def other_row(part):
    return near(part, lambda at: at ^ 2)


def along_x(part, hops):
    return near(part, lambda at: (at + 4 * hops) % 16)


def along_group(part, flip, hops):
    pairs = [(at, (at ^ (4 * flip)) // 4 * 4 + (at + hops) % RINGZ) for at in range(8)]
    return lax.ppermute(part, "group", pairs)


def my_place():
    spot = lax.axis_index("dp")
    return spot >> 2, (spot >> 1) & 1, spot & 1


def my_group():
    group = lax.axis_index("group")
    return group >> 2, group & 3


def rows_at(start, count=BLK):
    return pl.ds(pl.multiple_of(start, 32), count)


def small_call(kernel, outs, ins, slot_first=False, scratch=(), name=None, vmem=12):
    specs = [pl.BlockSpec(memory_space=pltpu.VMEM)] * len(ins)
    if slot_first:
        specs[0] = pl.BlockSpec(memory_space=pltpu.SMEM)
    return pl.pallas_call(
        kernel,
        out_shape=[jax.ShapeDtypeStruct((rows, WIDE), kind) for rows, kind in outs],
        in_specs=specs,
        out_specs=[pl.BlockSpec(memory_space=pltpu.VMEM)] * len(outs),
        scratch_shapes=list(scratch),
        compiler_params=pltpu.CompilerParams(vmem_limit_bytes=vmem << 20),
        name=name,
    )(*ins)


def far_spec():
    return pl.BlockSpec(memory_space=pltpu.HBM)


def far_call(kernel, outs, ins, slot_first=False, scratch=(), name=None, vmem=64):
    lead, count, total = int(slot_first), len(ins) - int(slot_first), len(outs)

    def body(*refs):
        far, near = refs[lead : lead + count + total], refs[lead + count + total :]
        sems, rest = near[count + total], near[count + total + 1 :]
        come = [
            pltpu.make_async_copy(far[at], near[at], sems.at[at]) for at in range(count)
        ]
        for copy in come:
            copy.start()
        for copy in come:
            copy.wait()
        kernel(*refs[:lead], *near[: count + total], *rest)
        leave = [
            pltpu.make_async_copy(near[at], far[at], sems.at[at])
            for at in range(count, count + total)
        ]
        for copy in leave:
            copy.start()
        for copy in leave:
            copy.wait()

    return pl.pallas_call(
        body,
        out_shape=[jax.ShapeDtypeStruct((rows, WIDE), kind) for rows, kind in outs],
        in_specs=[pl.BlockSpec(memory_space=pltpu.SMEM)] * lead + [far_spec()] * count,
        out_specs=[far_spec()] * total,
        scratch_shapes=[pltpu.VMEM(part.shape, part.dtype) for part in ins[lead:]]
        + [pltpu.VMEM((rows, WIDE), kind) for rows, kind in outs]
        + [pltpu.SemaphoreType.DMA((count + total,))]
        + list(scratch),
        compiler_params=pltpu.CompilerParams(vmem_limit_bytes=vmem << 20),
        cost_estimate=pl.CostEstimate(flops=1 << 20, bytes_accessed=1 << 16, transcendentals=0),
        name=name,
    )(*ins)


def choose_kernel(slot_ref, *refs):
    pairs, (first_ref, third_ref), hold = refs[:4], refs[4:6], refs[6]
    flip, z = my_group()
    spread = None
    for turn, hops in STEPS:
        base = turn * (BLK + VPAD)
        hold[turn * RINGZ + hops] = pairs[hops][base : base + BLK]
        piece = full(pairs[hops][base + BLK : base + BLK + VPAD])
        spread = piece if spread is None else spread + piece

    def matrix(mat_index):
        slot = slot_ref[mat_index]
        return hold[((slot >> 2) ^ flip) * RINGZ + ((slot - z) & 3)]

    first_ref[4 * BLK :] = half(spread)
    for member in range(4):
        first_ref[member * BLK : (member + 1) * BLK] = matrix(member)
        third_ref[member * BLK : (member + 1) * BLK] = matrix(4 + member)


def merge_first_kernel(*refs):
    parts, head_ref, hidden_ref, hold = refs[:4], refs[4], refs[5], refs[6]
    merge_heads(parts, head_ref, hold)
    merge_hidden(parts, hidden_ref, 0)
    total = full(parts[0][4 * BLK :])
    for at in range(1, 4):
        total = total + full(parts[at][4 * BLK :])
    head_ref[4 * BLK :] = half(total)


def merge_third_kernel(*refs):
    parts, out_ref, hold = refs[:4], refs[4], refs[5]
    merge_heads(parts, out_ref, hold)
    merge_hidden(parts, out_ref, 4 * BLK)


def merge_heads(parts, out_ref, hold):
    x, _, _ = my_place()
    for at in range(4):
        hold[at] = parts[at][: 2 * BLK]
    for at in range(3):
        out_ref[at * BLK : (at + 1) * BLK] = hold[(at - x) & 3, :BLK]
    out_ref[3 * BLK : 4 * BLK] = hold[(0 - x) & 3, BLK:]


def merge_hidden(parts, out_ref, put):
    for member in (2, 3):
        for part in parts:
            out_ref[put : put + BLK] = part[member * BLK : (member + 1) * BLK]
            put += BLK


def swap_four(parts, row, core):
    parts = [jnp.where(core == 0, parts[at], parts[at ^ 1]) for at in range(4)]
    return [jnp.where(row == 0, parts[at], parts[at ^ 2]) for at in range(4)]


def lanes(block):
    return slice(block * BLK, (block + 1) * BLK)


def rotate_four(parts, count):
    parts = [jnp.where((count & 1) == 0, parts[at], parts[(at + 1) & 3]) for at in range(4)]
    return [jnp.where((count & 2) == 0, parts[at], parts[(at + 2) & 3]) for at in range(4)]


def to_own_order(vec_ref, base, out_ref):
    x, row, core = my_place()
    cube = [
        swap_four([vec_ref[base + at : base + at + 1, lanes(part)] for part in range(4)], row, core)
        for at in range(RINGX)
    ]
    for part in range(4):
        put = (part & 1) * 2 + (part >> 1)
        for hops, value in enumerate(rotate_four([four[part] for four in cube], x)):
            out_ref[put : put + 1, lanes(hops)] = value


def from_own_order(own_ref, vec_ref, base):
    x, row, core = my_place()
    cube = []
    for hops in range(RINGX):
        got = [(at & 1) * 2 + (at >> 1) for at in range(4)]
        cube.append(swap_four([own_ref[at : at + 1, lanes(hops)] for at in got], row, core))
    for part in range(4):
        for at, value in enumerate(rotate_four([four[part] for four in cube], 4 - x)):
            vec_ref[base + at : base + at + 1, lanes(part)] = value


def final_kernel(heads, hidden, spread, *refs):
    if spread:
        rows = refs[0].shape[0] // 2
        parts = [ref.at[pl.ds(at * rows, rows)] for ref in refs[:2] for at in range(2)]
        outs = list(refs[2:])
    else:
        parts, outs = refs[:4], list(refs[4:])
    _, row, core = my_place()
    base = 0
    if heads:
        qkv_ref, out_ref = outs[:2]
        outs = outs[2:]
        for at_part, part in enumerate(parts):
            piece = (row ^ (at_part & 1)) * 2 * BLK + (core ^ (at_part >> 1)) * BLK
            for at in range(3):
                qkv_ref[rows_at(at * WIDE + piece)] = part[at * BLK : (at + 1) * BLK]
            out_ref[rows_at(piece)] = part[3 * BLK : 4 * BLK]
        base = 4 * BLK
    if hidden:
        for member in range(2):
            for at_part, part in enumerate(parts):
                start = base + member * WIDE
                outs[member][at_part * WIDE : (at_part + 1) * WIDE] = part[start : start + WIDE]
        base += 2 * WIDE
        outs = outs[2:]
    if spread:
        total = full(parts[0][base : base + VPAD])
        for part in parts[1:]:
            total = total + full(part[base : base + VPAD])
        outs[0][...] = total
        for layer_at in range(LAYERS):
            base = layer_at * (VROWS // LAYERS) + 8
            to_own_order(outs[0], base, outs[1 + layer_at])


def from_x(part):
    return [part] + [along_x(part, -hops) for hops in (1, 2, 3)]


HOLD_HEADS = pltpu.VMEM((4, 2 * BLK, WIDE), jnp.bfloat16)


def all_four(own):
    beside = other_row(own)
    return [own, beside, other_core(own), other_core(beside)]


def whole(parts, heads, hidden, spread, name):
    outs = []
    if heads:
        outs += [(3 * WIDE, jnp.bfloat16), (WIDE, jnp.bfloat16)]
    if hidden:
        outs += [(FF, jnp.bfloat16)] * 2
    if spread:
        outs += [(VPAD, jnp.float32)] + [(4, jnp.float32)] * LAYERS
    return far_call(
        lambda *refs: final_kernel(heads, hidden, spread, *refs), outs, parts, name=name + "_whole"
    )


def put_vec(ref, start, value):
    ref[start : start + VPAD] = half(value)


def get_vec(ref, start):
    return full(ref[start : start + VPAD])


def split_heads(grads, keep_ref, sent_ref):
    _, _, core = my_place()
    put = 0
    for row in range(2):
        for at in range(4):
            start = at * WIDE + row * 2 * BLK
            keep_ref[put : put + BLK] = grads[rows_at(start + core * BLK)]
            sent_ref[put : put + BLK] = grads[rows_at(start + (1 - core) * BLK)]
            put += BLK


def split_row_kernel(heads, hidden, spread, *refs):
    had_ref, came_ref = refs[:2]
    keep_ref, sent_ref = refs[2 + spread : 4 + spread]
    _, row, _ = my_place()

    def total(start):
        at = rows_at(start, WIDE)
        return full(had_ref[at]) + full(came_ref[at])

    put, base = 0, 0
    if heads:
        keep_ref[:WIDE] = total(row * WIDE)
        sent_ref[:WIDE] = half(total((1 - row) * WIDE))
        put, base = WIDE, 2 * WIDE
    if hidden:
        for _ in range(2):
            keep_ref[put : put + WIDE] = total(base)
            sent_ref[put : put + WIDE] = half(total(base + WIDE))
            put, base = put + WIDE, base + 2 * WIDE
    if spread:
        value = refs[2][...] + get_vec(came_ref, base)
        refs[-1][...] = value
        put_vec(sent_ref, put, value)


def split_x_kernel(heads, hidden, spread, *refs):
    had_ref, came_ref = refs[:2]
    keep_ref, *sent_refs = refs[2 + spread : 6 + spread]
    hold = refs[-1]
    x, _, _ = my_place()
    count = had_ref.shape[0]
    hold[...] = had_ref[...] + full(came_ref[:count])
    for hops, target in enumerate([keep_ref] + sent_refs):
        kind = target.dtype
        put, base = 0, 0
        if heads:
            at = (x + hops) & 3
            piece = hold[rows_at(at * BLK)]
            target[:BLK] = jnp.where(at == 3, 0.0, piece).astype(kind)
            target[BLK : 2 * BLK] = hold[3 * BLK : 4 * BLK].astype(kind)
            put, base = 2 * BLK, WIDE
        if hidden:
            for _ in range(2):
                start = base + hops * BLK
                target[put : put + BLK] = hold[start : start + BLK].astype(kind)
                put, base = put + BLK, base + WIDE
        if spread and hops:
            value = refs[2][...] + get_vec(came_ref, base)
            refs[-2][...] = value
            put_vec(target, put, value)


def sum_x_kernel(heads, keep_ref, *refs):
    parts, out_ref = refs[:3], refs[3]
    x, _, _ = my_place()
    total = keep_ref[...]
    for part in parts:
        total = total + full(part[...])
    out_ref[...] = total
    if heads:
        out_ref[BLK : 2 * BLK] = jnp.where(x == 0, total[BLK : 2 * BLK], 0.0)


def scatter_row(keep, came, heads, hidden, spread, name, vec_sum=None):
    rows = 4 * BLK * heads + 8 * BLK * hidden
    return (far_call if heads and hidden else small_call)(
        lambda *refs: split_row_kernel(heads, hidden, spread, *refs),
        [(rows, jnp.float32), (rows + VPAD * spread, jnp.bfloat16)]
        + [(VPAD, jnp.float32)] * spread,
        [keep, came] + [vec_sum] * spread,
        name=name + "_split_row",
    )


def scatter_x(keep, came, heads, hidden, spread, name, vec_sum=None):
    rows = 2 * BLK * heads + 2 * BLK * hidden
    return small_call(
        lambda *refs: split_x_kernel(heads, hidden, spread, *refs),
        [(rows, jnp.float32)]
        + [(rows + VPAD * spread, jnp.bfloat16)] * 3
        + [(VPAD, jnp.float32)] * spread,
        [keep, came] + [vec_sum] * spread,
        scratch=[pltpu.VMEM(keep.shape, jnp.float32)],
        name=name + "_split_x",
    )


def spread_x(sent):
    return [along_x(part, hops + 1) for hops, part in enumerate(sent)]


def split_group_kernel(slot_ref, *refs):
    second_ref, third_ref, keep_ref, *parts = refs[:6]
    vec_ref, own_ref = refs[6], refs[7]
    sent_refs, vec_out, hold = refs[8:15], refs[15], refs[16]
    flip, z = my_group()
    x, _, _ = my_place()
    total = keep_ref[...]
    value = vec_ref[...]
    for part in parts:
        total = total + full(part[: 2 * BLK])
        value = value + get_vec(part, 2 * BLK)
    vec_out[...] = value
    hold[0] = total[:BLK]
    hold[1] = jnp.where(x == 0, total[BLK:], 0.0)
    for member in range(2):
        hold[2 + member] = second_ref[member * BLK : (member + 1) * BLK]
    for member in range(4):
        hold[4 + member] = third_ref[member * BLK : (member + 1) * BLK]
    for at, (turn, hops) in enumerate(STEPS):
        slot = (flip ^ turn) * RINGZ + ((z + hops) & 3)
        mat_index = jnp.int32(0)
        for member in range(1, MATS):
            mat_index = jnp.where(slot_ref[member] == slot, member, mat_index)
        if at == 0:
            own_ref[...] = hold[mat_index]
        else:
            sent_refs[at - 1][:BLK] = half(hold[mat_index])
            put_vec(sent_refs[at - 1], BLK, value)


def renew_kernel(own_ref, *refs):
    parts, (vec_ref, moment_ref) = refs[:7], refs[7:9]
    grad_ref, new_ref, low_ref, vec_out = refs[9:]
    total, value = own_ref[...], vec_ref[...]
    for part in parts:
        total = total + full(part[:BLK])
        value = value + get_vec(part, BLK)
    grad_ref[...] = total
    vec_out[...] = value
    renewed = momentum_keep * moment_ref[...] + total
    new_ref[...] = renewed
    low_ref[...] = half(renewed)


def parts_of(value):
    high = half(value)
    return high, half(value - full(high))


def as_left(value):
    high, low = parts_of(value)
    return jnp.concatenate([high, high, low], 1)


def as_right(value):
    high, low = parts_of(value)
    return jnp.concatenate([high, low, high], 0)


def product(left, right):
    return jnp.dot(left, right, preferred_element_type=jnp.float32)


def newton_kernel(slot_ref, *refs):
    parts, own_ref, weight_ref, out_ref = refs[:4], refs[4], refs[5], refs[6]
    size = WIDE
    gram = None
    for part in parts:
        piece = row_contract(part[...], part[...])
        gram = piece if gram is None else gram + piece
    diagonal = lax.broadcasted_iota(jnp.int32, (size, size), 0) == lax.broadcasted_iota(
        jnp.int32, (size, size), 1
    )
    trace = jnp.sum(jnp.where(diagonal, gram, 0.0), keepdims=True)
    inverse = 1.0 / (jnp.sqrt(trace) + ortho_eps)
    gram = gram * inverse * inverse
    total = None
    for iteration in range(NEWTON_STEPS):
        squared = product(as_left(gram), as_right(gram))
        step = jnp.where(diagonal, coef_a, 0.0) + coef_b * gram + coef_c * squared
        left = as_left(step)
        if iteration == 0:
            total = step
            gram = product(left, as_right(product(left, as_right(gram))))
        elif iteration < NEWTON_STEPS - 1:
            both = product(left, as_right(jnp.concatenate([gram, total], 1)))
            total = both[:, size:]
            gram = product(left, as_right(both[:, :size]))
        else:
            total = product(left, as_right(total))
    high, low = parts_of(total * inverse)
    own = own_ref[...]
    ortho = product(own, high) + product(own, low)
    group = lax.axis_index("group")
    widths = [3 * WIDE, WIDE, FF, FF] * LAYERS
    scale = jnp.float32(0.0)
    for member in range(MATS):
        rate = muon_rate * muon_shape * widths[member] ** 0.5
        scale = jnp.where(slot_ref[member] == group, jnp.float32(rate), scale)
    out_ref[...] = weight_ref[...] * (1.0 - muon_rate * muon_decay) - scale * ortho


def turned(part):
    return half(full(part).T)


def column(index):
    return slice(index * 128, (index + 1) * 128)


def row_of(vec_ref, layer_at, index):
    at = layer_at * (VROWS // LAYERS) + index
    return vec_ref[at : at + 1]


def attend_kernel(layer_at, need, flush, in_ref, qkv_w, out_w, vec_ref, mid_ref, qkv_ref, attn_ref, prob_ref):
    normed, _ = normalize(in_ref[...])
    normed_low = half(normed * row_of(vec_ref, layer_at, 0) + row_of(vec_ref, layer_at, 1))
    for third in range(3):
        rows = slice(third * WIDE, (third + 1) * WIDE)
        value = col_contract(normed_low, qkv_w[rows])
        if third != 1:
            value = value + row_of(vec_ref, layer_at, 2 if third == 0 else 3)
        qkv_ref[:, rows] = half(value)
    flush(1)
    for at in range(HEADS // 2):
        attend_pair(at, qkv_ref, attn_ref, prob_ref)
        flush(3, at)
    flush(2)
    need(0)
    mid_ref[...] = in_ref[...] + (
        col_contract(attn_ref[...], out_w[...]) + row_of(vec_ref, layer_at, 4)
    )


def attend_pair(at, qkv_ref, attn_ref, prob_ref):
    queries = qkv_ref[:, column(at)] * jnp.bfloat16(0.125)
    keys, values = qkv_ref[:, column(3 + at)], qkv_ref[:, column(6 + at)]
    lane = lax.broadcasted_iota(jnp.int32, keys.shape, 1)
    values_t = turned(values)
    sums = []
    for head in range(2):
        mine = half(jnp.where((lane >> 6) == head, 1.0, 0.0))
        scores = col_contract(keys * mine, queries)
        exponent = jnp.exp(scores - jnp.max(scores, 0, keepdims=True))
        probs = half(exponent * (1.0 / jnp.sum(exponent, 0, keepdims=True)))
        prob_ref[2 * at + head] = probs
        sums.append(product(values_t, probs))
    row = lax.broadcasted_iota(jnp.int32, sums[0].shape, 0)
    attn_ref[:, column(at)] = half(jnp.where(row < 64, sums[0], sums[1]).T)


def attend_back_kernel(layer_at, need, flush, up_ref, in_ref, qkv_ref, attn_ref, prob_ref, qkv_w, out_w, vec_ref, *refs):
    spread = len(refs) > 8
    others = refs[:5] if spread else ()
    grad_ref, keep_ref, sent_ref, total_ref, upstream_ref, back_ref, grads_ref, sum_ref = refs[-8:]
    sum_ref[...] = jnp.zeros_like(sum_ref)
    out_low = half(up_ref[...])
    grads_ref[3 * WIDE :] = half(row_contract(out_low, attn_ref[...]))
    upstream_ref[...] = half(product(out_low, out_w[...]))
    sum_ref[4:5] = jnp.sum(full(out_low), 0, keepdims=True)
    for at in range(HEADS // 2):
        need(at)
        attend_back_pair(at, qkv_ref, upstream_ref, prob_ref, back_ref)
    normed, inv_std = normalize(in_ref[...])
    gain = row_of(vec_ref, layer_at, 0)
    normed_low = half(normed * gain + row_of(vec_ref, layer_at, 1))
    back_normed = jnp.zeros(normed.shape, jnp.float32)
    for third in range(3):
        rows = slice(third * WIDE, (third + 1) * WIDE)
        piece = back_ref[:, rows]
        grads_ref[rows] = half(row_contract(piece, normed_low))
        back_normed = back_normed + product(piece, qkv_w[rows])
        if third != 1:
            put = 2 if third == 0 else 3
            sum_ref[put : put + 1] = jnp.sum(full(piece), 0, keepdims=True)
    sum_ref[0:1] = jnp.sum(back_normed * normed, 0, keepdims=True)
    sum_ref[1:2] = jnp.sum(back_normed, 0, keepdims=True)
    grad_ref[...] = up_ref[...] + norm_back(back_normed, normed, inv_std, gain)
    flush(0)
    split_heads(grads_ref, keep_ref, sent_ref)
    if not spread:
        total_ref[...] = sum_ref[...]
        return
    total_ref[VROWS:] = jnp.zeros((VPAD - VROWS, WIDE), jnp.float32)
    pieces = (sum_ref, *others)
    for layer in range(LAYERS):
        base = layer * (VROWS // LAYERS)
        one, two, three = pieces[3 * layer : 3 * layer + 3]
        total_ref[base : base + 5] = one[:5]
        total_ref[base + 5 : base + 8] = two[:3]
        from_own_order(three, total_ref, base + 8)
    put_vec(sent_ref, 2 * WIDE, total_ref[...])


def attend_back_pair(at, qkv_ref, upstream_ref, prob_ref, back_ref):
    queries, keys, values = (qkv_ref[:, column(3 * third + at)] for third in range(3))
    upstream = upstream_ref[:, column(at)]
    lane = lax.broadcasted_iota(jnp.int32, keys.shape, 1)
    keys_t = turned(keys)
    got = []
    for head in range(2):
        mine = half(jnp.where((lane >> 6) == head, 1.0, 0.0))
        probs_low = prob_ref[2 * at + head]
        probs = full(probs_low)
        prob_grad = col_contract(values * mine, upstream)
        inner = jnp.sum(prob_grad * probs, 0, keepdims=True)
        score_low = half(probs * (prob_grad - inner))
        got.append(
            (product(keys_t, score_low), product(score_low, queries), product(probs_low, upstream))
        )
    row = lax.broadcasted_iota(jnp.int32, got[0][0].shape, 0)
    back_ref[:, column(at)] = half(jnp.where(row < 64, got[0][0], got[1][0]).T * 0.125)
    back_ref[:, column(3 + at)] = half(jnp.where(lane < 64, got[0][1], got[1][1]) * 0.125)
    back_ref[:, column(6 + at)] = half(jnp.where(lane < 64, got[0][2], got[1][2]))


def hidden_kernel(layer_at, need, flush, mid_ref, up_w, down_w, vec_ref, bias_ref, out_ref, act_ref, slope_ref):
    normed, _ = normalize(mid_ref[...])
    hidden_low = half(normed * row_of(vec_ref, layer_at, 5) + row_of(vec_ref, layer_at, 6))
    total = mid_ref[...] + row_of(vec_ref, layer_at, 7)
    for chunk in range(4):
        need(chunk)
        rows = slice(chunk * WIDE, (chunk + 1) * WIDE)
        hidden = col_contract(hidden_low, up_w[rows]) + bias_ref[chunk : chunk + 1]
        share = 0.5 * (1.0 + lax.erf(hidden * half_root))
        active_low = half(hidden * share)
        act_ref[:, rows] = active_low
        slope_ref[:, rows] = share + hidden * jnp.exp(-0.5 * hidden * hidden) * density
        total = total + product(active_low, down_w[rows])
        flush(1, chunk)
        flush(2, chunk)
    out_ref[...] = total


def hidden_back_kernel(layer_at, need, flush, up_ref, mid_ref, act_ref, slope_ref, up_w, down_w, vec_ref, grad_ref, keep_ref, sent_ref, sum_ref, bias_ref):
    down_low = half(up_ref[...])
    normed, inv_std = normalize(mid_ref[...])
    gain = row_of(vec_ref, layer_at, 5)
    hidden_low = half(normed * gain + row_of(vec_ref, layer_at, 6))
    back_hidden = jnp.zeros(normed.shape, jnp.float32)
    sum_ref[...] = jnp.zeros_like(sum_ref)
    for chunk in range(4):
        need(chunk)
        rows = slice(chunk * WIDE, (chunk + 1) * WIDE)
        up_low = half(col_contract(down_low, down_w[rows]) * slope_ref[:, rows])
        target, turn_at = (keep_ref, sent_ref)[chunk // 2], chunk % 2
        for member, value in enumerate(
            (row_contract(up_low, hidden_low), row_contract(act_ref[:, rows], down_low))
        ):
            put = (2 * member + turn_at) * WIDE
            target[put : put + WIDE] = half(value)
            flush(1 + chunk // 2, 2 * member + turn_at)
        bias_ref[chunk : chunk + 1] = jnp.sum(full(up_low), 0, keepdims=True)
        back_hidden = back_hidden + product(up_low, up_w[rows])
    sum_ref[0:1] = jnp.sum(back_hidden * normed, 0, keepdims=True)
    sum_ref[1:2] = jnp.sum(back_hidden, 0, keepdims=True)
    sum_ref[2:3] = jnp.sum(full(down_low), 0, keepdims=True)
    grad_ref[...] = up_ref[...] + norm_back(back_hidden, normed, inv_std, gain)


def layer_one_kernel(layer_at, need, flush, in_ref, cot_ref, qkv_w, out_w, up_w, down_w, vec_ref, bias_ref, *refs):
    stream_ref, grad_ref, keep_ref, sent_ref, one_ref, two_ref, bias_sum_ref = refs[:7]
    mid_ref, qkv_ref, attn_ref, prob_ref, act_ref, slope_ref, mid_grad_ref, *rest = refs[7:]
    heads, hidden = pl.ds(0, 2 * WIDE), pl.ds(2 * WIDE, 4 * WIDE)

    def nothing(*_):
        pass

    attend_kernel(
        layer_at, need, nothing, in_ref, qkv_w, out_w, vec_ref, mid_ref, qkv_ref, attn_ref, prob_ref
    )
    hidden_kernel(
        layer_at,
        nothing,
        nothing,
        mid_ref,
        up_w,
        down_w,
        vec_ref,
        bias_ref,
        stream_ref,
        act_ref,
        slope_ref,
    )
    flush(0)
    hidden_back_kernel(
        layer_at,
        nothing,
        nothing,
        cot_ref,
        mid_ref,
        act_ref,
        slope_ref,
        up_w,
        down_w,
        vec_ref,
        mid_grad_ref,
        keep_ref.at[hidden],
        sent_ref.at[hidden],
        two_ref,
        bias_sum_ref,
    )
    for piece in (1, 2):
        flush(2, piece)
        flush(3, piece)
    attend_back_kernel(
        layer_at,
        nothing,
        nothing,
        mid_grad_ref,
        in_ref,
        qkv_ref,
        attn_ref,
        prob_ref,
        qkv_w,
        out_w,
        vec_ref,
        grad_ref,
        keep_ref.at[heads],
        sent_ref.at[heads],
        one_ref,
        *rest,
    )


def cut_piece(ref, how, at):
    if how is None:
        return ref
    dimension, pieces = how
    size = ref.shape[dimension] // pieces
    return ref.at[(slice(None),) * dimension + (pl.ds(at * size, size),)]


def layer_call(kernel, layer_at, ins, outs, in_cut, out_cut, scratch=(), name=None):
    count, total = len(ins), len(outs)
    pieces = max([how[1] for how in in_cut.values()] + [1])
    in_plan = [(at, None, 0) for at in range(count) if at not in in_cut]
    in_plan += [(at, in_cut[at], piece) for piece in range(pieces) for at in sorted(in_cut)]
    out_plan = []
    for at in range(total):
        how = out_cut.get(at)
        out_plan += [(at, how, piece) for piece in range(how[1] if how else 1)]

    def body(*refs):
        far, near = refs[: count + total], refs[count + total : 2 * (count + total)]
        come_sems, leave_sems = refs[2 * (count + total) : 2 * (count + total) + 2]
        rest = refs[2 * (count + total) + 2 :]
        come = [
            pltpu.make_async_copy(
                cut_piece(far[at], how, piece), cut_piece(near[at], how, piece), come_sems.at[index]
            )
            for index, (at, how, piece) in enumerate(in_plan)
        ]
        leave = [
            pltpu.make_async_copy(
                cut_piece(near[count + at], how, piece),
                cut_piece(far[count + at], how, piece),
                leave_sems.at[index],
            )
            for index, (at, how, piece) in enumerate(out_plan)
        ]
        started = []

        def need(wanted):
            for (_, how, piece), copy in zip(in_plan, come):
                if (how is None and wanted is None) or (how is not None and piece == wanted):
                    copy.wait()

        def flush(out_at, wanted=0):
            index = [(at, piece) for at, _, piece in out_plan].index((out_at, wanted))
            leave[index].start()
            started.append(index)

        for copy in come:
            copy.start()
        need(None)
        kernel(layer_at, need, flush, *near, *rest)
        for index, copy in enumerate(leave):
            if index not in started:
                copy.start()
        for copy in leave:
            copy.wait()

    return pl.pallas_call(
        body,
        out_shape=[jax.ShapeDtypeStruct(shape, kind) for shape, kind in outs],
        in_specs=[far_spec()] * count,
        out_specs=[far_spec()] * total,
        scratch_shapes=[pltpu.VMEM(part.shape, part.dtype) for part in ins]
        + [pltpu.VMEM(shape, kind) for shape, kind in outs]
        + [pltpu.SemaphoreType.DMA((len(in_plan),)), pltpu.SemaphoreType.DMA((len(out_plan),))]
        + list(scratch),
        compiler_params=pltpu.CompilerParams(vmem_limit_bytes=64 << 20),
        cost_estimate=pl.CostEstimate(flops=1 << 20, bytes_accessed=1 << 16, transcendentals=0),
        name=name,
    )(*ins)


def attention_forward(layer_at, inputs, w_qkv, w_out, vec_full):
    length = inputs.shape[0]
    return layer_call(
        attend_kernel,
        layer_at,
        [inputs, w_qkv, w_out, vec_full],
        [
            (inputs.shape, jnp.float32),
            ((length, 3 * WIDE), jnp.bfloat16),
            (inputs.shape, jnp.bfloat16),
            ((HEADS, length, length), jnp.bfloat16),
        ],
        {2: (0, 1)},
        {3: (0, HEADS // 2)},
        name="attend",
    )


def back_scratch(length):
    return [
        pltpu.VMEM((length, WIDE), jnp.bfloat16),
        pltpu.VMEM((length, 3 * WIDE), jnp.bfloat16),
        pltpu.VMEM((4 * WIDE, WIDE), jnp.bfloat16),
        pltpu.VMEM((8, WIDE), jnp.float32),
    ]


def attention_backward(layer_at, upstream, inputs, stored, w_qkv, w_out, vec_full, others):
    qkv_low, attn_low, probs = stored
    return layer_call(
        attend_back_kernel,
        layer_at,
        [upstream, inputs, qkv_low, attn_low, probs, w_qkv, w_out, vec_full, *others],
        [
            (inputs.shape, jnp.float32),
            ((2 * WIDE, WIDE), jnp.bfloat16),
            ((2 * WIDE + VPAD, WIDE), jnp.bfloat16),
            ((VPAD, WIDE), jnp.float32),
        ],
        {4: (0, HEADS // 2)},
        {},
        scratch=back_scratch(inputs.shape[0]),
        name="attend_back",
    )


def layer_one(inputs, cotangent, w_qkv, w_out, w_up, w_down, vec_full, bias_up):
    length = inputs.shape[0]
    return layer_call(
        layer_one_kernel,
        1,
        [inputs, cotangent, w_qkv, w_out, w_up, w_down, vec_full, bias_up],
        [
            (inputs.shape, jnp.float32),
            (inputs.shape, jnp.float32),
            ((6 * WIDE, WIDE), jnp.bfloat16),
            ((6 * WIDE, WIDE), jnp.bfloat16),
            ((8, WIDE), jnp.float32),
            ((8, WIDE), jnp.float32),
            ((4, WIDE), jnp.float32),
        ],
        {1: (0, 1), 3: (0, 1), 4: (0, 1), 5: (0, 1)},
        {2: (0, 3), 3: (0, 3)},
        scratch=[
            pltpu.VMEM(inputs.shape, jnp.float32),
            pltpu.VMEM((length, 3 * WIDE), jnp.bfloat16),
            pltpu.VMEM(inputs.shape, jnp.bfloat16),
            pltpu.VMEM((HEADS, length, length), jnp.bfloat16),
            pltpu.VMEM((length, FF), jnp.bfloat16),
            pltpu.VMEM((length, FF), jnp.float32),
            pltpu.VMEM(inputs.shape, jnp.float32),
            *back_scratch(length),
        ],
        name="layer_one",
    )


def hidden_forward(layer_at, middle, w_up, w_down, vec_full, bias_up):
    wide = (middle.shape[0], FF)
    return layer_call(
        hidden_kernel,
        layer_at,
        [middle, w_up, w_down, vec_full, bias_up],
        [(middle.shape, jnp.float32), (wide, jnp.bfloat16), (wide, jnp.float32)],
        {1: (0, 4), 2: (0, 4)},
        {1: (1, 4), 2: (1, 4)},
        name="hidden",
    )


def hidden_backward(layer_at, upstream, middle, stored, w_up, w_down, vec_full):
    return layer_call(
        hidden_back_kernel,
        layer_at,
        [upstream, middle, *stored, w_up, w_down, vec_full],
        [
            (middle.shape, jnp.float32),
            (w_up.shape, jnp.bfloat16),
            (w_up.shape, jnp.bfloat16),
            ((8, WIDE), jnp.float32),
            ((4, WIDE), jnp.float32),
        ],
        {2: (1, 4), 3: (1, 4), 4: (0, 4), 5: (0, 4)},
        {1: (0, 4), 2: (0, 4)},
        name="hidden_back",
    )


def on_device(tokens, cotangent, live, slot_of, weights, momentum, vec, vec_first, vec_second):
    group_at = lax.axis_index("group")
    data_at = lax.axis_index("dp")
    vec_here, vec_cols = vec.shape
    per_layer = VROWS // LAYERS
    tie = lax.optimization_barrier
    spread = lax.dynamic_update_slice(
        jnp.zeros((VPAD, WIDE), jnp.bfloat16),
        half(vec),
        (group_at * vec_here, data_at * vec_cols),
    )
    own_block = jnp.concatenate([half(weights[0].T), spread], 0)
    pair = jnp.concatenate([own_block, along_group(own_block, 1, 0)], 0)
    slots = [pair] + [along_group(pair, 0, -hops) for hops in (1, 2, 3)]
    first, third = small_call(
        choose_kernel,
        [(4 * BLK + VPAD, jnp.bfloat16), (4 * BLK, jnp.bfloat16)],
        [slot_of] + slots,
        slot_first=True,
        scratch=[pltpu.VMEM((MATS, BLK, WIDE), jnp.bfloat16)],
        name="choose",
    )
    first_x, second_x = small_call(
        merge_first_kernel,
        [(4 * BLK + VPAD, jnp.bfloat16), (8 * BLK, jnp.bfloat16)],
        from_x(first),
        scratch=[HOLD_HEADS],
        name="first_merge_x",
    )
    second_x, third, first_x = tie((second_x, third, first_x))
    beside_first = other_row(first_x)
    pair_first = jnp.concatenate([first_x, beside_first], 0)
    first_parts = [pair_first, other_core(pair_first)]
    beside_second, core_second = other_row(second_x), other_core(second_x)
    third_parts = from_x(third)
    w_qkv0, w_out0, vec_full, bias0, bias1 = whole(first_parts, True, False, True, "first")
    inputs0 = tokens[0]
    middle0, *attn0 = attention_forward(0, inputs0, w_qkv0, w_out0, vec_full)
    third_parts, beside_second, middle0 = tie((third_parts, beside_second, middle0))
    (third_x,) = small_call(
        merge_third_kernel,
        [(12 * BLK, jnp.bfloat16)],
        third_parts,
        scratch=[HOLD_HEADS],
        name="third_merge_x",
    )
    beside = other_row(third_x)
    core_third = other_core(third_x)
    second_parts = [second_x, beside_second, core_second, other_core(beside_second)]
    w_up0, w_down0 = whole(second_parts, False, True, False, "second")
    inputs1, *mlp0 = hidden_forward(0, middle0, w_up0, w_down0, vec_full, bias0)
    beside, inputs1 = tie((beside, inputs1))
    third_parts = [third_x, beside, core_third, other_core(beside)]
    w_qkv1, w_out1, w_up1, w_down1 = whole(third_parts, True, True, False, "third")
    upstream = cotangent[0] * full(live)[0]
    stream, upstream, keep, sent, sums_one1, sums_two1, sums_up1 = layer_one(
        inputs1, upstream, w_qkv1, w_out1, w_up1, w_down1, vec_full, bias1
    )
    came = other_core(sent)
    mid_grad, keep_f, sent_f, sums_two0, sums_up0 = hidden_backward(
        0, upstream, middle0, mlp0, w_up0, w_down0, vec_full
    )
    came_f = other_core(sent_f)
    vec_full, came = tie((vec_full, came))
    keep, sent = scatter_row(keep, came, True, True, False, "third")
    vec_full, sent = tie((vec_full, sent))
    came = other_row(sent)
    token_grad, keep_h, sent_h, vec_sum = attention_backward(
        0,
        mid_grad,
        inputs0,
        attn0,
        w_qkv0,
        w_out0,
        vec_full,
        (sums_two0, sums_up0, sums_one1, sums_two1, sums_up1),
    )
    vec_sum, came_f = tie((vec_sum, came_f))
    keep_f, sent_f = scatter_row(keep_f, came_f, False, True, False, "second")
    sent_h, sent_f, came = tie((sent_h, sent_f, came))
    came_f = other_row(sent_f)
    came_h = other_core(sent_h)
    keep, *sent_x = scatter_x(keep, came, True, True, False, "third")
    came_x = spread_x(sent_x)
    came_f, came_x = tie((came_f, came_x))
    keep_h, sent_h, vec_sum = scatter_row(keep_h, came_h, True, False, True, "first", vec_sum)
    came_h = other_row(sent_h)
    keep_f, *sent_f = scatter_x(keep_f, came_f, False, True, False, "second")
    (third_sum,) = small_call(
        lambda *refs: sum_x_kernel(True, *refs),
        [(4 * BLK, jnp.float32)],
        [keep] + came_x,
        name="third_sum_x",
    )
    came_f = spread_x(sent_f)
    (second_sum,) = small_call(
        lambda *refs: sum_x_kernel(False, *refs),
        [(2 * BLK, jnp.float32)],
        [keep_f] + came_f,
        name="second_sum_x",
    )
    keep_h, *sent_h, vec_sum = scatter_x(keep_h, came_h, True, False, True, "first", vec_sum)
    came_h = spread_x(sent_h)
    own, *sent_g, vec_sum = small_call(
        split_group_kernel,
        [(BLK, jnp.float32)]
        + [(BLK + VPAD, jnp.bfloat16)] * 7
        + [(VPAD, jnp.float32)],
        [slot_of, second_sum, third_sum, keep_h] + came_h + [vec_sum],
        slot_first=True,
        scratch=[pltpu.VMEM((MATS, BLK, WIDE), jnp.float32)],
        name="split_group",
    )
    came_g = [along_group(part, flip, hops) for part, (flip, hops) in zip(sent_g, STEPS[1:])]
    grad_rows, moment_rows, moment_low, vec_sum = small_call(
        renew_kernel,
        [(BLK, jnp.float32), (BLK, jnp.float32), (BLK, jnp.bfloat16), (VPAD, jnp.float32)],
        [own] + came_g + [vec_sum, momentum[0].T],
        name="renew",
    )
    ring = jnp.concatenate([moment_low] + [along_x(moment_low, -hops) for hops in (1, 2, 3)], 0)
    beside = other_row(ring)
    (weight_rows,) = small_call(
        newton_kernel,
        [(BLK, jnp.float32)],
        [slot_of, ring, beside, other_core(ring), other_core(beside), moment_low, weights[0].T],
        slot_first=True,
        name="newton",
    )
    shard_vec = lax.dynamic_slice(
        vec_sum, (group_at * vec_here, data_at * vec_cols), (vec_here, vec_cols)
    )
    first_new = first_keep * vec_first + (1.0 - first_keep) * shard_vec
    second_new = second_keep * vec_second + (1.0 - second_keep) * shard_vec * shard_vec
    vec_new = vec - adam_rate * (
        first_new
        / (1.0 - first_keep**STEP)
        / (jnp.sqrt(second_new / (1.0 - second_keep**STEP)) + adam_eps)
    )
    return (
        stream[None],
        token_grad[None],
        grad_rows.T[None],
        moment_rows.T[None],
        weight_rows.T[None],
        first_new,
        second_new,
        vec_new,
    )


def solution(mesh):
    placed = (
        P(("group", "dp"), None, None),
        P(("group", "dp"), None, None),
        P(("group", "dp")),
        P(),
        P("group", None, "dp"),
        P("group", None, "dp"),
        P("group", "dp"),
        P("group", "dp"),
        P("group", "dp"),
    )
    return jax.shard_map(
        on_device,
        mesh=mesh,
        in_specs=placed,
        out_specs=(
            P(("group", "dp"), None, None),
            P(("group", "dp"), None, None),
            P("group", None, "dp"),
            P("group", None, "dp"),
            P("group", None, "dp"),
            P("group", "dp"),
            P("group", "dp"),
            P("group", "dp"),
        ),
        check_vma=False,
    )
```

```python
import jax
import jax.numpy as jnp
from jax import lax
from jax.experimental import pallas as pl
from jax.experimental.pallas import tpu as pltpu
from jax.sharding import PartitionSpec as P

HEADS = 6
FF = 1536
LAYERS = 2
NEWTON_STEPS = 5
STEP = 10
MATS = 8
VROWS = 24


norm_eps = 1e-06
ortho_eps = 1e-07
coef_a = 3.4445
coef_b = -4.775
coef_c = 2.0315
momentum_keep = 0.95
muon_rate = 0.25
muon_decay = 0.01
muon_shape = 0.5
adam_rate = 0.4
first_keep = 0.9
second_keep = 0.999
adam_eps = 1e-08
half_root = 0.7071067811865476
density = 0.3989422804014327


def normalize(values):
    center = values - jnp.mean(values, -1, keepdims=True)
    inv_std = lax.rsqrt(jnp.mean(center * center, -1, keepdims=True) + norm_eps)
    return (center * inv_std, inv_std)


def norm_back(upstream, normed, inv_std, gain):
    scaled = upstream * gain
    return inv_std * (
        scaled
        - jnp.mean(scaled, -1, keepdims=True)
        - normed * jnp.mean(scaled * normed, -1, keepdims=True)
    )


def gelu_slope(values):
    return (
        0.5 * (1.0 + lax.erf(values * half_root))
        + values * jnp.exp(-0.5 * values * values) * density
    )


def row_contract(left_op, right_op):
    return lax.dot_general(
        left_op, right_op, (((0,), (0,)), ((), ())), preferred_element_type=jnp.float32
    )


def col_contract(left_op, right_op):
    return lax.dot_general(
        left_op, right_op, (((1,), (1,)), ((), ())), preferred_element_type=jnp.float32
    )


BLK = 96
WIDE = 384
VPAD = 32
RINGX = 4
RINGZ = 4
STEPS = [(flip, hops) for flip in range(2) for hops in range(RINGZ)]


def half(part):
    return part.astype(jnp.bfloat16)


def full(part):
    return part.astype(jnp.float32)


def near(part, change):
    return lax.ppermute(part, "dp", [(at, change(at)) for at in range(16)])


def other_core(part):
    return near(part, lambda at: at ^ 1)


def other_row(part):
    return near(part, lambda at: at ^ 2)


def along_x(part, hops):
    return near(part, lambda at: (at + 4 * hops) % 16)


def along_group(part, flip, hops):
    pairs = [(at, (at ^ (4 * flip)) // 4 * 4 + (at + hops) % RINGZ) for at in range(8)]
    return lax.ppermute(part, "group", pairs)


def my_place():
    spot = lax.axis_index("dp")
    return spot >> 2, (spot >> 1) & 1, spot & 1


def my_group():
    group = lax.axis_index("group")
    return group >> 2, group & 3


def rows_at(start, count=BLK):
    return pl.ds(pl.multiple_of(start, 32), count)


def small_call(kernel, outs, ins, slot_first=False, scratch=(), name=None, vmem=12):
    specs = [pl.BlockSpec(memory_space=pltpu.VMEM)] * len(ins)
    if slot_first:
        specs[0] = pl.BlockSpec(memory_space=pltpu.SMEM)
    return pl.pallas_call(
        kernel,
        out_shape=[jax.ShapeDtypeStruct((rows, WIDE), kind) for rows, kind in outs],
        in_specs=specs,
        out_specs=[pl.BlockSpec(memory_space=pltpu.VMEM)] * len(outs),
        scratch_shapes=list(scratch),
        compiler_params=pltpu.CompilerParams(vmem_limit_bytes=vmem << 20),
        name=name,
    )(*ins)


def far_spec():
    return pl.BlockSpec(memory_space=pltpu.HBM)


def far_call(kernel, outs, ins, slot_first=False, scratch=(), name=None, vmem=64):
    lead, count, total = int(slot_first), len(ins) - int(slot_first), len(outs)

    def body(*refs):
        far, near = refs[lead : lead + count + total], refs[lead + count + total :]
        sems, rest = near[count + total], near[count + total + 1 :]
        come = [
            pltpu.make_async_copy(far[at], near[at], sems.at[at]) for at in range(count)
        ]
        for copy in come:
            copy.start()
        for copy in come:
            copy.wait()
        kernel(*refs[:lead], *near[: count + total], *rest)
        leave = [
            pltpu.make_async_copy(near[at], far[at], sems.at[at])
            for at in range(count, count + total)
        ]
        for copy in leave:
            copy.start()
        for copy in leave:
            copy.wait()

    return pl.pallas_call(
        body,
        out_shape=[jax.ShapeDtypeStruct((rows, WIDE), kind) for rows, kind in outs],
        in_specs=[pl.BlockSpec(memory_space=pltpu.SMEM)] * lead + [far_spec()] * count,
        out_specs=[far_spec()] * total,
        scratch_shapes=[pltpu.VMEM(part.shape, part.dtype) for part in ins[lead:]]
        + [pltpu.VMEM((rows, WIDE), kind) for rows, kind in outs]
        + [pltpu.SemaphoreType.DMA((count + total,))]
        + list(scratch),
        compiler_params=pltpu.CompilerParams(vmem_limit_bytes=vmem << 20),
        cost_estimate=pl.CostEstimate(flops=1 << 20, bytes_accessed=1 << 16, transcendentals=0),
        name=name,
    )(*ins)


def choose_kernel(slot_ref, *refs):
    pairs, (first_ref, third_ref), hold = refs[:4], refs[4:6], refs[6]
    flip, z = my_group()
    spread = None
    for turn, hops in STEPS:
        base = turn * (BLK + VPAD)
        hold[turn * RINGZ + hops] = pairs[hops][base : base + BLK]
        piece = full(pairs[hops][base + BLK : base + BLK + VPAD])
        spread = piece if spread is None else spread + piece

    def matrix(mat_index):
        slot = slot_ref[mat_index]
        return hold[((slot >> 2) ^ flip) * RINGZ + ((slot - z) & 3)]

    first_ref[4 * BLK :] = half(spread)
    for member in range(4):
        first_ref[member * BLK : (member + 1) * BLK] = matrix(member)
        third_ref[member * BLK : (member + 1) * BLK] = matrix(4 + member)


def merge_first_kernel(*refs):
    parts, head_ref, hidden_ref, hold = refs[:4], refs[4], refs[5], refs[6]
    merge_heads(parts, head_ref, hold)
    merge_hidden(parts, hidden_ref, 0)
    total = full(parts[0][4 * BLK :])
    for at in range(1, 4):
        total = total + full(parts[at][4 * BLK :])
    head_ref[4 * BLK :] = half(total)


def merge_third_kernel(*refs):
    parts, out_ref, hold = refs[:4], refs[4], refs[5]
    merge_heads(parts, out_ref, hold)
    merge_hidden(parts, out_ref, 4 * BLK)


def merge_heads(parts, out_ref, hold):
    x, _, _ = my_place()
    for at in range(4):
        hold[at] = parts[at][: 2 * BLK]
    for at in range(3):
        out_ref[at * BLK : (at + 1) * BLK] = hold[(at - x) & 3, :BLK]
    out_ref[3 * BLK : 4 * BLK] = hold[(0 - x) & 3, BLK:]


def merge_hidden(parts, out_ref, put):
    for member in (2, 3):
        for part in parts:
            out_ref[put : put + BLK] = part[member * BLK : (member + 1) * BLK]
            put += BLK


def swap_four(parts, row, core):
    parts = [jnp.where(core == 0, parts[at], parts[at ^ 1]) for at in range(4)]
    return [jnp.where(row == 0, parts[at], parts[at ^ 2]) for at in range(4)]


def lanes(block):
    return slice(block * BLK, (block + 1) * BLK)


def rotate_four(parts, count):
    parts = [jnp.where((count & 1) == 0, parts[at], parts[(at + 1) & 3]) for at in range(4)]
    return [jnp.where((count & 2) == 0, parts[at], parts[(at + 2) & 3]) for at in range(4)]


def to_own_order(vec_ref, base, out_ref):
    x, row, core = my_place()
    cube = [
        swap_four([vec_ref[base + at : base + at + 1, lanes(part)] for part in range(4)], row, core)
        for at in range(RINGX)
    ]
    for part in range(4):
        put = (part & 1) * 2 + (part >> 1)
        for hops, value in enumerate(rotate_four([four[part] for four in cube], x)):
            out_ref[put : put + 1, lanes(hops)] = value


def from_own_order(own_ref, vec_ref, base):
    x, row, core = my_place()
    cube = []
    for hops in range(RINGX):
        got = [(at & 1) * 2 + (at >> 1) for at in range(4)]
        cube.append(swap_four([own_ref[at : at + 1, lanes(hops)] for at in got], row, core))
    for part in range(4):
        for at, value in enumerate(rotate_four([four[part] for four in cube], 4 - x)):
            vec_ref[base + at : base + at + 1, lanes(part)] = value


def final_kernel(heads, hidden, spread, *refs):
    if spread:
        rows = refs[0].shape[0] // 2
        parts = [ref.at[pl.ds(at * rows, rows)] for ref in refs[:2] for at in range(2)]
        outs = list(refs[2:])
    else:
        parts, outs = refs[:4], list(refs[4:])
    _, row, core = my_place()
    base = 0
    if heads:
        qkv_ref, out_ref = outs[:2]
        outs = outs[2:]
        for at_part, part in enumerate(parts):
            piece = (row ^ (at_part & 1)) * 2 * BLK + (core ^ (at_part >> 1)) * BLK
            for at in range(3):
                qkv_ref[rows_at(at * WIDE + piece)] = part[at * BLK : (at + 1) * BLK]
            out_ref[rows_at(piece)] = part[3 * BLK : 4 * BLK]
        base = 4 * BLK
    if hidden:
        for member in range(2):
            for at_part, part in enumerate(parts):
                start = base + member * WIDE
                outs[member][at_part * WIDE : (at_part + 1) * WIDE] = part[start : start + WIDE]
        base += 2 * WIDE
        outs = outs[2:]
    if spread:
        total = full(parts[0][base : base + VPAD])
        for part in parts[1:]:
            total = total + full(part[base : base + VPAD])
        outs[0][...] = total
        for layer_at in range(LAYERS):
            base = layer_at * (VROWS // LAYERS) + 8
            to_own_order(outs[0], base, outs[1 + layer_at])


def from_x(part):
    return [part] + [along_x(part, -hops) for hops in (1, 2, 3)]


HOLD_HEADS = pltpu.VMEM((4, 2 * BLK, WIDE), jnp.bfloat16)


def all_four(own):
    beside = other_row(own)
    return [own, beside, other_core(own), other_core(beside)]


def whole(parts, heads, hidden, spread, name):
    outs = []
    if heads:
        outs += [(3 * WIDE, jnp.bfloat16), (WIDE, jnp.bfloat16)]
    if hidden:
        outs += [(FF, jnp.bfloat16)] * 2
    if spread:
        outs += [(VPAD, jnp.float32)] + [(4, jnp.float32)] * LAYERS
    return far_call(
        lambda *refs: final_kernel(heads, hidden, spread, *refs), outs, parts, name=name + "_whole"
    )


def put_vec(ref, start, value):
    ref[start : start + VPAD] = half(value)


def get_vec(ref, start):
    return full(ref[start : start + VPAD])


def split_heads(grads, keep_ref, sent_ref):
    _, _, core = my_place()
    put = 0
    for row in range(2):
        for at in range(4):
            start = at * WIDE + row * 2 * BLK
            keep_ref[put : put + BLK] = grads[rows_at(start + core * BLK)]
            sent_ref[put : put + BLK] = grads[rows_at(start + (1 - core) * BLK)]
            put += BLK


def split_row_kernel(heads, hidden, spread, *refs):
    had_ref, came_ref = refs[:2]
    keep_ref, sent_ref = refs[2 + spread : 4 + spread]
    _, row, _ = my_place()

    def total(start):
        at = rows_at(start, WIDE)
        return full(had_ref[at]) + full(came_ref[at])

    put, base = 0, 0
    if heads:
        keep_ref[:WIDE] = total(row * WIDE)
        sent_ref[:WIDE] = half(total((1 - row) * WIDE))
        put, base = WIDE, 2 * WIDE
    if hidden:
        for _ in range(2):
            keep_ref[put : put + WIDE] = total(base)
            sent_ref[put : put + WIDE] = half(total(base + WIDE))
            put, base = put + WIDE, base + 2 * WIDE
    if spread:
        value = refs[2][...] + get_vec(came_ref, base)
        refs[-1][...] = value
        put_vec(sent_ref, put, value)


def split_x_kernel(heads, hidden, spread, *refs):
    had_ref, came_ref = refs[:2]
    keep_ref, *sent_refs = refs[2 + spread : 6 + spread]
    hold = refs[-1]
    x, _, _ = my_place()
    count = had_ref.shape[0]
    hold[...] = had_ref[...] + full(came_ref[:count])
    for hops, target in enumerate([keep_ref] + sent_refs):
        kind = target.dtype
        put, base = 0, 0
        if heads:
            at = (x + hops) & 3
            piece = hold[rows_at(at * BLK)]
            target[:BLK] = jnp.where(at == 3, 0.0, piece).astype(kind)
            target[BLK : 2 * BLK] = hold[3 * BLK : 4 * BLK].astype(kind)
            put, base = 2 * BLK, WIDE
        if hidden:
            for _ in range(2):
                start = base + hops * BLK
                target[put : put + BLK] = hold[start : start + BLK].astype(kind)
                put, base = put + BLK, base + WIDE
        if spread and hops:
            value = refs[2][...] + get_vec(came_ref, base)
            refs[-2][...] = value
            put_vec(target, put, value)


def sum_x_kernel(heads, keep_ref, *refs):
    parts, out_ref = refs[:3], refs[3]
    x, _, _ = my_place()
    total = keep_ref[...]
    for part in parts:
        total = total + full(part[...])
    out_ref[...] = total
    if heads:
        out_ref[BLK : 2 * BLK] = jnp.where(x == 0, total[BLK : 2 * BLK], 0.0)


def scatter_row(keep, came, heads, hidden, spread, name, vec_sum=None):
    rows = 4 * BLK * heads + 8 * BLK * hidden
    return (far_call if heads and hidden else small_call)(
        lambda *refs: split_row_kernel(heads, hidden, spread, *refs),
        [(rows, jnp.float32), (rows + VPAD * spread, jnp.bfloat16)]
        + [(VPAD, jnp.float32)] * spread,
        [keep, came] + [vec_sum] * spread,
        name=name + "_split_row",
    )


def scatter_x(keep, came, heads, hidden, spread, name, vec_sum=None):
    rows = 2 * BLK * heads + 2 * BLK * hidden
    return small_call(
        lambda *refs: split_x_kernel(heads, hidden, spread, *refs),
        [(rows, jnp.float32)]
        + [(rows + VPAD * spread, jnp.bfloat16)] * 3
        + [(VPAD, jnp.float32)] * spread,
        [keep, came] + [vec_sum] * spread,
        scratch=[pltpu.VMEM(keep.shape, jnp.float32)],
        name=name + "_split_x",
    )


def spread_x(sent):
    return [along_x(part, hops + 1) for hops, part in enumerate(sent)]


def split_group_kernel(slot_ref, *refs):
    second_ref, third_ref, keep_ref, *parts = refs[:6]
    vec_ref, own_ref = refs[6], refs[7]
    sent_refs, vec_out, hold = refs[8:15], refs[15], refs[16]
    flip, z = my_group()
    x, _, _ = my_place()
    total = keep_ref[...]
    value = vec_ref[...]
    for part in parts:
        total = total + full(part[: 2 * BLK])
        value = value + get_vec(part, 2 * BLK)
    vec_out[...] = value
    hold[0] = total[:BLK]
    hold[1] = jnp.where(x == 0, total[BLK:], 0.0)
    for member in range(2):
        hold[2 + member] = second_ref[member * BLK : (member + 1) * BLK]
    for member in range(4):
        hold[4 + member] = third_ref[member * BLK : (member + 1) * BLK]
    for at, (turn, hops) in enumerate(STEPS):
        slot = (flip ^ turn) * RINGZ + ((z + hops) & 3)
        mat_index = jnp.int32(0)
        for member in range(1, MATS):
            mat_index = jnp.where(slot_ref[member] == slot, member, mat_index)
        if at == 0:
            own_ref[...] = hold[mat_index]
        else:
            sent_refs[at - 1][:BLK] = half(hold[mat_index])
            put_vec(sent_refs[at - 1], BLK, value)


def renew_kernel(own_ref, *refs):
    parts, (vec_ref, moment_ref) = refs[:7], refs[7:9]
    grad_ref, new_ref, low_ref, vec_out = refs[9:]
    total, value = own_ref[...], vec_ref[...]
    for part in parts:
        total = total + full(part[:BLK])
        value = value + get_vec(part, BLK)
    grad_ref[...] = total
    vec_out[...] = value
    renewed = momentum_keep * moment_ref[...] + total
    new_ref[...] = renewed
    low_ref[...] = half(renewed)


def parts_of(value):
    high = half(value)
    return high, half(value - full(high))


def as_left(value):
    high, low = parts_of(value)
    return jnp.concatenate([high, high, low], 1)


def as_right(value):
    high, low = parts_of(value)
    return jnp.concatenate([high, low, high], 0)


def product(left, right):
    return jnp.dot(left, right, preferred_element_type=jnp.float32)


def newton_kernel(slot_ref, *refs):
    parts, own_ref, weight_ref, out_ref = refs[:4], refs[4], refs[5], refs[6]
    size = WIDE
    gram = None
    for part in parts:
        piece = row_contract(part[...], part[...])
        gram = piece if gram is None else gram + piece
    diagonal = lax.broadcasted_iota(jnp.int32, (size, size), 0) == lax.broadcasted_iota(
        jnp.int32, (size, size), 1
    )
    trace = jnp.sum(jnp.where(diagonal, gram, 0.0), keepdims=True)
    inverse = 1.0 / (jnp.sqrt(trace) + ortho_eps)
    gram = gram * inverse * inverse
    total = None
    for iteration in range(NEWTON_STEPS):
        squared = product(as_left(gram), as_right(gram))
        step = jnp.where(diagonal, coef_a, 0.0) + coef_b * gram + coef_c * squared
        left = as_left(step)
        if iteration == 0:
            total = step
            gram = product(left, as_right(product(left, as_right(gram))))
        elif iteration < NEWTON_STEPS - 1:
            both = product(left, as_right(jnp.concatenate([gram, total], 1)))
            total = both[:, size:]
            gram = product(left, as_right(both[:, :size]))
        else:
            total = product(left, as_right(total))
    high, low = parts_of(total * inverse)
    own = own_ref[...]
    ortho = product(own, high) + product(own, low)
    group = lax.axis_index("group")
    widths = [3 * WIDE, WIDE, FF, FF] * LAYERS
    scale = jnp.float32(0.0)
    for member in range(MATS):
        rate = muon_rate * muon_shape * widths[member] ** 0.5
        scale = jnp.where(slot_ref[member] == group, jnp.float32(rate), scale)
    out_ref[...] = weight_ref[...] * (1.0 - muon_rate * muon_decay) - scale * ortho


def turned(part):
    return half(full(part).T)


def column(index):
    return slice(index * 128, (index + 1) * 128)


def row_of(vec_ref, layer_at, index):
    at = layer_at * (VROWS // LAYERS) + index
    return vec_ref[at : at + 1]


def attend_kernel(layer_at, need, flush, in_ref, qkv_w, out_w, vec_ref, mid_ref, qkv_ref, attn_ref, prob_ref):
    normed, _ = normalize(in_ref[...])
    normed_low = half(normed * row_of(vec_ref, layer_at, 0) + row_of(vec_ref, layer_at, 1))
    for third in range(3):
        rows = slice(third * WIDE, (third + 1) * WIDE)
        value = col_contract(normed_low, qkv_w[rows])
        if third != 1:
            value = value + row_of(vec_ref, layer_at, 2 if third == 0 else 3)
        qkv_ref[:, rows] = half(value)
    flush(1)
    for at in range(HEADS // 2):
        attend_pair(at, qkv_ref, attn_ref, prob_ref)
        flush(3, at)
    flush(2)
    need(0)
    mid_ref[...] = in_ref[...] + (
        col_contract(attn_ref[...], out_w[...]) + row_of(vec_ref, layer_at, 4)
    )


def attend_pair(at, qkv_ref, attn_ref, prob_ref):
    queries = qkv_ref[:, column(at)] * jnp.bfloat16(0.125)
    keys, values = qkv_ref[:, column(3 + at)], qkv_ref[:, column(6 + at)]
    lane = lax.broadcasted_iota(jnp.int32, keys.shape, 1)
    values_t = turned(values)
    sums = []
    for head in range(2):
        mine = half(jnp.where((lane >> 6) == head, 1.0, 0.0))
        scores = col_contract(keys * mine, queries)
        exponent = jnp.exp(scores - jnp.max(scores, 0, keepdims=True))
        probs = half(exponent * (1.0 / jnp.sum(exponent, 0, keepdims=True)))
        prob_ref[2 * at + head] = probs
        sums.append(product(values_t, probs))
    row = lax.broadcasted_iota(jnp.int32, sums[0].shape, 0)
    attn_ref[:, column(at)] = half(jnp.where(row < 64, sums[0], sums[1]).T)


def attend_back_kernel(layer_at, need, flush, up_ref, in_ref, qkv_ref, attn_ref, prob_ref, qkv_w, out_w, vec_ref, *refs):
    spread = len(refs) > 8
    others = refs[:5] if spread else ()
    grad_ref, keep_ref, sent_ref, total_ref, upstream_ref, back_ref, grads_ref, sum_ref = refs[-8:]
    sum_ref[...] = jnp.zeros_like(sum_ref)
    out_low = half(up_ref[...])
    grads_ref[3 * WIDE :] = half(row_contract(out_low, attn_ref[...]))
    upstream_ref[...] = half(product(out_low, out_w[...]))
    sum_ref[4:5] = jnp.sum(full(out_low), 0, keepdims=True)
    for at in range(HEADS // 2):
        need(at)
        attend_back_pair(at, qkv_ref, upstream_ref, prob_ref, back_ref)
    normed, inv_std = normalize(in_ref[...])
    gain = row_of(vec_ref, layer_at, 0)
    normed_low = half(normed * gain + row_of(vec_ref, layer_at, 1))
    back_normed = jnp.zeros(normed.shape, jnp.float32)
    for third in range(3):
        rows = slice(third * WIDE, (third + 1) * WIDE)
        piece = back_ref[:, rows]
        grads_ref[rows] = half(row_contract(piece, normed_low))
        back_normed = back_normed + product(piece, qkv_w[rows])
        if third != 1:
            put = 2 if third == 0 else 3
            sum_ref[put : put + 1] = jnp.sum(full(piece), 0, keepdims=True)
    sum_ref[0:1] = jnp.sum(back_normed * normed, 0, keepdims=True)
    sum_ref[1:2] = jnp.sum(back_normed, 0, keepdims=True)
    grad_ref[...] = up_ref[...] + norm_back(back_normed, normed, inv_std, gain)
    flush(0)
    split_heads(grads_ref, keep_ref, sent_ref)
    if not spread:
        total_ref[...] = sum_ref[...]
        return
    total_ref[VROWS:] = jnp.zeros((VPAD - VROWS, WIDE), jnp.float32)
    pieces = (sum_ref, *others)
    for layer in range(LAYERS):
        base = layer * (VROWS // LAYERS)
        one, two, three = pieces[3 * layer : 3 * layer + 3]
        total_ref[base : base + 5] = one[:5]
        total_ref[base + 5 : base + 8] = two[:3]
        from_own_order(three, total_ref, base + 8)
    put_vec(sent_ref, 2 * WIDE, total_ref[...])


def attend_back_pair(at, qkv_ref, upstream_ref, prob_ref, back_ref):
    queries, keys, values = (qkv_ref[:, column(3 * third + at)] for third in range(3))
    upstream = upstream_ref[:, column(at)]
    lane = lax.broadcasted_iota(jnp.int32, keys.shape, 1)
    keys_t = turned(keys)
    got = []
    for head in range(2):
        mine = half(jnp.where((lane >> 6) == head, 1.0, 0.0))
        probs_low = prob_ref[2 * at + head]
        probs = full(probs_low)
        prob_grad = col_contract(values * mine, upstream)
        inner = jnp.sum(prob_grad * probs, 0, keepdims=True)
        score_low = half(probs * (prob_grad - inner))
        got.append(
            (product(keys_t, score_low), product(score_low, queries), product(probs_low, upstream))
        )
    row = lax.broadcasted_iota(jnp.int32, got[0][0].shape, 0)
    back_ref[:, column(at)] = half(jnp.where(row < 64, got[0][0], got[1][0]).T * 0.125)
    back_ref[:, column(3 + at)] = half(jnp.where(lane < 64, got[0][1], got[1][1]) * 0.125)
    back_ref[:, column(6 + at)] = half(jnp.where(lane < 64, got[0][2], got[1][2]))


def hidden_kernel(layer_at, need, flush, mid_ref, up_w, down_w, vec_ref, bias_ref, out_ref, act_ref, slope_ref):
    normed, _ = normalize(mid_ref[...])
    hidden_low = half(normed * row_of(vec_ref, layer_at, 5) + row_of(vec_ref, layer_at, 6))
    total = mid_ref[...] + row_of(vec_ref, layer_at, 7)
    for chunk in range(4):
        need(chunk)
        rows = slice(chunk * WIDE, (chunk + 1) * WIDE)
        hidden = col_contract(hidden_low, up_w[rows]) + bias_ref[chunk : chunk + 1]
        share = 0.5 * (1.0 + lax.erf(hidden * half_root))
        active_low = half(hidden * share)
        act_ref[:, rows] = active_low
        slope_ref[:, rows] = share + hidden * jnp.exp(-0.5 * hidden * hidden) * density
        total = total + product(active_low, down_w[rows])
        flush(1, chunk)
        flush(2, chunk)
    out_ref[...] = total


def hidden_back_kernel(layer_at, need, flush, up_ref, mid_ref, act_ref, slope_ref, up_w, down_w, vec_ref, grad_ref, keep_ref, sent_ref, sum_ref, bias_ref):
    down_low = half(up_ref[...])
    normed, inv_std = normalize(mid_ref[...])
    gain = row_of(vec_ref, layer_at, 5)
    hidden_low = half(normed * gain + row_of(vec_ref, layer_at, 6))
    back_hidden = jnp.zeros(normed.shape, jnp.float32)
    sum_ref[...] = jnp.zeros_like(sum_ref)
    for chunk in range(4):
        need(chunk)
        rows = slice(chunk * WIDE, (chunk + 1) * WIDE)
        up_low = half(col_contract(down_low, down_w[rows]) * slope_ref[:, rows])
        target, turn_at = (keep_ref, sent_ref)[chunk // 2], chunk % 2
        for member, value in enumerate(
            (row_contract(up_low, hidden_low), row_contract(act_ref[:, rows], down_low))
        ):
            put = (2 * member + turn_at) * WIDE
            target[put : put + WIDE] = half(value)
            flush(1 + chunk // 2, 2 * member + turn_at)
        bias_ref[chunk : chunk + 1] = jnp.sum(full(up_low), 0, keepdims=True)
        back_hidden = back_hidden + product(up_low, up_w[rows])
    sum_ref[0:1] = jnp.sum(back_hidden * normed, 0, keepdims=True)
    sum_ref[1:2] = jnp.sum(back_hidden, 0, keepdims=True)
    sum_ref[2:3] = jnp.sum(full(down_low), 0, keepdims=True)
    grad_ref[...] = up_ref[...] + norm_back(back_hidden, normed, inv_std, gain)


def layer_one_kernel(layer_at, need, flush, in_ref, cot_ref, qkv_w, out_w, up_w, down_w, vec_ref, bias_ref, *refs):
    stream_ref, grad_ref, keep_ref, sent_ref, one_ref, two_ref, bias_sum_ref = refs[:7]
    mid_ref, qkv_ref, attn_ref, prob_ref, act_ref, slope_ref, mid_grad_ref, *rest = refs[7:]
    heads, hidden = pl.ds(0, 2 * WIDE), pl.ds(2 * WIDE, 4 * WIDE)

    def nothing(*_):
        pass

    attend_kernel(
        layer_at, need, nothing, in_ref, qkv_w, out_w, vec_ref, mid_ref, qkv_ref, attn_ref, prob_ref
    )
    hidden_kernel(
        layer_at,
        nothing,
        nothing,
        mid_ref,
        up_w,
        down_w,
        vec_ref,
        bias_ref,
        stream_ref,
        act_ref,
        slope_ref,
    )
    flush(0)
    hidden_back_kernel(
        layer_at,
        nothing,
        nothing,
        cot_ref,
        mid_ref,
        act_ref,
        slope_ref,
        up_w,
        down_w,
        vec_ref,
        mid_grad_ref,
        keep_ref.at[hidden],
        sent_ref.at[hidden],
        two_ref,
        bias_sum_ref,
    )
    for piece in (1, 2):
        flush(2, piece)
        flush(3, piece)
    attend_back_kernel(
        layer_at,
        nothing,
        nothing,
        mid_grad_ref,
        in_ref,
        qkv_ref,
        attn_ref,
        prob_ref,
        qkv_w,
        out_w,
        vec_ref,
        grad_ref,
        keep_ref.at[heads],
        sent_ref.at[heads],
        one_ref,
        *rest,
    )


def cut_piece(ref, how, at):
    if how is None:
        return ref
    dimension, pieces = how
    size = ref.shape[dimension] // pieces
    return ref.at[(slice(None),) * dimension + (pl.ds(at * size, size),)]


def layer_call(kernel, layer_at, ins, outs, in_cut, out_cut, scratch=(), name=None):
    count, total = len(ins), len(outs)
    pieces = max([how[1] for how in in_cut.values()] + [1])
    in_plan = [(at, None, 0) for at in range(count) if at not in in_cut]
    in_plan += [(at, in_cut[at], piece) for piece in range(pieces) for at in sorted(in_cut)]
    out_plan = []
    for at in range(total):
        how = out_cut.get(at)
        out_plan += [(at, how, piece) for piece in range(how[1] if how else 1)]

    def body(*refs):
        far, near = refs[: count + total], refs[count + total : 2 * (count + total)]
        come_sems, leave_sems = refs[2 * (count + total) : 2 * (count + total) + 2]
        rest = refs[2 * (count + total) + 2 :]
        come = [
            pltpu.make_async_copy(
                cut_piece(far[at], how, piece), cut_piece(near[at], how, piece), come_sems.at[index]
            )
            for index, (at, how, piece) in enumerate(in_plan)
        ]
        leave = [
            pltpu.make_async_copy(
                cut_piece(near[count + at], how, piece),
                cut_piece(far[count + at], how, piece),
                leave_sems.at[index],
            )
            for index, (at, how, piece) in enumerate(out_plan)
        ]
        started = []

        def need(wanted):
            for (_, how, piece), copy in zip(in_plan, come):
                if (how is None and wanted is None) or (how is not None and piece == wanted):
                    copy.wait()

        def flush(out_at, wanted=0):
            index = [(at, piece) for at, _, piece in out_plan].index((out_at, wanted))
            leave[index].start()
            started.append(index)

        for copy in come:
            copy.start()
        need(None)
        kernel(layer_at, need, flush, *near, *rest)
        for index, copy in enumerate(leave):
            if index not in started:
                copy.start()
        for copy in leave:
            copy.wait()

    return pl.pallas_call(
        body,
        out_shape=[jax.ShapeDtypeStruct(shape, kind) for shape, kind in outs],
        in_specs=[far_spec()] * count,
        out_specs=[far_spec()] * total,
        scratch_shapes=[pltpu.VMEM(part.shape, part.dtype) for part in ins]
        + [pltpu.VMEM(shape, kind) for shape, kind in outs]
        + [pltpu.SemaphoreType.DMA((len(in_plan),)), pltpu.SemaphoreType.DMA((len(out_plan),))]
        + list(scratch),
        compiler_params=pltpu.CompilerParams(vmem_limit_bytes=64 << 20),
        cost_estimate=pl.CostEstimate(flops=1 << 20, bytes_accessed=1 << 16, transcendentals=0),
        name=name,
    )(*ins)


def attention_forward(layer_at, inputs, w_qkv, w_out, vec_full):
    length = inputs.shape[0]
    return layer_call(
        attend_kernel,
        layer_at,
        [inputs, w_qkv, w_out, vec_full],
        [
            (inputs.shape, jnp.float32),
            ((length, 3 * WIDE), jnp.bfloat16),
            (inputs.shape, jnp.bfloat16),
            ((HEADS, length, length), jnp.bfloat16),
        ],
        {2: (0, 1)},
        {3: (0, HEADS // 2)},
        name="attend",
    )


def back_scratch(length):
    return [
        pltpu.VMEM((length, WIDE), jnp.bfloat16),
        pltpu.VMEM((length, 3 * WIDE), jnp.bfloat16),
        pltpu.VMEM((4 * WIDE, WIDE), jnp.bfloat16),
        pltpu.VMEM((8, WIDE), jnp.float32),
    ]


def attention_backward(layer_at, upstream, inputs, stored, w_qkv, w_out, vec_full, others):
    qkv_low, attn_low, probs = stored
    return layer_call(
        attend_back_kernel,
        layer_at,
        [upstream, inputs, qkv_low, attn_low, probs, w_qkv, w_out, vec_full, *others],
        [
            (inputs.shape, jnp.float32),
            ((2 * WIDE, WIDE), jnp.bfloat16),
            ((2 * WIDE + VPAD, WIDE), jnp.bfloat16),
            ((VPAD, WIDE), jnp.float32),
        ],
        {4: (0, HEADS // 2)},
        {},
        scratch=back_scratch(inputs.shape[0]),
        name="attend_back",
    )


def layer_one(inputs, cotangent, w_qkv, w_out, w_up, w_down, vec_full, bias_up):
    length = inputs.shape[0]
    return layer_call(
        layer_one_kernel,
        1,
        [inputs, cotangent, w_qkv, w_out, w_up, w_down, vec_full, bias_up],
        [
            (inputs.shape, jnp.float32),
            (inputs.shape, jnp.float32),
            ((6 * WIDE, WIDE), jnp.bfloat16),
            ((6 * WIDE, WIDE), jnp.bfloat16),
            ((8, WIDE), jnp.float32),
            ((8, WIDE), jnp.float32),
            ((4, WIDE), jnp.float32),
        ],
        {1: (0, 1), 3: (0, 1), 4: (0, 1), 5: (0, 1)},
        {2: (0, 3), 3: (0, 3)},
        scratch=[
            pltpu.VMEM(inputs.shape, jnp.float32),
            pltpu.VMEM((length, 3 * WIDE), jnp.bfloat16),
            pltpu.VMEM(inputs.shape, jnp.bfloat16),
            pltpu.VMEM((HEADS, length, length), jnp.bfloat16),
            pltpu.VMEM((length, FF), jnp.bfloat16),
            pltpu.VMEM((length, FF), jnp.float32),
            pltpu.VMEM(inputs.shape, jnp.float32),
            *back_scratch(length),
        ],
        name="layer_one",
    )


def hidden_forward(layer_at, middle, w_up, w_down, vec_full, bias_up):
    wide = (middle.shape[0], FF)
    return layer_call(
        hidden_kernel,
        layer_at,
        [middle, w_up, w_down, vec_full, bias_up],
        [(middle.shape, jnp.float32), (wide, jnp.bfloat16), (wide, jnp.float32)],
        {1: (0, 4), 2: (0, 4)},
        {1: (1, 4), 2: (1, 4)},
        name="hidden",
    )


def hidden_backward(layer_at, upstream, middle, stored, w_up, w_down, vec_full):
    return layer_call(
        hidden_back_kernel,
        layer_at,
        [upstream, middle, *stored, w_up, w_down, vec_full],
        [
            (middle.shape, jnp.float32),
            (w_up.shape, jnp.bfloat16),
            (w_up.shape, jnp.bfloat16),
            ((8, WIDE), jnp.float32),
            ((4, WIDE), jnp.float32),
        ],
        {2: (1, 4), 3: (1, 4), 4: (0, 4), 5: (0, 4)},
        {1: (0, 4), 2: (0, 4)},
        name="hidden_back",
    )


def on_device(tokens, cotangent, live, slot_of, weights, momentum, vec, vec_first, vec_second):
    group_at = lax.axis_index("group")
    data_at = lax.axis_index("dp")
    vec_here, vec_cols = vec.shape
    per_layer = VROWS // LAYERS
    tie = lax.optimization_barrier
    spread = lax.dynamic_update_slice(
        jnp.zeros((VPAD, WIDE), jnp.bfloat16),
        half(vec),
        (group_at * vec_here, data_at * vec_cols),
    )
    own_block = jnp.concatenate([half(weights[0].T), spread], 0)
    pair = jnp.concatenate([own_block, along_group(own_block, 1, 0)], 0)
    slots = [pair] + [along_group(pair, 0, -hops) for hops in (1, 2, 3)]
    first, third = small_call(
        choose_kernel,
        [(4 * BLK + VPAD, jnp.bfloat16), (4 * BLK, jnp.bfloat16)],
        [slot_of] + slots,
        slot_first=True,
        scratch=[pltpu.VMEM((MATS, BLK, WIDE), jnp.bfloat16)],
        name="choose",
    )
    first_x, second_x = small_call(
        merge_first_kernel,
        [(4 * BLK + VPAD, jnp.bfloat16), (8 * BLK, jnp.bfloat16)],
        from_x(first),
        scratch=[HOLD_HEADS],
        name="first_merge_x",
    )
    second_x, third, first_x = tie((second_x, third, first_x))
    beside_first = other_row(first_x)
    pair_first = jnp.concatenate([first_x, beside_first], 0)
    first_parts = [pair_first, other_core(pair_first)]
    beside_second, core_second = other_row(second_x), other_core(second_x)
    third_parts = from_x(third)
    w_qkv0, w_out0, vec_full, bias0, bias1 = whole(first_parts, True, False, True, "first")
    inputs0 = tokens[0]
    middle0, *attn0 = attention_forward(0, inputs0, w_qkv0, w_out0, vec_full)
    third_parts, beside_second, middle0 = tie((third_parts, beside_second, middle0))
    (third_x,) = small_call(
        merge_third_kernel,
        [(12 * BLK, jnp.bfloat16)],
        third_parts,
        scratch=[HOLD_HEADS],
        name="third_merge_x",
    )
    beside = other_row(third_x)
    core_third = other_core(third_x)
    second_parts = [second_x, beside_second, core_second, other_core(beside_second)]
    w_up0, w_down0 = whole(second_parts, False, True, False, "second")
    inputs1, *mlp0 = hidden_forward(0, middle0, w_up0, w_down0, vec_full, bias0)
    beside, inputs1 = tie((beside, inputs1))
    third_parts = [third_x, beside, core_third, other_core(beside)]
    w_qkv1, w_out1, w_up1, w_down1 = whole(third_parts, True, True, False, "third")
    upstream = cotangent[0] * full(live)[0]
    stream, upstream, keep, sent, sums_one1, sums_two1, sums_up1 = layer_one(
        inputs1, upstream, w_qkv1, w_out1, w_up1, w_down1, vec_full, bias1
    )
    came = other_core(sent)
    mid_grad, keep_f, sent_f, sums_two0, sums_up0 = hidden_backward(
        0, upstream, middle0, mlp0, w_up0, w_down0, vec_full
    )
    came_f = other_core(sent_f)
    vec_full, came = tie((vec_full, came))
    keep, sent = scatter_row(keep, came, True, True, False, "third")
    vec_full, sent = tie((vec_full, sent))
    came = other_row(sent)
    token_grad, keep_h, sent_h, vec_sum = attention_backward(
        0,
        mid_grad,
        inputs0,
        attn0,
        w_qkv0,
        w_out0,
        vec_full,
        (sums_two0, sums_up0, sums_one1, sums_two1, sums_up1),
    )
    vec_sum, came_f = tie((vec_sum, came_f))
    keep_f, sent_f = scatter_row(keep_f, came_f, False, True, False, "second")
    sent_h, sent_f, came = tie((sent_h, sent_f, came))
    came_f = other_row(sent_f)
    came_h = other_core(sent_h)
    keep, *sent_x = scatter_x(keep, came, True, True, False, "third")
    came_x = spread_x(sent_x)
    keep_h, sent_h, vec_sum = scatter_row(keep_h, came_h, True, False, True, "first", vec_sum)
    came_h = other_row(sent_h)
    keep_f, *sent_f = scatter_x(keep_f, came_f, False, True, False, "second")
    (third_sum,) = small_call(
        lambda *refs: sum_x_kernel(True, *refs),
        [(4 * BLK, jnp.float32)],
        [keep] + came_x,
        name="third_sum_x",
    )
    came_f = spread_x(sent_f)
    (second_sum,) = small_call(
        lambda *refs: sum_x_kernel(False, *refs),
        [(2 * BLK, jnp.float32)],
        [keep_f] + came_f,
        name="second_sum_x",
    )
    keep_h, *sent_h, vec_sum = scatter_x(keep_h, came_h, True, False, True, "first", vec_sum)
    came_h = spread_x(sent_h)
    own, *sent_g, vec_sum = small_call(
        split_group_kernel,
        [(BLK, jnp.float32)]
        + [(BLK + VPAD, jnp.bfloat16)] * 7
        + [(VPAD, jnp.float32)],
        [slot_of, second_sum, third_sum, keep_h] + came_h + [vec_sum],
        slot_first=True,
        scratch=[pltpu.VMEM((MATS, BLK, WIDE), jnp.float32)],
        name="split_group",
    )
    came_g = [along_group(part, flip, hops) for part, (flip, hops) in zip(sent_g, STEPS[1:])]
    grad_rows, moment_rows, moment_low, vec_sum = small_call(
        renew_kernel,
        [(BLK, jnp.float32), (BLK, jnp.float32), (BLK, jnp.bfloat16), (VPAD, jnp.float32)],
        [own] + came_g + [vec_sum, momentum[0].T],
        name="renew",
    )
    ring = jnp.concatenate([moment_low] + [along_x(moment_low, -hops) for hops in (1, 2, 3)], 0)
    beside = other_row(ring)
    (weight_rows,) = small_call(
        newton_kernel,
        [(BLK, jnp.float32)],
        [slot_of, ring, beside, other_core(ring), other_core(beside), moment_low, weights[0].T],
        slot_first=True,
        name="newton",
    )
    shard_vec = lax.dynamic_slice(
        vec_sum, (group_at * vec_here, data_at * vec_cols), (vec_here, vec_cols)
    )
    first_new = first_keep * vec_first + (1.0 - first_keep) * shard_vec
    second_new = second_keep * vec_second + (1.0 - second_keep) * shard_vec * shard_vec
    vec_new = vec - adam_rate * (
        first_new
        / (1.0 - first_keep**STEP)
        / (jnp.sqrt(second_new / (1.0 - second_keep**STEP)) + adam_eps)
    )
    return (
        stream[None],
        token_grad[None],
        grad_rows.T[None],
        moment_rows.T[None],
        weight_rows.T[None],
        first_new,
        second_new,
        vec_new,
    )


def solution(mesh):
    placed = (
        P(("group", "dp"), None, None),
        P(("group", "dp"), None, None),
        P(("group", "dp")),
        P(),
        P("group", None, "dp"),
        P("group", None, "dp"),
        P("group", "dp"),
        P("group", "dp"),
        P("group", "dp"),
    )
    return jax.shard_map(
        on_device,
        mesh=mesh,
        in_specs=placed,
        out_specs=(
            P(("group", "dp"), None, None),
            P(("group", "dp"), None, None),
            P("group", None, "dp"),
            P("group", None, "dp"),
            P("group", None, "dp"),
            P("group", "dp"),
            P("group", "dp"),
            P("group", "dp"),
        ),
        check_vma=False,
    )
```
